256 devices in a mesh: dp: 128 (over y_hi, x, z, core), tensor: 2 (over y_lo).
Axes of the slice: x: 4, y: 4 (y_hi: 2, y_lo: 2; y = y_hi * 2 + y_lo), z: 8, core: 2. Of those that a mesh axis runs over, the one named last changes fastest.
Arguments:
- image_raw: bfloat16 [8192, 1152], P(('dp', 'tensor')), may hold values from -0.1875 to 0.1875
- text_raw: bfloat16 [8192, 1152], P('dp'), may hold values from -0.1875 to 0.1875
- logit_scale: float32 [], replicated, may hold values from 8 to 24
- logit_bias: float32 [], replicated, may hold values from -4 to -1
- pair_offset: int32 [8192], P(('dp', 'tensor')), may hold values from 0 to 448
- normed_patches: bfloat16 [93312, 1152], P('dp'), may hold values from -24 to 24
- head_cotangent: bfloat16 [93312, 1152], P('dp'), may hold values from -0.25 to 0.25
- hidden_pre: bfloat16 [93312, 4304], P('dp', 'tensor'), may hold values from -6 to 6
- pool_share: float32 [93312], P('dp'), may hold values from 0.0005 to 0.005
- down_weight: bfloat16 [4304, 1152], P('tensor'), may hold values from -0.09375 to 0.09375
Outputs:
- image_grad: bfloat16 [8192, 1152], P(('dp', 'tensor'))
- text_grad: bfloat16 [8192, 1152], P('dp')
- up_grad: float32 [1152, 4304], P('dp', 'tensor')
The draws below stay inside these ranges and needn't reach their ends.
All inputs are finite; a program needn't handle non-finite values.
Results may differ from the reference program's by a relative error of at most 0.0058.
Values may be sent and summed in bfloat16 or wider, within the bound.
No kernel may reach another device: no remote copies, remote signals or barrier semaphores. Data moves between devices by JAX's collectives and lax.ppermute only.
A program may use at most 128 MiB of HBM per device.

```python
import math
import jax
import jax.numpy as jnp
from jax import lax

D = 1152
FF = 4304
TXT_DEV = 64
PATCH = 729
WINDOW = 8
TOKENS = 8192
PATCHES = 93312
N_DP = 128


def place_ends(drawn, rng, low, high):
    spot = [jax.random.randint(jax.random.fold_in(rng, axis), (), 0, length) for axis, length in enumerate(drawn.shape)]
    longest = drawn.shape.index(max(drawn.shape))
    neighbour = spot[:longest] + [(spot[longest] + 1) % drawn.shape[longest]] + spot[longest + 1:]
    return drawn.at[tuple(spot)].set(low).at[tuple(neighbour)].set(high)


def raised(entries, rng, source, target, blocks, factor):
    owner, partner = [(jnp.arange(entries.shape[axis_at]) // (entries.shape[axis_at] // blocks)).reshape([-1 if axis == axis_at else 1 for axis in range(entries.ndim)]) for axis_at in (source, target)]
    chosen = jax.random.permutation(rng, blocks)[partner]
    strong = (owner == chosen) | (owner == (partner + blocks // 2) % blocks)
    return jnp.where(strong, factor * entries, entries)


def steps_of(key, shape, shards, low, top_value):
    level, own = 1.0, jax.random.fold_in(key, 6)
    for position, shards_of in shards:
        heights = jnp.exp(jax.random.uniform(jax.random.fold_in(own, position), (shards_of,), jnp.float32, low / len(shards), top_value / len(shards)))
        level = level * jnp.repeat(heights, shape[position] // shards_of).reshape([-1 if axis == position else 1 for axis in range(len(shape))])
    return level


def scatter_about(rng, extent, spread, limit, split=(), held_as=jnp.bfloat16):
    factor_of = steps_of(rng, extent, split, -0.22, 0.18) if split else 1.0
    result = jax.random.normal(rng, extent, jnp.float32) * spread * factor_of
    return jnp.minimum(jnp.maximum(result, -limit), limit).astype(held_as)


def heavy_noise(rng, shape, width, reach, shards, heavy, kind=jnp.bfloat16):
    drawn = width * jax.random.normal(rng, shape, jnp.float32)
    if shards:
        drawn = drawn * steps_of(rng, shape, shards, -0.22, 0.18)
    return jnp.clip(raised(drawn, jax.random.fold_in(rng, 3), *heavy), -reach, reach).astype(kind)


def setup_inputs(seed: int = 0) -> dict:
    key_of = jax.random.split(jax.random.key(seed), 11)
    image_raw = scatter_about(key_of[0], (TOKENS, D), (D ** -0.5), 0.1875, ((0, 256),))
    text_raw = scatter_about(key_of[1], (TOKENS, D), (D ** -0.5), 0.1875, ((0, 128),))
    logit_scale = jnp.clip(jax.random.uniform(key_of[2], (), jnp.float32, 8.0, 24.0), 8.0, 24.0)
    logit_bias = jnp.clip(jax.random.uniform(key_of[3], (), jnp.float32, -4.0, -1.0), -4.0, -1.0)
    pair_offset = place_ends(jax.random.randint(key_of[4], (TOKENS,), 0, (WINDOW - 1) * TXT_DEV + 1), jax.random.fold_in(key_of[4], 1), 0, (WINDOW - 1) * TXT_DEV).astype(jnp.int32)
    normed_patches = heavy_noise(key_of[5], (PATCHES, D), 1.0, 24.0, ((0, 128),), (0, 1, 128, 5.5))
    head_cotangent = heavy_noise(key_of[6], (PATCHES, D), 0.01, 0.25, ((0, 128),), (0, 1, 128, 5.5))
    hidden_pre = scatter_about(key_of[7], (PATCHES, FF), 1.0, 6.0, ((0, 128), (1, 2)))
    pool_share = jnp.clip(jnp.exp(math.log(0.005) - 2.30258502 * jax.random.uniform(key_of[8], (PATCHES,), jnp.float32) ** steps_of(key_of[8], (PATCHES,), ((0, 128),), -0.2, 0.2)), 0.0005, 0.005)
    down_weight = scatter_about(key_of[9], (FF, D), FF ** -0.5, 0.09375, ((0, 2),))
    return dict(image_raw=image_raw, text_raw=text_raw, logit_scale=logit_scale, logit_bias=logit_bias, pair_offset=pair_offset, normed_patches=normed_patches, head_cotangent=head_cotangent, hidden_pre=hidden_pre, pool_share=pool_share, down_weight=down_weight)


epsilon = 1e-06
gelu_root = 0.7978845608028654
gelu_cubic = 0.044715

def unit_rows(raw_rows):
    widened = raw_rows.astype(jnp.float32)
    lengths = jnp.sqrt(lax.optimization_barrier(jnp.sum(widened * widened, axis=-1, keepdims=True)) + epsilon)
    return (widened / lengths, lengths)

def project_back(unit_part, lengths, direction):
    radial = lax.optimization_barrier(jnp.sum(unit_part * direction, axis=-1, keepdims=True))
    return (direction - unit_part * radial) / lengths

def gelu_slope(hidden_in):
    inner = gelu_root * (hidden_in + gelu_cubic * hidden_in * hidden_in * hidden_in)
    tangent = jnp.tanh(inner)
    return 0.5 * (1.0 + tangent) + 0.5 * hidden_in * (1.0 - tangent * tangent) * gelu_root * (1.0 + 3.0 * gelu_cubic * hidden_in * hidden_in)

def reference(image_raw, text_raw, logit_scale, logit_bias, pair_offset, normed_patches, head_cotangent, hidden_pre, pool_share, down_weight):
    image_unit, image_length = unit_rows(image_raw)
    text_unit, text_length = unit_rows(text_raw)
    image_key = image_unit.astype(jnp.bfloat16)
    text_key = text_unit.astype(jnp.bfloat16)
    window_rows = WINDOW * TXT_DEV
    leading = (WINDOW - 1) * TXT_DEV
    extended = jnp.concatenate([text_key[TOKENS - leading:], text_key], axis=0)
    image_blocks = image_key.reshape(N_DP, TXT_DEV, D)
    offset_blocks = pair_offset.reshape(N_DP, TXT_DEV)
    columns = jnp.arange(window_rows, dtype=jnp.int32)
    rows_here = jnp.arange(TXT_DEV, dtype=jnp.int32)

    def one_block(text_total, block_index):
        keys_here = lax.dynamic_index_in_dim(image_blocks, block_index, 0, keepdims=False)
        offsets = lax.dynamic_index_in_dim(offset_blocks, block_index, 0, keepdims=False)
        begin = (block_index * TXT_DEV).astype(jnp.int32)
        window = lax.dynamic_slice_in_dim(extended, begin, window_rows, 0)
        cosine = lax.dot_general(keys_here, window, (((1,), (1,)), ((), ())), preferred_element_type=jnp.float32)
        logits = logit_scale * cosine + logit_bias
        target = (columns[None, :] == (rows_here + leading - offsets)[:, None]).astype(jnp.float32)
        weight = (jax.nn.sigmoid(logits) - target).astype(jnp.bfloat16)
        image_part = logit_scale * jnp.dot(weight, window, preferred_element_type=jnp.float32)
        text_part = logit_scale * lax.dot_general(weight, keys_here, (((0,), (0,)), ((), ())), preferred_element_type=jnp.float32)
        current = lax.dynamic_slice_in_dim(text_total, begin, window_rows, 0)
        text_total = lax.dynamic_update_slice_in_dim(text_total, current + text_part, begin, 0)
        return (text_total, image_part)
    text_total, image_parts = lax.scan(one_block, jnp.zeros((TOKENS + leading, D), jnp.float32), jnp.arange(N_DP, dtype=jnp.int32))
    text_dir = text_total[leading:]
    text_dir = text_dir.at[TOKENS - leading:].add(text_total[:leading])
    image_dir = image_parts.reshape(TOKENS, D)
    image_grad = project_back(image_unit, image_length, image_dir).astype(jnp.bfloat16)
    text_grad = project_back(text_unit, text_length, text_dir).astype(jnp.bfloat16)
    pooled_grad = image_grad[::TXT_DEV].astype(jnp.float32)

    def vision_block(up_total, block_index):
        begin = (block_index * PATCH).astype(jnp.int32)
        inputs = lax.dynamic_slice_in_dim(normed_patches, begin, PATCH, 0)
        cotangent = lax.dynamic_slice_in_dim(head_cotangent, begin, PATCH, 0).astype(jnp.float32)
        hidden_in = lax.dynamic_slice_in_dim(hidden_pre, begin, PATCH, 0).astype(jnp.float32)
        shares = lax.dynamic_slice_in_dim(pool_share, begin, PATCH, 0)
        grad_row = lax.dynamic_index_in_dim(pooled_grad, block_index, 0, keepdims=False)
        out_grad = (cotangent + shares[:, None] * grad_row[None, :]).astype(jnp.bfloat16)
        hidden_grad = lax.dot_general(out_grad, down_weight, (((1,), (1,)), ((), ())), preferred_element_type=jnp.float32)
        pre_grad = (hidden_grad * gelu_slope(hidden_in)).astype(jnp.bfloat16)
        up_total = up_total + lax.dot_general(inputs, pre_grad, (((0,), (0,)), ((), ())), preferred_element_type=jnp.float32)
        return (up_total, None)
    up_grad, unused = lax.scan(vision_block, jnp.zeros((D, FF), jnp.float32), jnp.arange(N_DP, dtype=jnp.int32))
    return (image_grad, text_grad, up_grad)
```

```python
import jax
import jax.numpy as jnp
from jax import lax
from jax.sharding import PartitionSpec as P

WINDOW = 8
N_YH, N_X, N_Z, N_CORE = 2, 4, 8, 2
N_DP = N_YH * N_X * N_Z * N_CORE
N_TENSOR = 2
LANES = 128

epsilon = 1e-06
gelu_root = 0.7978845608028654
gelu_cubic = 0.044715

f32 = jnp.float32
bf16 = jnp.bfloat16


def encode(yh, x, z, core):
    return (((yh % N_YH) * N_X + x % N_X) * N_Z + z % N_Z) * N_CORE + core % N_CORE


def torus_pairs(yh=0, x=0, z=0, core=0):
    pairs = []
    for j in range(N_DP):
        own = (j // (N_CORE * N_Z * N_X), j // (N_CORE * N_Z) % N_X, j // N_CORE % N_Z, j % N_CORE)
        pairs.append((j, encode(own[0] + yh, own[1] + x, own[2] + z, own[3] + core)))
    return pairs


def torus_send(array, **shift):
    return lax.ppermute(array, "dp", torus_pairs(**shift))


def ring_send(array, by, only=None):
    pairs = [(j, (j + by) % N_DP) for j in range(N_DP) if only is None or j % N_CORE == only]
    return lax.ppermute(array, "dp", pairs)


def tensor_swap(array):
    return lax.ppermute(array, "tensor", [(0, 1), (1, 0)])


def unit_rows(raw_rows):
    widened = raw_rows.astype(f32)
    lengths = jnp.sqrt(jnp.sum(widened * widened, axis=-1, keepdims=True) + epsilon)
    return (widened / lengths, lengths)


def project_back(unit_part, lengths, direction):
    radial = jnp.sum(unit_part * direction, axis=-1, keepdims=True)
    return (direction - unit_part * radial) / lengths


def gelu_slope(hidden_in):
    inner = gelu_root * (hidden_in + gelu_cubic * hidden_in * hidden_in * hidden_in)
    tangent = jnp.tanh(inner)
    return 0.5 * (1.0 + tangent) + 0.5 * hidden_in * (1.0 - tangent * tangent) * gelu_root * (
        1.0 + 3.0 * gelu_cubic * hidden_in * hidden_in
    )


def dot_nt(a, b):
    return lax.dot_general(a, b, (((1,), (1,)), ((), ())), preferred_element_type=f32)


def dot_tn(a, b):
    return lax.dot_general(a, b, (((0,), (0,)), ((), ())), preferred_element_type=f32)


def pair_weight(image_keys, text_keys, image_offset, text_place, logit_scale, logit_bias):
    logits = logit_scale * dot_nt(image_keys, text_keys) + logit_bias
    target = (text_place[None, :] == image_offset[:, None]).astype(f32)
    return (jax.nn.sigmoid(logits) - target).astype(bf16)


def block_window(first, behind, core):
    sign = 1 if behind else -1
    even = [first] + [ring_send(first, sign * 2 * d) for d in (1, 2, 3)]
    last = ring_send(first, sign * 8, only=1 if behind else 0)
    shifted = jnp.stack(even[1:] + [last])
    plain = jnp.stack(even)
    odd = torus_send(jnp.where(core == (1 if behind else 0), shifted, plain), core=1)
    return jnp.concatenate([plain, odd], axis=0)


def per_device(
    image_raw,
    text_raw,
    logit_scale,
    logit_bias,
    pair_offset,
    normed_patches,
    head_cotangent,
    hidden_pre,
    pool_share,
    down_weight,
):
    place = lax.axis_index("dp")
    tensor_index = lax.axis_index("tensor")
    yh = place // (N_CORE * N_Z * N_X)
    x = place // (N_CORE * N_Z) % N_X
    core = place % N_CORE
    image_rows, width = image_raw.shape
    text_rows = text_raw.shape[0]
    half = text_rows // N_TENSOR
    hidden_here = hidden_pre.shape[1]

    text_unit, text_length = unit_rows(text_raw)
    text_key = text_unit.astype(bf16)
    text_half = lax.dynamic_slice_in_dim(text_key, tensor_index * half, half, 0)
    rels = jnp.array([0, 2, 4, 6, 1, 3, 5, 7], jnp.int32)
    text_window = block_window(text_half, True, core).reshape(WINDOW * half, width)

    marks = jnp.zeros((image_rows, LANES), bf16)
    marks = marks.at[:, 0].set((pair_offset // 64).astype(bf16)).at[:, 1].set((pair_offset % 64).astype(bf16))
    image_other = tensor_swap(jnp.concatenate([image_raw, marks], axis=1))
    other_offset = (64.0 * image_other[:, width].astype(f32) + image_other[:, width + 1].astype(f32)).astype(jnp.int32)
    image_all = jnp.concatenate([image_raw, image_other[:, :width]], axis=0)
    image_unit, image_length = unit_rows(image_all)
    image_key = image_unit.astype(bf16)
    row = jnp.arange(image_rows, dtype=jnp.int32)
    own_row = row + tensor_index * image_rows
    other_row = row + (1 - tensor_index) * image_rows

    columns = 9 * LANES
    start = 8 * LANES
    padded = start + columns
    normed_other = torus_send(normed_patches, core=1)
    cotangent_other = torus_send(head_cotangent, core=1)
    share_other = torus_send(pool_share, core=1)
    hidden_padded = jnp.pad(hidden_pre, ((0, 0), (0, padded - hidden_here)))
    weight_padded = jnp.pad(down_weight, ((0, padded - hidden_here), (0, 0)))
    hidden_mine = lax.dynamic_slice_in_dim(hidden_padded, core * start, columns, 1)
    hidden_other = torus_send(
        lax.dynamic_slice_in_dim(hidden_padded, (1 - core) * start, columns, 1), core=1
    )
    weight_mine = lax.dynamic_slice_in_dim(weight_padded, core * start, columns, 0)

    patches = normed_patches.shape[0]
    cotangent = jnp.concatenate([head_cotangent, cotangent_other], axis=0)
    normed = jnp.concatenate([normed_patches, normed_other], axis=0)
    hidden = jnp.concatenate([hidden_mine, hidden_other], axis=0)
    slope = gelu_slope(hidden.astype(f32))
    hidden_base = dot_nt(cotangent, weight_mine)

    text_place = (tensor_index * half + jnp.arange(half, dtype=jnp.int32))[None, :] - 64 * rels[:, None]
    image_target = jnp.concatenate([own_row - pair_offset, other_row - other_offset])
    weight = pair_weight(
        image_key, text_window, image_target, text_place.reshape(-1), logit_scale, logit_bias
    )
    image_part = jnp.dot(weight, text_window, preferred_element_type=f32)
    zero_row = jnp.where(tensor_index == 0, image_part[:1], image_part[image_rows : image_rows + 1])
    zero_dir = logit_scale * (zero_row + tensor_swap(zero_row))
    zero_unit = jnp.where(tensor_index == 0, image_unit[:1], image_unit[image_rows : image_rows + 1])
    zero_length = jnp.where(tensor_index == 0, image_length[:1], image_length[image_rows : image_rows + 1])
    pooled = project_back(zero_unit, zero_length, zero_dir).astype(bf16)
    pooled_both = jnp.concatenate([pooled, torus_send(pooled, core=1)], axis=0)

    lift = dot_nt(pooled_both, weight_mine)
    lifted = jnp.concatenate(
        [pool_share[:, None] * lift[0][None, :], share_other[:, None] * lift[1][None, :]], axis=0
    )
    pre_grad = ((hidden_base + lifted) * slope).astype(bf16)
    split = 5 * LANES
    blocks = width // (N_YH * N_X)
    part_a = dot_tn(normed, pre_grad[:, :split]).reshape(N_YH, N_X, blocks, split)
    part_c = dot_tn(normed, pre_grad[:, split:]).reshape(N_YH, N_X, blocks, columns - split)

    def take_x(array, dx):
        return lax.dynamic_index_in_dim(array, (x + dx) % N_X, 1, keepdims=False)

    def take_y(array, dy):
        return lax.dynamic_index_in_dim(array, (yh + dy) % N_YH, 0, keepdims=False)

    a_sent = [torus_send(take_x(part_a, dx).astype(bf16), x=dx) for dx in (2, 1, 3)]
    c_sent = torus_send(take_y(part_c, 1).astype(bf16), yh=1)
    part_a = take_x(part_a, 0) + sum(piece.astype(f32) for piece in a_sent)
    part_c = take_y(part_c, 0) + c_sent.astype(f32)
    c_sent = [
        torus_send(lax.dynamic_index_in_dim(part_c, (x + dx) % N_X, 0, keepdims=False).astype(bf16), x=dx)
        for dx in (2, 1, 3)
    ]
    a_sent = torus_send(take_y(part_a, 1).astype(bf16), yh=1)
    part_a = take_y(part_a, 0) + a_sent.astype(f32)
    part_c = lax.dynamic_index_in_dim(part_c, x, 0, keepdims=False) + sum(
        piece.astype(f32) for piece in c_sent
    )
    rows_chip = blocks // N_Z
    chunk = jnp.concatenate([part_a.astype(bf16), part_c.astype(bf16)], axis=1)
    chunk = chunk.reshape(N_Z, rows_chip, columns)
    z_groups = [
        [encode(g // (N_X * N_CORE), g // N_CORE % N_X, zz, g % N_CORE) for zz in range(N_Z)]
        for g in range(N_DP // N_Z)
    ]
    chunk = lax.all_to_all(chunk, "dp", 0, 0, axis_index_groups=z_groups, tiled=True)
    total = jnp.sum(chunk.astype(f32), axis=0)
    rows_here = rows_chip // N_CORE
    mine = jnp.where(core == 0, total[:rows_here], total[rows_here:])
    theirs = torus_send(jnp.where(core == 0, total[rows_here:], total[:rows_here]), core=1)
    left = jnp.where(core == 0, mine, theirs)
    right = jnp.where(core == 0, theirs, mine)
    up_grad = jnp.concatenate([left, right[:, columns - start : hidden_here - start]], axis=1)

    image_dir = logit_scale * (image_part[:image_rows] + tensor_swap(image_part[image_rows:]))
    image_grad = project_back(image_unit[:image_rows], image_length[:image_rows], image_dir).astype(bf16)

    image_ext = jnp.concatenate([image_key[:image_rows], marks], axis=1)
    image_window = block_window(image_ext, False, core).reshape(WINDOW * image_rows, width + LANES)
    window_key = image_window[:, :width]
    window_offset = (
        64.0 * image_window[:, width].astype(f32) + image_window[:, width + 1].astype(f32)
    ).astype(jnp.int32)
    window_row = (own_row[None, :] + 64 * rels[:, None]).reshape(-1)
    weight = pair_weight(
        window_key,
        text_key,
        window_row - window_offset,
        jnp.arange(text_rows, dtype=jnp.int32),
        logit_scale,
        logit_bias,
    )
    text_part = dot_tn(weight, window_key)
    text_dir = logit_scale * (text_part + tensor_swap(text_part))
    text_grad = project_back(text_unit, text_length, text_dir).astype(bf16)
    return (image_grad, text_grad, up_grad)


def solution(mesh):
    return jax.shard_map(
        per_device,
        mesh=mesh,
        in_specs=(
            P(("dp", "tensor"), None),
            P("dp", None),
            P(),
            P(),
            P(("dp", "tensor")),
            P("dp", None),
            P("dp", None),
            P("dp", "tensor"),
            P("dp"),
            P("tensor", None),
        ),
        out_specs=(P(("dp", "tensor"), None), P("dp", None), P("dp", "tensor")),
        check_vma=False,
    )
```

```python
import functools

import jax
import jax.numpy as jnp
from jax import lax
from jax.experimental import pallas as pl
from jax.experimental.pallas import tpu as pltpu
from jax.sharding import PartitionSpec as P

WINDOW = 8
N_YH, N_X, N_Z, N_CORE = 2, 4, 8, 2
N_DP = N_YH * N_X * N_Z * N_CORE
N_TENSOR = 2
LANES = 128

epsilon = 1e-06
gelu_root = 0.7978845608028654
gelu_cubic = 0.044715

f32 = jnp.float32
bf16 = jnp.bfloat16


def encode(yh, x, z, core):
    return (((yh % N_YH) * N_X + x % N_X) * N_Z + z % N_Z) * N_CORE + core % N_CORE


def torus_pairs(yh=0, x=0, z=0, core=0):
    pairs = []
    for j in range(N_DP):
        own = (j // (N_CORE * N_Z * N_X), j // (N_CORE * N_Z) % N_X, j // N_CORE % N_Z, j % N_CORE)
        pairs.append((j, encode(own[0] + yh, own[1] + x, own[2] + z, own[3] + core)))
    return pairs


def torus_send(array, **shift):
    return lax.ppermute(array, "dp", torus_pairs(**shift))


def ring_send(array, by, only=None):
    pairs = [(j, (j + by) % N_DP) for j in range(N_DP) if only is None or j % N_CORE == only]
    return lax.ppermute(array, "dp", pairs)


def tensor_swap(array):
    return lax.ppermute(array, "tensor", [(0, 1), (1, 0)])


def unit_rows(raw_rows):
    widened = raw_rows.astype(f32)
    lengths = jnp.sqrt(jnp.sum(widened * widened, axis=-1, keepdims=True) + epsilon)
    return (widened / lengths, lengths)


def project_back(unit_part, lengths, direction):
    radial = jnp.sum(unit_part * direction, axis=-1, keepdims=True)
    return (direction - unit_part * radial) / lengths


def gelu_slope(hidden_in):
    inner = gelu_root * (hidden_in + gelu_cubic * hidden_in * hidden_in * hidden_in)
    tangent = jnp.tanh(inner)
    return 0.5 * (1.0 + tangent) + 0.5 * hidden_in * (1.0 - tangent * tangent) * gelu_root * (
        1.0 + 3.0 * gelu_cubic * hidden_in * hidden_in
    )


def dot_nt(a, b):
    return lax.dot_general(a, b, (((1,), (1,)), ((), ())), preferred_element_type=f32)


def dot_tn(a, b):
    return lax.dot_general(a, b, (((0,), (0,)), ((), ())), preferred_element_type=f32)


def pair_weight(image_keys, text_keys, image_offset, text_place, logit_scale, logit_bias):
    logits = logit_scale * dot_nt(image_keys, text_keys) + logit_bias
    target = (text_place[None, :] == image_offset[:, None]).astype(f32)
    return (jax.nn.sigmoid(logits) - target).astype(bf16)


def read_marks(marks):
    lane = lax.broadcasted_iota(jnp.int32, marks.shape, 1)
    scale = jnp.where(lane == 0, 64.0, jnp.where(lane == 1, 1.0, 0.0))
    return jnp.sum(marks.astype(f32) * scale, axis=-1).astype(jnp.int32)


def base_kernel(patches, core_ref, cotangent_ref, weight_ref, hidden_ref, base_ref, slope_ref):
    grad = dot_nt(cotangent_ref[...], weight_ref[...])
    slope = gelu_slope(hidden_ref[...].astype(f32))
    kept = lax.broadcasted_iota(jnp.int32, slope.shape, 0) < patches
    slope_ref[...] = jnp.where(kept, slope, 0.0).astype(bf16)
    base_ref[...] = jnp.where(kept, grad * slope, 0.0)


def hidden_base(core, cotangent, weight, hidden):
    patches, width = cotangent.shape
    wide = weight.shape[0]
    step = 2 * LANES
    rows = -(-patches // step) * step
    return pl.pallas_call(
        functools.partial(base_kernel, patches),
        grid_spec=pltpu.PrefetchScalarGridSpec(
            num_scalar_prefetch=1,
            grid=(wide // step,),
            in_specs=[
                pl.BlockSpec((rows, width), lambda i, core: (0, 0)),
                pl.BlockSpec((step, width), lambda i, core: (i, 0)),
                pl.BlockSpec((rows, step), lambda i, core: (0, 4 * core[0] + i)),
            ],
            out_specs=[
                pl.BlockSpec((rows, step), lambda i, core: (0, i)),
                pl.BlockSpec((rows, step), lambda i, core: (0, i)),
            ],
        ),
        out_shape=[
            jax.ShapeDtypeStruct((rows, wide), f32),
            jax.ShapeDtypeStruct((rows, wide), bf16),
        ],
        compiler_params=pltpu.CompilerParams(vmem_limit_bytes=32 * 2**20),
        cost_estimate=pl.CostEstimate(
            flops=2 * rows * width * wide, bytes_accessed=12 * rows * wide, transcendentals=rows * wide
        ),
    )(core[None], cotangent, weight, hidden)


def terms_kernel(
    targets_ref, normed_ref, base0_ref, base1_ref, slope0_ref, slope1_ref, share_ref, lift_ref, *refs
):
    outs, pre_ref = refs[:-1], refs[-1]
    rows = base0_ref.shape[0]
    for image, (base_ref, slope_ref) in enumerate(((base0_ref, slope0_ref), (base1_ref, slope1_ref))):
        lifted = share_ref[image] * lift_ref[image : image + 1, :]
        grad = base_ref[...] + lifted * slope_ref[...].astype(f32)
        pre_ref[image * rows : (image + 1) * rows, :] = grad.astype(bf16)
    height = outs[0].shape[0]
    for slot, out in enumerate(outs):
        begin = pl.multiple_of(targets_ref[slot] * height, 16)
        product = jnp.dot(normed_ref[pl.ds(begin, height), :], pre_ref[...], preferred_element_type=f32)
        out[...] = product.astype(out.dtype)


def up_terms(targets, normed_t, base_own, base_other, slope_own, slope_other, shares, lift):
    count = targets.shape[0]
    width, depth = normed_t.shape
    rows = base_own.shape[0]
    columns = lift.shape[1]
    step = 3 * LANES
    height = width // count
    kinds = [bf16] * (count - 1) + [f32]
    image_spec = pl.BlockSpec((rows, step), lambda i, targets: (0, i))
    return pl.pallas_call(
        terms_kernel,
        grid_spec=pltpu.PrefetchScalarGridSpec(
            num_scalar_prefetch=1,
            grid=(columns // step,),
            in_specs=[
                pl.BlockSpec((width, depth), lambda i, targets: (0, 0)),
                image_spec,
                image_spec,
                image_spec,
                image_spec,
                pl.BlockSpec((2, rows, 1), lambda i, targets: (0, 0, 0)),
                pl.BlockSpec((2, step), lambda i, targets: (0, i)),
            ],
            out_specs=[pl.BlockSpec((height, step), lambda i, targets: (0, i))] * count,
            scratch_shapes=[pltpu.VMEM((2 * rows, step), bf16)],
        ),
        out_shape=[jax.ShapeDtypeStruct((height, columns), kind) for kind in kinds],
        compiler_params=pltpu.CompilerParams(vmem_limit_bytes=32 * 2**20),
        cost_estimate=pl.CostEstimate(
            flops=2 * width * depth * columns, bytes_accessed=16 * rows * columns, transcendentals=0
        ),
    )(targets, normed_t, base_own, base_other, slope_own, slope_other, shares, lift)


def block_window(first, behind, core):
    sign = 1 if behind else -1
    even = [first] + [ring_send(first, sign * 2 * d) for d in (1, 2, 3)]
    last = ring_send(first, sign * 8, only=1 if behind else 0)
    shifted = jnp.stack(even[1:] + [last])
    plain = jnp.stack(even)
    odd = torus_send(jnp.where(core == (1 if behind else 0), shifted, plain), core=1)
    return jnp.concatenate([plain, odd], axis=0)


def per_device(
    image_raw,
    text_raw,
    logit_scale,
    logit_bias,
    pair_offset,
    normed_patches,
    head_cotangent,
    hidden_pre,
    pool_share,
    down_weight,
):
    place = lax.axis_index("dp")
    tensor_index = lax.axis_index("tensor")
    yh = place // (N_CORE * N_Z * N_X)
    x = place // (N_CORE * N_Z) % N_X
    z = place // N_CORE % N_Z
    core = place % N_CORE
    image_rows, width = image_raw.shape
    text_rows = text_raw.shape[0]
    half = text_rows // N_TENSOR
    hidden_here = hidden_pre.shape[1]

    text_unit, text_length = unit_rows(text_raw)
    text_key = text_unit.astype(bf16)
    text_half = lax.dynamic_slice_in_dim(text_key, tensor_index * half, half, 0)
    rels = jnp.array([0, 2, 4, 6, 1, 3, 5, 7], jnp.int32)
    text_window = block_window(text_half, True, core).reshape(WINDOW * half, width)

    lane = lax.broadcasted_iota(jnp.int32, (image_rows, LANES), 1)
    marks = jnp.where(
        lane == 0, (pair_offset // 64)[:, None], jnp.where(lane == 1, (pair_offset % 64)[:, None], 0)
    ).astype(bf16)
    image_other = tensor_swap(jnp.concatenate([image_raw, marks], axis=1))
    other_offset = read_marks(image_other[:, width:])
    image_all = jnp.concatenate([image_raw, image_other[:, :width]], axis=0)
    image_unit, image_length = unit_rows(image_all)
    image_key = image_unit.astype(bf16)
    row = jnp.arange(image_rows, dtype=jnp.int32)
    own_row = row + tensor_index * image_rows
    other_row = row + (1 - tensor_index) * image_rows

    columns = 9 * LANES
    start = 8 * LANES
    wide = 10 * LANES
    patches = normed_patches.shape[0]
    normed_other = torus_send(normed_patches, core=1)
    cotangent_other = torus_send(head_cotangent, core=1)
    share_other = torus_send(pool_share, core=1)
    hidden_other = torus_send(hidden_pre, core=1)
    weight_padded = jnp.pad(down_weight, ((0, start + wide - hidden_here), (0, 0)))
    weight_mine = lax.dynamic_slice_in_dim(weight_padded, core * start, wide, 0)
    base_own, slope_own = hidden_base(core, head_cotangent, weight_mine, hidden_pre)
    base_other, slope_other = hidden_base(core, cotangent_other, weight_mine, hidden_other)
    patch_pad = base_own.shape[0] - patches
    normed_t = jnp.concatenate(
        [jnp.pad(part.T, ((0, 0), (0, patch_pad))) for part in (normed_patches, normed_other)], axis=1
    )
    shares = jnp.pad(jnp.stack([pool_share, share_other]), ((0, 0), (0, patch_pad)))[:, :, None]

    text_place = (tensor_index * half + jnp.arange(half, dtype=jnp.int32))[None, :] - 64 * rels[:, None]
    image_target = jnp.concatenate([own_row - pair_offset, other_row - other_offset])
    weight = pair_weight(
        image_key, text_window, image_target, text_place.reshape(-1), logit_scale, logit_bias
    )
    image_part = jnp.dot(weight, text_window, preferred_element_type=f32)
    zero_row = jnp.where(tensor_index == 0, image_part[:1], image_part[image_rows : image_rows + 1])
    zero_dir = logit_scale * (zero_row + tensor_swap(zero_row))
    zero_unit = jnp.where(tensor_index == 0, image_unit[:1], image_unit[image_rows : image_rows + 1])
    zero_length = jnp.where(tensor_index == 0, image_length[:1], image_length[image_rows : image_rows + 1])
    pooled = project_back(zero_unit, zero_length, zero_dir).astype(bf16)
    pooled_both = jnp.concatenate([pooled, torus_send(pooled, core=1)], axis=0)

    lift = dot_nt(pooled_both, weight_mine[:columns])
    hops = [(1, 2), (0, 2), (1, 1), (1, 3), (1, 0), (0, 1), (0, 3), (0, 0)]
    targets = jnp.stack([(yh + dy) % N_YH * N_X + (x + dx) % N_X for dy, dx in hops])
    terms = up_terms(targets, normed_t, base_own, base_other, slope_own, slope_other, shares, lift)
    total = terms[-1]
    for (dy, dx), term in zip(hops[:-1], terms):
        total = total + torus_send(term, yh=dy, x=dx).astype(f32)

    rows_chip = total.shape[0] // N_Z
    chunks = total.reshape(N_Z, rows_chip, columns)
    total = lax.dynamic_index_in_dim(chunks, z, 0, keepdims=False)
    for dz in (4, 3, 5, 2, 6, 1, 7):
        chunk = lax.dynamic_index_in_dim(chunks, (z + dz) % N_Z, 0, keepdims=False).astype(bf16)
        total = total + torus_send(chunk, z=dz).astype(f32)
    rows_here = rows_chip // N_CORE
    mine = jnp.where(core == 0, total[:rows_here], total[rows_here:])
    theirs = torus_send(jnp.where(core == 0, total[rows_here:], total[:rows_here]), core=1)
    left = jnp.where(core == 0, mine, theirs)
    right = jnp.where(core == 0, theirs, mine)
    up_grad = jnp.concatenate([left, right[:, columns - start : hidden_here - start]], axis=1)

    image_dir = logit_scale * (image_part[:image_rows] + tensor_swap(image_part[image_rows:]))
    image_grad = project_back(image_unit[:image_rows], image_length[:image_rows], image_dir).astype(bf16)

    image_ext = jnp.concatenate([image_key[:image_rows], marks], axis=1)
    image_ext, _ = lax.optimization_barrier((image_ext, terms[-1]))
    image_window = block_window(image_ext, False, core).reshape(WINDOW * image_rows, width + LANES)
    window_key = image_window[:, :width]
    window_offset = read_marks(image_window[:, width:])
    window_row = (own_row[None, :] + 64 * rels[:, None]).reshape(-1)
    weight = pair_weight(
        window_key,
        text_key,
        window_row - window_offset,
        jnp.arange(text_rows, dtype=jnp.int32),
        logit_scale,
        logit_bias,
    )
    text_part = dot_tn(weight, window_key)
    text_dir = logit_scale * (text_part + tensor_swap(text_part))
    text_grad = project_back(text_unit, text_length, text_dir).astype(bf16)
    return (image_grad, text_grad, up_grad)


def solution(mesh):
    return jax.shard_map(
        per_device,
        mesh=mesh,
        in_specs=(
            P(("dp", "tensor"), None),
            P("dp", None),
            P(),
            P(),
            P(("dp", "tensor")),
            P("dp", None),
            P("dp", None),
            P("dp", "tensor"),
            P("dp"),
            P("tensor", None),
        ),
        out_specs=(P(("dp", "tensor"), None), P("dp", None), P("dp", "tensor")),
        check_vma=False,
    )
```

```python
import functools

import jax
import jax.numpy as jnp
from jax import lax
from jax.experimental import pallas as pl
from jax.experimental.pallas import tpu as pltpu
from jax.sharding import PartitionSpec as P

WINDOW = 8
N_YH, N_X, N_Z, N_CORE = 2, 4, 8, 2
N_DP = N_YH * N_X * N_Z * N_CORE
N_TENSOR = 2
LANES = 128

epsilon = 1e-06
gelu_root = 0.7978845608028654
gelu_cubic = 0.044715

f32 = jnp.float32
bf16 = jnp.bfloat16


def encode(yh, x, z, core):
    return (((yh % N_YH) * N_X + x % N_X) * N_Z + z % N_Z) * N_CORE + core % N_CORE


def torus_pairs(yh=0, x=0, z=0, core=0):
    pairs = []
    for j in range(N_DP):
        own = (j // (N_CORE * N_Z * N_X), j // (N_CORE * N_Z) % N_X, j // N_CORE % N_Z, j % N_CORE)
        pairs.append((j, encode(own[0] + yh, own[1] + x, own[2] + z, own[3] + core)))
    return pairs


def torus_send(array, **shift):
    return lax.ppermute(array, "dp", torus_pairs(**shift))


def ring_send(array, by, only=None):
    pairs = [(j, (j + by) % N_DP) for j in range(N_DP) if only is None or j % N_CORE == only]
    return lax.ppermute(array, "dp", pairs)


def tensor_swap(array):
    return lax.ppermute(array, "tensor", [(0, 1), (1, 0)])


def unit_rows(raw_rows):
    widened = raw_rows.astype(f32)
    lengths = jnp.sqrt(jnp.sum(widened * widened, axis=-1, keepdims=True) + epsilon)
    return (widened / lengths, lengths)


def project_back(unit_part, lengths, direction):
    radial = jnp.sum(unit_part * direction, axis=-1, keepdims=True)
    return (direction - unit_part * radial) / lengths


def gelu_slope(hidden_in):
    square = hidden_in * hidden_in
    tangent = jnp.tanh(hidden_in * (gelu_root + gelu_root * gelu_cubic * square))
    inner_slope = hidden_in * (0.5 * gelu_root + 1.5 * gelu_root * gelu_cubic * square)
    return 0.5 + 0.5 * tangent + (1.0 - tangent * tangent) * inner_slope


def dot_nt(a, b):
    return lax.dot_general(a, b, (((1,), (1,)), ((), ())), preferred_element_type=f32)


def dot_tn(a, b):
    return lax.dot_general(a, b, (((0,), (0,)), ((), ())), preferred_element_type=f32)


def key_rows(raw):
    return unit_rows(raw)[0].astype(bf16)


def text_key_kernel(half, place_ref, raw_ref, half_ref):
    begin = pl.multiple_of(place_ref[1] * half, half)
    half_ref[...] = key_rows(raw_ref[pl.ds(begin, half), :])


def text_half_key(place, text_raw, half):
    return pl.pallas_call(
        functools.partial(text_key_kernel, half),
        in_specs=[pl.BlockSpec(memory_space=pltpu.SMEM), pl.BlockSpec(memory_space=pltpu.VMEM)],
        out_specs=pl.BlockSpec(memory_space=pltpu.VMEM),
        out_shape=jax.ShapeDtypeStruct((half, text_raw.shape[1]), bf16),
    )(place, text_raw)


def pair_kernel(n_fixed, place_ref, scalar_ref, fixed_value_ref, window_value_ref, valid_ref, *refs):
    fixed_refs, window_refs = refs[:n_fixed], refs[n_fixed:-4]
    part_ref, zero_ref, fixed_key, window_key = refs[-4:]
    width = fixed_key.shape[1]
    begin = 0
    for ref in fixed_refs:
        fixed_key[begin : begin + ref.shape[0], :] = key_rows(ref[...])
        begin += ref.shape[0]
    begin = 0
    for ref in window_refs:
        window_key[begin : begin + ref.shape[0], :] = ref[:, :width]
        begin += ref.shape[0]
    scale = scalar_ref[0]
    logits = scale * dot_nt(fixed_key[...], window_key[...]) + scalar_ref[1]
    target = (fixed_value_ref[...] == window_value_ref[...]).astype(f32)
    weight = jnp.where(valid_ref[...] > 0, jax.nn.sigmoid(logits) - target, 0.0).astype(bf16)
    part = jnp.dot(weight, window_key[...], preferred_element_type=f32)
    part_ref[...] = part
    half = part.shape[0] // 2
    zero_ref[...] = jnp.where(place_ref[1] == 0, part[:1], part[half : half + 1])


def pair_products(place, scalars, fixed_value, window_value, valid, fixed, window):
    width = fixed[0].shape[1]
    rows = fixed_value.shape[0]
    depth = window_value.shape[0]
    smem = pl.BlockSpec(memory_space=pltpu.SMEM)
    vmem = pl.BlockSpec(memory_space=pltpu.VMEM)
    return pl.pallas_call(
        functools.partial(pair_kernel, len(fixed)),
        in_specs=[smem, smem] + [vmem] * (3 + len(fixed) + len(window)),
        out_specs=[vmem, vmem],
        out_shape=[jax.ShapeDtypeStruct((rows, width), f32), jax.ShapeDtypeStruct((1, width), f32)],
        scratch_shapes=[pltpu.VMEM((rows, width), bf16), pltpu.VMEM((depth, width), bf16)],
        compiler_params=pltpu.CompilerParams(vmem_limit_bytes=16 * 2**20),
        cost_estimate=pl.CostEstimate(
            flops=4 * rows * depth * width, bytes_accessed=4 * (rows + depth) * width, transcendentals=rows * depth
        ),
    )(
        place,
        scalars,
        fixed_value[:, None],
        window_value[None, :],
        valid.astype(jnp.int32)[None, :],
        *fixed,
        *window,
    )


def pooled_kernel(place_ref, scalar_ref, own_ref, other_ref, mine_ref, theirs_ref, pooled_ref):
    raw = jnp.where(place_ref[1] == 0, own_ref[:1, :].astype(f32), other_ref[:1, :].astype(f32))
    unit, length = unit_rows(raw)
    direction = scalar_ref[0] * (mine_ref[...] + theirs_ref[...])
    pooled_ref[...] = project_back(unit, length, direction).astype(bf16)


def pooled_row(place, scalars, own, other, mine, theirs):
    smem = pl.BlockSpec(memory_space=pltpu.SMEM)
    vmem = pl.BlockSpec(memory_space=pltpu.VMEM)
    return pl.pallas_call(
        pooled_kernel,
        in_specs=[smem, smem] + [vmem] * 4,
        out_specs=vmem,
        out_shape=jax.ShapeDtypeStruct(mine.shape, bf16),
    )(place, scalars, own, other, mine, theirs)


def transpose_kernel(patches, normed_ref, out_ref):
    block = normed_ref[...]
    kept = lax.broadcasted_iota(jnp.int32, block.shape, 0) < patches
    out_ref[...] = jnp.where(kept, block, jnp.zeros_like(block)).T


def transposed(normed, rows):
    patches, width = normed.shape
    step = 3 * LANES
    return pl.pallas_call(
        functools.partial(transpose_kernel, patches),
        grid=(width // step,),
        in_specs=[pl.BlockSpec((rows, step), lambda i: (0, i))],
        out_specs=pl.BlockSpec((step, rows), lambda i: (i, 0)),
        out_shape=jax.ShapeDtypeStruct((width, rows), bf16),
        compiler_params=pltpu.CompilerParams(vmem_limit_bytes=16 * 2**20),
        cost_estimate=pl.CostEstimate(flops=0, bytes_accessed=4 * rows * width, transcendentals=0),
    )(normed)


def read_marks(marks):
    lane = lax.broadcasted_iota(jnp.int32, marks.shape, 1)
    scale = jnp.where(lane == 0, 64.0, jnp.where(lane == 1, 1.0, 0.0))
    return jnp.sum(marks.astype(f32) * scale, axis=-1).astype(jnp.int32)


def base_kernel(patches, core_ref, cotangent_ref, weight_ref, hidden_ref, base_ref, slope_ref):
    grad = dot_nt(cotangent_ref[...], weight_ref[...])
    slope = gelu_slope(hidden_ref[...].astype(f32))
    kept = lax.broadcasted_iota(jnp.int32, slope.shape, 0) < patches
    slope_ref[...] = jnp.where(kept, slope, 0.0).astype(bf16)
    base_ref[...] = jnp.where(kept, grad * slope, 0.0)


def hidden_base(core, cotangent, weight, hidden):
    patches, width = cotangent.shape
    wide = 10 * LANES
    step = 2 * LANES
    rows = -(-patches // step) * step
    return pl.pallas_call(
        functools.partial(base_kernel, patches),
        grid_spec=pltpu.PrefetchScalarGridSpec(
            num_scalar_prefetch=1,
            grid=(wide // step,),
            in_specs=[
                pl.BlockSpec((rows, width), lambda i, core: (0, 0)),
                pl.BlockSpec((step, width), lambda i, core: (4 * core[0] + i, 0)),
                pl.BlockSpec((rows, step), lambda i, core: (0, 4 * core[0] + i)),
            ],
            out_specs=[
                pl.BlockSpec((rows, step), lambda i, core: (0, i)),
                pl.BlockSpec((rows, step), lambda i, core: (0, i)),
            ],
        ),
        out_shape=[
            jax.ShapeDtypeStruct((rows, wide), f32),
            jax.ShapeDtypeStruct((rows, wide), bf16),
        ],
        compiler_params=pltpu.CompilerParams(vmem_limit_bytes=32 * 2**20),
        cost_estimate=pl.CostEstimate(
            flops=2 * rows * width * wide, bytes_accessed=12 * rows * wide, transcendentals=rows * wide
        ),
    )(core[None], cotangent, weight, hidden)


def terms_kernel(
    targets_ref,
    normed0_ref,
    normed1_ref,
    base0_ref,
    base1_ref,
    slope0_ref,
    slope1_ref,
    share_ref,
    lift_ref,
    *refs,
):
    outs, pre_ref = refs[:-1], refs[-1]
    rows = base0_ref.shape[0]
    for image, (base_ref, slope_ref) in enumerate(((base0_ref, slope0_ref), (base1_ref, slope1_ref))):
        lifted = share_ref[image] * lift_ref[image : image + 1, :]
        grad = base_ref[...] + lifted * slope_ref[...].astype(f32)
        pre_ref[image * rows : (image + 1) * rows, :] = grad.astype(bf16)
    height = outs[0].shape[0]
    for slot, out in enumerate(outs):
        begin = pl.multiple_of(targets_ref[slot] * height, 16)
        product = jnp.dot(normed0_ref[pl.ds(begin, height), :], pre_ref[:rows, :], preferred_element_type=f32)
        product += jnp.dot(normed1_ref[pl.ds(begin, height), :], pre_ref[rows:, :], preferred_element_type=f32)
        out[...] = product.astype(out.dtype)


def up_terms(targets, columns, normed_t, base_own, base_other, slope_own, slope_other, shares, lift):
    count = targets.shape[0]
    width, rows = normed_t[0].shape
    step = 2 * LANES
    height = width // count
    kinds = [bf16] * (count - 1) + [f32]
    image_spec = pl.BlockSpec((rows, step), lambda i, targets: (0, i))
    return pl.pallas_call(
        terms_kernel,
        grid_spec=pltpu.PrefetchScalarGridSpec(
            num_scalar_prefetch=1,
            grid=(-(-columns // step),),
            in_specs=[
                pl.BlockSpec((width, rows), lambda i, targets: (0, 0)),
                pl.BlockSpec((width, rows), lambda i, targets: (0, 0)),
                image_spec,
                image_spec,
                image_spec,
                image_spec,
                pl.BlockSpec((2, rows, 1), lambda i, targets: (0, 0, 0)),
                pl.BlockSpec((2, step), lambda i, targets: (0, i)),
            ],
            out_specs=[pl.BlockSpec((height, step), lambda i, targets: (0, i))] * count,
            scratch_shapes=[pltpu.VMEM((2 * rows, step), bf16)],
        ),
        out_shape=[jax.ShapeDtypeStruct((height, columns), kind) for kind in kinds],
        compiler_params=pltpu.CompilerParams(vmem_limit_bytes=32 * 2**20),
        cost_estimate=pl.CostEstimate(
            flops=4 * width * rows * columns, bytes_accessed=16 * rows * columns, transcendentals=0
        ),
    )(targets, *normed_t, base_own, base_other, slope_own, slope_other, shares, lift)


def per_device(
    image_raw,
    text_raw,
    logit_scale,
    logit_bias,
    pair_offset,
    normed_patches,
    head_cotangent,
    hidden_pre,
    pool_share,
    down_weight,
):
    place = lax.axis_index("dp")
    tensor_index = lax.axis_index("tensor")
    yh = place // (N_CORE * N_Z * N_X)
    x = place // (N_CORE * N_Z) % N_X
    z = place // N_CORE % N_Z
    core = place % N_CORE
    image_rows, width = image_raw.shape
    text_rows = text_raw.shape[0]
    half = text_rows // N_TENSOR
    hidden_here = hidden_pre.shape[1]
    spot = jnp.stack([core, tensor_index]).astype(jnp.int32)
    scalars = jnp.stack([logit_scale, logit_bias])

    text_half = text_half_key(spot, text_raw, half)
    text_far = ring_send(text_half, 7, only=1)
    text_near = jnp.concatenate([text_half, ring_send(text_half, 2)], axis=0)
    text_next = ring_send(text_near, 4)
    text_window = [text_near, text_next, torus_send(text_near, core=1), torus_send(text_next, core=1), text_far]
    rels = jnp.concatenate(
        [
            jnp.array([0, 2, 4, 6], jnp.int32),
            jnp.array([-1, 1, 3, 5], jnp.int32) + 2 * core,
            jnp.array([7], jnp.int32) + 2 * core,
        ]
    )
    text_row = jnp.arange(half, dtype=jnp.int32) + tensor_index * half
    text_value = (text_row[None, :] - text_rows * rels[:, None]).reshape(-1)
    text_valid = jnp.repeat((rels >= 0) & (rels < WINDOW), half)

    image_other = tensor_swap(image_raw)
    offset_other = tensor_swap(pair_offset)
    row = jnp.arange(image_rows, dtype=jnp.int32)
    own_row = row + tensor_index * image_rows
    other_row = row + (1 - tensor_index) * image_rows
    image_value = jnp.concatenate([own_row - pair_offset, other_row - offset_other])

    columns = 9 * LANES
    start = 8 * LANES
    wide = 10 * LANES
    patches = normed_patches.shape[0]
    cotangent_other = torus_send(head_cotangent, core=1)
    hidden_other = torus_send(hidden_pre, core=1)
    share_other = torus_send(pool_share, core=1)
    base_own, slope_own = hidden_base(core, head_cotangent, down_weight, hidden_pre)
    padded = base_own.shape[0]
    normed_own = transposed(normed_patches, padded)
    normed_other = torus_send(normed_own, core=1)
    base_other, slope_other = hidden_base(core, cotangent_other, down_weight, hidden_other)
    shares = jnp.pad(jnp.stack([pool_share, share_other]), ((0, 0), (0, padded - patches)))[:, :, None]
    weight_padded = jnp.pad(down_weight, ((0, start + wide - hidden_here), (0, 0)))
    weight_mine = lax.dynamic_slice_in_dim(weight_padded, core * start, wide, 0)

    image_part, zero_row = pair_products(
        spot, scalars, image_value, text_value, text_valid, [image_raw, image_other], text_window
    )
    zero_theirs = tensor_swap(zero_row)
    zero_theirs, base_other, slope_other, weight_mine, shares = lax.optimization_barrier(
        (zero_theirs, base_other, slope_other, weight_mine, shares)
    )
    pooled = pooled_row(spot, scalars, image_raw, image_other, zero_row, zero_theirs)
    pooled_both = jnp.concatenate([pooled, torus_send(pooled, core=1)], axis=0)

    lift = dot_nt(pooled_both, weight_mine)
    hops = [(1, 2), (0, 2), (1, 1), (1, 3), (1, 0), (0, 1), (0, 3), (0, 0)]
    targets = jnp.stack([(yh + dy) % N_YH * N_X + (x + dx) % N_X for dy, dx in hops])
    terms = up_terms(
        targets, columns, [normed_own, normed_other], base_own, base_other, slope_own, slope_other, shares, lift
    )
    arrived = [torus_send(term, yh=dy, x=dx) for (dy, dx), term in zip(hops[:-1], terms)]
    total = terms[-1]
    for term in arrived:
        total = total + term.astype(f32)

    rows_chip = total.shape[0] // N_Z
    chunks = total.reshape(N_Z, rows_chip, columns)
    total = lax.dynamic_index_in_dim(chunks, z, 0, keepdims=False)
    for dz in (4, 3, 5, 2, 6, 1, 7):
        chunk = lax.dynamic_index_in_dim(chunks, (z + dz) % N_Z, 0, keepdims=False).astype(bf16)
        total = total + torus_send(chunk, z=dz).astype(f32)
    rows_here = rows_chip // N_CORE
    mine = jnp.where(core == 0, total[:rows_here], total[rows_here:])
    theirs = torus_send(jnp.where(core == 0, total[rows_here:], total[:rows_here]), core=1)
    left = jnp.where(core == 0, mine, theirs)
    right = jnp.where(core == 0, theirs, mine)
    up_grad = jnp.concatenate([left, right[:, columns - start : hidden_here - start]], axis=1)

    image_unit, image_length = unit_rows(image_raw)
    image_dir = logit_scale * (image_part[:image_rows] + tensor_swap(image_part[image_rows:]))
    image_grad = project_back(image_unit, image_length, image_dir).astype(bf16)

    lane = lax.broadcasted_iota(jnp.int32, (image_rows, LANES), 1)
    marks = jnp.where(
        lane == 0, (pair_offset // 64)[:, None], jnp.where(lane == 1, (pair_offset % 64)[:, None], 0)
    ).astype(bf16)
    image_ext = jnp.concatenate([image_unit.astype(bf16), marks], axis=1)
    image_ext, _ = lax.optimization_barrier((image_ext, arrived[5]))
    image_near = jnp.concatenate([image_ext, ring_send(image_ext, -2)], axis=0)
    image_even = jnp.concatenate([image_near, ring_send(image_near, -4)], axis=0)
    image_odd = ring_send(image_even, -1)
    window_row = own_row[None, :] + 2 * text_rows * jnp.arange(WINDOW // 2, dtype=jnp.int32)[:, None]
    window_row = jnp.concatenate([window_row, window_row + text_rows]).reshape(-1)
    window_offset = jnp.concatenate([read_marks(image_even[:, width:]), read_marks(image_odd[:, width:])])
    text_part, _ = pair_products(
        spot,
        scalars,
        jnp.arange(text_rows, dtype=jnp.int32),
        window_row - window_offset,
        jnp.ones_like(window_row),
        [text_raw],
        [image_even, image_odd],
    )
    text_unit, text_length = unit_rows(text_raw)
    text_dir = logit_scale * (text_part + tensor_swap(text_part))
    text_grad = project_back(text_unit, text_length, text_dir).astype(bf16)
    return (image_grad, text_grad, up_grad)


def solution(mesh):
    return jax.shard_map(
        per_device,
        mesh=mesh,
        in_specs=(
            P(("dp", "tensor"), None),
            P("dp", None),
            P(),
            P(),
            P(("dp", "tensor")),
            P("dp", None),
            P("dp", None),
            P("dp", "tensor"),
            P("dp"),
            P("tensor", None),
        ),
        out_specs=(P(("dp", "tensor"), None), P("dp", None), P("dp", "tensor")),
        check_vma=False,
    )
```

```python
import functools

import jax
import jax.numpy as jnp
from jax import lax
from jax.experimental import pallas as pl
from jax.experimental.pallas import tpu as pltpu
from jax.sharding import PartitionSpec as P

WINDOW = 8
N_YH, N_X, N_Z, N_CORE = 2, 4, 8, 2
N_DP = N_YH * N_X * N_Z * N_CORE
N_TENSOR = 2
LANES = 128
LIGHT = pl.CostEstimate(flops=1, bytes_accessed=1, transcendentals=0)

epsilon = 1e-06
gelu_root = 0.7978845608028654
gelu_cubic = 0.044715

f32 = jnp.float32
bf16 = jnp.bfloat16


def encode(yh, x, z, core):
    return (((yh % N_YH) * N_X + x % N_X) * N_Z + z % N_Z) * N_CORE + core % N_CORE


def torus_pairs(yh=0, x=0, z=0, core=0):
    pairs = []
    for j in range(N_DP):
        own = (j // (N_CORE * N_Z * N_X), j // (N_CORE * N_Z) % N_X, j // N_CORE % N_Z, j % N_CORE)
        pairs.append((j, encode(own[0] + yh, own[1] + x, own[2] + z, own[3] + core)))
    return pairs


def torus_send(array, **shift):
    return lax.ppermute(array, "dp", torus_pairs(**shift))


def ring_send(array, by, only=None):
    pairs = [(j, (j + by) % N_DP) for j in range(N_DP) if only is None or j % N_CORE == only]
    return lax.ppermute(array, "dp", pairs)


def tensor_swap(array):
    return lax.ppermute(array, "tensor", [(0, 1), (1, 0)])


def unit_rows(raw_rows):
    widened = raw_rows.astype(f32)
    lengths = jnp.sqrt(jnp.sum(widened * widened, axis=-1, keepdims=True) + epsilon)
    return (widened / lengths, lengths)


def project_back(unit_part, lengths, direction):
    radial = jnp.sum(unit_part * direction, axis=-1, keepdims=True)
    return (direction - unit_part * radial) / lengths


def gelu_slope(hidden_in):
    square = hidden_in * hidden_in
    tangent = jnp.tanh(hidden_in * (gelu_root + gelu_root * gelu_cubic * square))
    inner_slope = hidden_in * (0.5 * gelu_root + 1.5 * gelu_root * gelu_cubic * square)
    return 0.5 + 0.5 * tangent + (1.0 - tangent * tangent) * inner_slope


def dot_nt(a, b):
    return lax.dot_general(a, b, (((1,), (1,)), ((), ())), preferred_element_type=f32)


def dot_tn(a, b):
    return lax.dot_general(a, b, (((0,), (0,)), ((), ())), preferred_element_type=f32)


def key_rows(raw):
    return unit_rows(raw)[0].astype(bf16)


def text_key_kernel(half, place_ref, raw_ref, half_ref):
    begin = pl.multiple_of(place_ref[1] * half, half)
    half_ref[...] = key_rows(raw_ref[pl.ds(begin, half), :])


def text_half_key(place, text_raw, half):
    return pl.pallas_call(
        functools.partial(text_key_kernel, half),
        in_specs=[pl.BlockSpec(memory_space=pltpu.SMEM), pl.BlockSpec(memory_space=pltpu.VMEM)],
        out_specs=pl.BlockSpec(memory_space=pltpu.VMEM),
        out_shape=jax.ShapeDtypeStruct((half, text_raw.shape[1]), bf16),
    )(place, text_raw)


def pair_kernel(place_ref, scalar_ref, value_ref, window_value_ref, valid_ref, own_ref, other_ref, *refs):
    window_refs = refs[:-5]
    part_ref, zero_ref, weight_ref, key_ref, window_key = refs[-5:]
    half = own_ref.shape[0]
    key_ref[:half, :] = key_rows(own_ref[...])
    key_ref[half:, :] = key_rows(other_ref[...])
    begin = 0
    for ref in window_refs:
        window_key[begin : begin + ref.shape[0], :] = ref[...]
        begin += ref.shape[0]
    logits = scalar_ref[0] * dot_nt(key_ref[...], window_key[...]) + scalar_ref[1]
    target = (value_ref[...] == window_value_ref[...]).astype(f32)
    weight = jnp.where(valid_ref[...] > 0, jax.nn.sigmoid(logits) - target, 0.0).astype(bf16)
    weight_ref[...] = weight
    part = jnp.dot(weight, window_key[...], preferred_element_type=f32)
    part_ref[...] = part
    zero_ref[...] = jnp.where(place_ref[1] == 0, part[:1], part[half : half + 1])


def pair_products(place, scalars, value, window_value, valid, own, other, window):
    width = own.shape[1]
    rows = value.shape[0]
    depth = window_value.shape[0]
    smem = pl.BlockSpec(memory_space=pltpu.SMEM)
    vmem = pl.BlockSpec(memory_space=pltpu.VMEM)
    return pl.pallas_call(
        pair_kernel,
        in_specs=[smem, smem] + [vmem] * (5 + len(window)),
        out_specs=[vmem] * 4,
        out_shape=[
            jax.ShapeDtypeStruct((rows, width), f32),
            jax.ShapeDtypeStruct((1, width), f32),
            jax.ShapeDtypeStruct((rows, depth), bf16),
            jax.ShapeDtypeStruct((rows, width), bf16),
        ],
        scratch_shapes=[pltpu.VMEM((depth, width), bf16)],
        compiler_params=pltpu.CompilerParams(vmem_limit_bytes=16 * 2**20),
        cost_estimate=LIGHT,
    )(
        place,
        scalars,
        value[:, None],
        window_value[None, :],
        valid.astype(jnp.int32)[None, :],
        own,
        other,
        *window,
    )


def pooled_kernel(place_ref, scalar_ref, own_ref, other_ref, mine_ref, theirs_ref, pooled_ref):
    raw = jnp.where(place_ref[1] == 0, own_ref[:1, :].astype(f32), other_ref[:1, :].astype(f32))
    unit, length = unit_rows(raw)
    direction = scalar_ref[0] * (mine_ref[...] + theirs_ref[...])
    pooled_ref[...] = project_back(unit, length, direction).astype(bf16)


def pooled_row(place, scalars, own, other, mine, theirs):
    smem = pl.BlockSpec(memory_space=pltpu.SMEM)
    vmem = pl.BlockSpec(memory_space=pltpu.VMEM)
    return pl.pallas_call(
        pooled_kernel,
        in_specs=[smem, smem] + [vmem] * 4,
        out_specs=vmem,
        out_shape=jax.ShapeDtypeStruct(mine.shape, bf16),
    )(place, scalars, own, other, mine, theirs)


def transpose_kernel(patches, normed_ref, out_ref):
    block = normed_ref[...]
    kept = lax.broadcasted_iota(jnp.int32, block.shape, 0) < patches
    out_ref[...] = jnp.where(kept, block, jnp.zeros_like(block)).T


def transposed(normed, rows):
    patches, width = normed.shape
    step = 3 * LANES
    return pl.pallas_call(
        functools.partial(transpose_kernel, patches),
        grid=(width // step,),
        in_specs=[pl.BlockSpec((rows, step), lambda i: (0, i))],
        out_specs=pl.BlockSpec((step, rows), lambda i: (i, 0)),
        out_shape=jax.ShapeDtypeStruct((width, rows), bf16),
        compiler_params=pltpu.CompilerParams(vmem_limit_bytes=8 * 2**20),
        cost_estimate=LIGHT,
    )(normed)


def copy_all(pairs, sems, first):
    copies = [pltpu.make_async_copy(src, dst, sems.at[first + i]) for i, (src, dst) in enumerate(pairs)]
    for copy in copies:
        copy.start()
    return copies


def base_kernel(
    place_ref,
    share_ref,
    weight_tail,
    hidden_tail,
    cotangent_hbm,
    weight_hbm,
    hidden_hbm,
    base_hbm,
    slope_hbm,
    cotangent,
    weight,
    hidden,
    base,
    slope,
    sems,
):
    patches, columns = base.shape
    start = columns - LANES
    step = start // 2
    begin = place_ref[0] * start
    halves = [pl.ds(pl.multiple_of(begin + i * step, step), step) for i in range(2)]
    wheres = [pl.ds(i * step, step) for i in range(2)]
    loads = copy_all(
        [
            (cotangent_hbm, cotangent),
            (weight_hbm.at[halves[0], :], weight.at[wheres[0], :]),
            (hidden_hbm.at[:, halves[0]], hidden.at[:, wheres[0]]),
            (weight_hbm.at[halves[1], :], weight.at[wheres[1], :]),
            (hidden_hbm.at[:, halves[1]], hidden.at[:, wheres[1]]),
        ],
        sems,
        0,
    )
    share = share_ref[...].T[:patches, :1]

    def block(weight_rows, hidden_block, where):
        kept = gelu_slope(hidden_block.astype(f32))
        slope[:, where] = (share * kept).astype(bf16)
        base[:, where] = dot_nt(cotangent[...], weight_rows) * kept

    stores = []
    loads[0].wait()
    for i, where in enumerate(wheres):
        loads[1 + 2 * i].wait()
        loads[2 + 2 * i].wait()
        block(weight[where, :], hidden[:, where], where)
        stores += copy_all(
            [(base.at[:, where], base_hbm.at[:, where]), (slope.at[:, where], slope_hbm.at[:, where])],
            sems,
            5 + 2 * i,
        )
    where = pl.ds(start, LANES)
    block(weight_tail[...], hidden_tail[...], where)
    stores += copy_all(
        [(base.at[:, where], base_hbm.at[:, where]), (slope.at[:, where], slope_hbm.at[:, where])], sems, 9
    )
    for copy in stores:
        copy.wait()


def hidden_base(place, columns, cotangent, share, weight, hidden, tails):
    patches, width = cotangent.shape
    start = columns - LANES
    vmem = pl.BlockSpec(memory_space=pltpu.VMEM)
    hbm = pl.BlockSpec(memory_space=pl.ANY)
    return pl.pallas_call(
        base_kernel,
        in_specs=[pl.BlockSpec(memory_space=pltpu.SMEM), vmem, vmem, vmem, hbm, hbm, hbm],
        out_specs=[hbm, hbm],
        out_shape=[
            jax.ShapeDtypeStruct((patches, columns), f32),
            jax.ShapeDtypeStruct((patches, columns), bf16),
        ],
        scratch_shapes=[
            pltpu.VMEM((patches, width), bf16),
            pltpu.VMEM((start, width), bf16),
            pltpu.VMEM((patches, start), bf16),
            pltpu.VMEM((patches, columns), f32),
            pltpu.VMEM((patches, columns), bf16),
            pltpu.SemaphoreType.DMA((11,)),
        ],
        compiler_params=pltpu.CompilerParams(vmem_limit_bytes=48 * 2**20),
        cost_estimate=LIGHT,
    )(place, share, *tails, cotangent, weight, hidden)


def terms_kernel(
    place_ref,
    targets_ref,
    pooled0_ref,
    pooled1_ref,
    weight_tail,
    normed0_hbm,
    normed1_hbm,
    base0_hbm,
    base1_hbm,
    slope0_hbm,
    slope1_hbm,
    weight_hbm,
    a_keep,
    a_sent1,
    a_sent2,
    a_sent3,
    c_keep,
    c_sent,
    weight,
    normed,
    base,
    slope,
    sum_a,
    sum_c,
    stage_a,
    stage_c,
    sems,
):
    _, patches, columns = base.shape
    width = weight.shape[1]
    start = columns - LANES
    split = a_keep.shape[2]
    height = a_keep.shape[1]
    begin = pl.multiple_of(place_ref[0] * start, start)
    loads = copy_all(
        [
            (weight_hbm.at[pl.ds(begin, start), :], weight),
            (slope0_hbm, slope.at[0]),
            (base0_hbm, base.at[0]),
            (normed0_hbm, normed.at[0]),
            (slope1_hbm, slope.at[1]),
            (base1_hbm, base.at[1]),
            (normed1_hbm, normed.at[1]),
        ],
        sems,
        0,
    )
    pooled = jnp.concatenate(
        [jnp.broadcast_to(ref[...].astype(f32), (8, width)) for ref in (pooled0_ref, pooled1_ref)], axis=0
    ).astype(bf16)
    loads[0].wait()
    lift = jnp.concatenate([dot_nt(pooled, weight[...]), dot_nt(pooled, weight_tail[...])], axis=1)

    def product(image, first, last):
        lifted = lift[8 * image : 8 * image + 1, first:last] * slope[image, :, first:last].astype(f32)
        grad = (base[image, :, first:last] + lifted).astype(bf16)
        return jnp.dot(normed[image, :, :patches], grad, preferred_element_type=f32)

    def rows(dy, dx):
        return pl.ds(pl.multiple_of(targets_ref[dy * N_X + dx] * height, 16), height)

    for copy in loads[1:4]:
        copy.wait()
    sum_c[...] = product(0, split, columns)
    for copy in loads[4:]:
        copy.wait()
    sum_c[...] += product(1, split, columns)
    for dx in range(N_X):
        stage_c[dx] = sum_c[rows(1, dx), :].astype(bf16)
    stores = copy_all(
        [(stage_c, c_sent)] + [(sum_c.at[rows(0, dx), :], c_keep.at[dx]) for dx in range(N_X)], sems, 7
    )
    sum_a[...] = product(0, 0, split) + product(1, 0, split)
    for dx in range(1, N_X):
        for dy in range(N_YH):
            stage_a[dx - 1, dy] = sum_a[rows(dy, dx), :].astype(bf16)
    stores += copy_all(
        [(stage_a.at[i], out) for i, out in enumerate((a_sent1, a_sent2, a_sent3))]
        + [(sum_a.at[rows(dy, 0), :], a_keep.at[dy]) for dy in range(N_YH)],
        sems,
        12,
    )
    for copy in stores:
        copy.wait()


def up_terms(place, targets, split, normed_t, base, slope, weight, weight_tail, pooled):
    width, depth = normed_t[0].shape
    patches, columns = base[0].shape
    height = width // (N_YH * N_X)
    vmem = pl.BlockSpec(memory_space=pltpu.VMEM)
    smem = pl.BlockSpec(memory_space=pltpu.SMEM)
    hbm = pl.BlockSpec(memory_space=pl.ANY)
    part_a, part_c = (N_YH, height, split), (N_X, height, columns - split)
    return pl.pallas_call(
        terms_kernel,
        in_specs=[smem, smem] + [vmem] * 3 + [hbm] * 7,
        out_specs=[hbm] * 6,
        out_shape=[
            jax.ShapeDtypeStruct(part_a, f32),
            jax.ShapeDtypeStruct(part_a, bf16),
            jax.ShapeDtypeStruct(part_a, bf16),
            jax.ShapeDtypeStruct(part_a, bf16),
            jax.ShapeDtypeStruct(part_c, f32),
            jax.ShapeDtypeStruct(part_c, bf16),
        ],
        scratch_shapes=[
            pltpu.VMEM((columns - LANES, width), bf16),
            pltpu.VMEM((2, width, depth), bf16),
            pltpu.VMEM((2, patches, columns), f32),
            pltpu.VMEM((2, patches, columns), bf16),
            pltpu.VMEM((width, split), f32),
            pltpu.VMEM((width, columns - split), f32),
            pltpu.VMEM((N_X - 1,) + part_a, bf16),
            pltpu.VMEM(part_c, bf16),
            pltpu.SemaphoreType.DMA((17,)),
        ],
        compiler_params=pltpu.CompilerParams(vmem_limit_bytes=48 * 2**20),
        cost_estimate=LIGHT,
    )(place, targets, *pooled, weight_tail, *normed_t, *base, *slope, weight)


def per_device(
    image_raw,
    text_raw,
    logit_scale,
    logit_bias,
    pair_offset,
    normed_patches,
    head_cotangent,
    hidden_pre,
    pool_share,
    down_weight,
):
    place = lax.axis_index("dp")
    tensor_index = lax.axis_index("tensor")
    yh = place // (N_CORE * N_Z * N_X)
    x = place // (N_CORE * N_Z) % N_X
    z = place // N_CORE % N_Z
    core = place % N_CORE
    image_rows, width = image_raw.shape
    text_rows = text_raw.shape[0]
    half = text_rows // N_TENSOR
    hidden_here = hidden_pre.shape[1]
    spot = jnp.stack([core, tensor_index]).astype(jnp.int32)
    scalars = jnp.stack([logit_scale, logit_bias])

    text_half = text_half_key(spot, text_raw, half)
    text_half, image_raw, pair_offset, normed_patches, head_cotangent, hidden_pre, pool_share = lax.optimization_barrier(
        (text_half, image_raw, pair_offset, normed_patches, head_cotangent, hidden_pre, pool_share)
    )
    text_far = ring_send(text_half, 7, only=1)
    text_near = jnp.concatenate([text_half, ring_send(text_half, 2)], axis=0)
    text_near, cotangent_own = lax.optimization_barrier((text_near, head_cotangent))
    text_next = ring_send(text_near, 4)
    text_window = [text_near, text_next, torus_send(text_near, core=1), torus_send(text_next, core=1), text_far]
    rels = jnp.concatenate(
        [
            jnp.array([0, 2, 4, 6], jnp.int32),
            jnp.array([-1, 1, 3, 5], jnp.int32) + 2 * core,
            jnp.array([7], jnp.int32) + 2 * core,
        ]
    )
    text_row = jnp.arange(half, dtype=jnp.int32) + tensor_index * half
    text_value = (text_row[None, :] - text_rows * rels[:, None]).reshape(-1)
    text_valid = jnp.repeat((rels >= 0) & (rels < WINDOW), half)

    image_other = tensor_swap(image_raw)
    offset_other = tensor_swap(pair_offset)
    row = jnp.arange(image_rows, dtype=jnp.int32)
    own_row = row + tensor_index * image_rows
    other_row = row + (1 - tensor_index) * image_rows
    image_value = jnp.concatenate([own_row - pair_offset, other_row - offset_other])

    columns = 9 * LANES
    start = 8 * LANES
    cotangent_other = torus_send(head_cotangent, core=1)
    hidden_other = torus_send(hidden_pre, core=1)
    share_other = torus_send(pool_share, core=1)
    last, missing = 2 * start, columns - (hidden_here - start)
    weight_tail = jnp.where(
        core == 0, down_weight[start:columns], jnp.pad(down_weight[last:], ((0, missing), (0, 0)))
    )
    tail_own, tail_other = [
        jnp.where(core == 0, part[:, start:columns], jnp.pad(part[:, last:], ((0, 0), (0, missing))))
        for part in (hidden_pre, hidden_other)
    ]
    share_own, share_other = [
        jnp.broadcast_to(jnp.pad(part, (0, 6 * LANES - part.shape[0]))[None, :], (8, 6 * LANES))
        for part in (pool_share, share_other)
    ]
    base_own, slope_own = hidden_base(
        spot, columns, cotangent_own, share_own, down_weight, hidden_pre, [weight_tail, tail_own]
    )
    normed_own = transposed(normed_patches, 6 * LANES)
    normed_other = torus_send(normed_own, core=1)

    text_last = text_window[3]
    text_last, base_own, slope_own, share_other, tail_other, weight_tail = lax.optimization_barrier(
        (text_last, base_own, slope_own, share_other, tail_other, weight_tail)
    )
    text_window[3] = text_last
    image_part, zero_row, weight, image_key = pair_products(
        spot, scalars, image_value, text_value, text_valid, image_raw, image_other, text_window
    )
    zero_theirs = tensor_swap(zero_row)

    text_part = dot_tn(weight, image_key)
    near, direct, ours = 2 * half, 4 * half, 8 * half
    returned = torus_send(text_part[direct:ours].astype(bf16), core=1)
    far = ring_send(text_part[ours:].astype(bf16), -7, only=0)
    image_swapped = tensor_swap(image_part[image_rows:].astype(bf16))
    zero_row, returned, cotangent_other = lax.optimization_barrier((zero_row, returned, cotangent_other))
    returned = returned.astype(f32)
    text_near = text_part[:near] + returned[:near]
    text_next = ring_send((text_part[near:direct] + returned[near:]).astype(bf16), -4)

    base_other, slope_other = hidden_base(
        spot, columns, cotangent_other, share_other, down_weight, hidden_other, [weight_tail, tail_other]
    )
    zero_theirs, base_other, slope_other = lax.optimization_barrier((zero_theirs, base_other, slope_other))
    pooled = pooled_row(spot, scalars, image_raw, image_other, zero_row, zero_theirs)
    pooled_other = torus_send(pooled, core=1)
    pooled_other, text_next, far, image_swapped = lax.optimization_barrier(
        (pooled_other, text_next, far, image_swapped)
    )

    split = 4 * LANES
    targets = jnp.stack(
        [(yh + dy) % N_YH * N_X + (x + dx) % N_X for dy in range(N_YH) for dx in range(N_X)]
    ).astype(jnp.int32)
    a_keep, a_sent1, a_sent2, a_sent3, c_keep, c_sent = up_terms(
        spot,
        targets,
        split,
        [normed_own, normed_other],
        [base_own, base_other],
        [slope_own, slope_other],
        down_weight,
        weight_tail,
        [pooled, pooled_other],
    )
    c_come = torus_send(c_sent, yh=1)
    a_come = [torus_send(part, x=dx) for dx, part in ((2, a_sent2), (1, a_sent1), (3, a_sent3))]
    c_keep = c_keep + c_come.astype(f32)
    a_keep = a_keep + (a_come[0].astype(f32) + a_come[1].astype(f32) + a_come[2].astype(f32))
    c_come = [torus_send(c_keep[dx].astype(bf16), x=dx) for dx in (2, 1, 3)]
    a_come = torus_send(a_keep[1].astype(bf16), yh=1)
    total = jnp.concatenate(
        [
            a_keep[0] + a_come.astype(f32),
            c_keep[0] + (c_come[0].astype(f32) + c_come[1].astype(f32) + c_come[2].astype(f32)),
        ],
        axis=1,
    )

    text_near = text_near + text_next.astype(f32)
    text_back = ring_send(text_near[half:].astype(bf16), -2)
    total, text_back = lax.optimization_barrier((total, text_back))
    text_dir = logit_scale * (text_near[:half] + text_back.astype(f32) + far.astype(f32))
    text_unit, text_length = unit_rows(lax.dynamic_slice_in_dim(text_raw, tensor_index * half, half, 0))
    text_mine = project_back(text_unit, text_length, text_dir).astype(bf16)

    image_unit, image_length = unit_rows(image_raw)
    image_dir = logit_scale * (image_part[:image_rows] + image_swapped.astype(f32))
    image_grad = project_back(image_unit, image_length, image_dir).astype(bf16)

    rows_chip = total.shape[0] // N_Z
    chunks = total.reshape(N_Z, rows_chip, columns)
    total = lax.dynamic_index_in_dim(chunks, z, 0, keepdims=False)
    for dz in (4, 3, 5, 2, 6, 1, 7):
        chunk = lax.dynamic_index_in_dim(chunks, (z + dz) % N_Z, 0, keepdims=False).astype(bf16)
        total = total + torus_send(chunk, z=dz).astype(f32)
    total, text_mine, image_grad = lax.optimization_barrier((total, text_mine, image_grad))
    rows_here = rows_chip // N_CORE
    mine = jnp.where(core == 0, total[:rows_here], total[rows_here:])
    theirs = torus_send(jnp.where(core == 0, total[rows_here:], total[:rows_here]), core=1)
    left = jnp.where(core == 0, mine, theirs)
    right = jnp.where(core == 0, theirs, mine)
    up_grad = jnp.concatenate([left, right[:, columns - start : hidden_here - start]], axis=1)

    text_theirs = tensor_swap(text_mine)
    text_grad = jnp.where(
        tensor_index == 0,
        jnp.concatenate([text_mine, text_theirs], axis=0),
        jnp.concatenate([text_theirs, text_mine], axis=0),
    )
    return (image_grad, text_grad, up_grad)


def solution(mesh):
    return jax.shard_map(
        per_device,
        mesh=mesh,
        in_specs=(
            P(("dp", "tensor"), None),
            P("dp", None),
            P(),
            P(),
            P(("dp", "tensor")),
            P("dp", None),
            P("dp", None),
            P("dp", "tensor"),
            P("dp"),
            P("tensor", None),
        ),
        out_specs=(P(("dp", "tensor"), None), P("dp", None), P("dp", "tensor")),
        check_vma=False,
    )
```

```python
import functools

import jax
import jax.numpy as jnp
from jax import lax
from jax.experimental import pallas as pl
from jax.experimental.pallas import tpu as pltpu
from jax.sharding import PartitionSpec as P

WINDOW = 8
N_YH, N_X, N_Z, N_CORE = 2, 4, 8, 2
N_DP = N_YH * N_X * N_Z * N_CORE
N_TENSOR = 2
LANES = 128
LIGHT = pl.CostEstimate(flops=1, bytes_accessed=1, transcendentals=0)

epsilon = 1e-06
gelu_root = 0.7978845608028654
gelu_cubic = 0.044715

f32 = jnp.float32
bf16 = jnp.bfloat16


def encode(yh, x, z, core):
    return (((yh % N_YH) * N_X + x % N_X) * N_Z + z % N_Z) * N_CORE + core % N_CORE


def torus_pairs(yh=0, x=0, z=0, core=0):
    pairs = []
    for j in range(N_DP):
        own = (j // (N_CORE * N_Z * N_X), j // (N_CORE * N_Z) % N_X, j // N_CORE % N_Z, j % N_CORE)
        pairs.append((j, encode(own[0] + yh, own[1] + x, own[2] + z, own[3] + core)))
    return pairs


def torus_send(array, **shift):
    return lax.ppermute(array, "dp", torus_pairs(**shift))


def ring_send(array, by, only=None):
    pairs = [(j, (j + by) % N_DP) for j in range(N_DP) if only is None or j % N_CORE == only]
    return lax.ppermute(array, "dp", pairs)


def tensor_swap(array):
    return lax.ppermute(array, "tensor", [(0, 1), (1, 0)])


def unit_rows(raw_rows):
    widened = raw_rows.astype(f32)
    lengths = jnp.sqrt(jnp.sum(widened * widened, axis=-1, keepdims=True) + epsilon)
    return (widened / lengths, lengths)


def project_back(unit_part, lengths, direction):
    radial = jnp.sum(unit_part * direction, axis=-1, keepdims=True)
    return (direction - unit_part * radial) / lengths


def gelu_slope(hidden_in):
    square = hidden_in * hidden_in
    tangent = jnp.tanh(hidden_in * (gelu_root + gelu_root * gelu_cubic * square))
    inner_slope = hidden_in * (0.5 * gelu_root + 1.5 * gelu_root * gelu_cubic * square)
    return 0.5 + 0.5 * tangent + (1.0 - tangent * tangent) * inner_slope


def dot_nt(a, b):
    return lax.dot_general(a, b, (((1,), (1,)), ((), ())), preferred_element_type=f32)


def dot_tn(a, b):
    return lax.dot_general(a, b, (((0,), (0,)), ((), ())), preferred_element_type=f32)


def key_rows(raw):
    return unit_rows(raw)[0].astype(bf16)


def text_key_kernel(half, place_ref, raw_ref, half_ref):
    begin = pl.multiple_of(place_ref[1] * half, half)
    half_ref[...] = key_rows(raw_ref[pl.ds(begin, half), :])


def text_half_key(place, text_raw, half):
    return pl.pallas_call(
        functools.partial(text_key_kernel, half),
        in_specs=[pl.BlockSpec(memory_space=pltpu.SMEM), pl.BlockSpec(memory_space=pltpu.VMEM)],
        out_specs=pl.BlockSpec(memory_space=pltpu.VMEM),
        out_shape=jax.ShapeDtypeStruct((half, text_raw.shape[1]), bf16),
    )(place, text_raw)


def pair_kernel(place_ref, scalar_ref, value_ref, window_value_ref, valid_ref, own_ref, other_ref, *refs):
    window_refs = refs[:-8]
    own_part, other_part, zero_ref, text_own, text_sibling, text_far, key_ref, window_key = refs[-8:]
    half = own_ref.shape[0]
    key_ref[:half, :] = key_rows(own_ref[...])
    key_ref[half:, :] = key_rows(other_ref[...])
    begin = 0
    for ref in window_refs:
        window_key[begin : begin + ref.shape[0], :] = ref[...]
        begin += ref.shape[0]
    logits = scalar_ref[0] * dot_nt(key_ref[...], window_key[...]) + scalar_ref[1]
    target = (value_ref[...] == window_value_ref[...]).astype(f32)
    weight = jnp.where(valid_ref[...] > 0, jax.nn.sigmoid(logits) - target, 0.0).astype(bf16)
    part = jnp.dot(weight, window_key[...], preferred_element_type=f32)
    own_part[...] = part[:half]
    other_part[...] = part[half:].astype(bf16)
    text_part = dot_tn(weight, key_ref[...])
    count = text_own.shape[0]
    text_own[...] = text_part[:count]
    text_sibling[...] = text_part[count : 2 * count].astype(bf16)
    text_far[...] = text_part[2 * count :].astype(bf16)
    zero_ref[...] = jnp.where(place_ref[1] == 0, part[:1], part[half : half + 1])


def pair_products(place, scalars, value, window_value, valid, own, other, window):
    width = own.shape[1]
    rows = value.shape[0]
    depth = window_value.shape[0]
    smem = pl.BlockSpec(memory_space=pltpu.SMEM)
    vmem = pl.BlockSpec(memory_space=pltpu.VMEM)
    return pl.pallas_call(
        pair_kernel,
        in_specs=[smem, smem] + [vmem] * (5 + len(window)),
        out_specs=[vmem] * 6,
        out_shape=[
            jax.ShapeDtypeStruct((rows // 2, width), f32),
            jax.ShapeDtypeStruct((rows // 2, width), bf16),
            jax.ShapeDtypeStruct((1, width), f32),
            jax.ShapeDtypeStruct((2 * rows, width), f32),
            jax.ShapeDtypeStruct((2 * rows, width), bf16),
            jax.ShapeDtypeStruct((depth - 4 * rows, width), bf16),
        ],
        scratch_shapes=[pltpu.VMEM((rows, width), bf16), pltpu.VMEM((depth, width), bf16)],
        compiler_params=pltpu.CompilerParams(vmem_limit_bytes=16 * 2**20),
        cost_estimate=LIGHT,
    )(
        place,
        scalars,
        value[:, None],
        window_value[None, :],
        valid.astype(jnp.int32)[None, :],
        own,
        other,
        *window,
    )


def pooled_kernel(place_ref, scalar_ref, own_ref, other_ref, mine_ref, theirs_ref, pooled_ref):
    raw = jnp.where(place_ref[1] == 0, own_ref[:1, :].astype(f32), other_ref[:1, :].astype(f32))
    unit, length = unit_rows(raw)
    direction = scalar_ref[0] * (mine_ref[...] + theirs_ref[...])
    pooled_ref[...] = project_back(unit, length, direction).astype(bf16)


def pooled_row(place, scalars, own, other, mine, theirs):
    smem = pl.BlockSpec(memory_space=pltpu.SMEM)
    vmem = pl.BlockSpec(memory_space=pltpu.VMEM)
    return pl.pallas_call(
        pooled_kernel,
        in_specs=[smem, smem] + [vmem] * 4,
        out_specs=vmem,
        out_shape=jax.ShapeDtypeStruct(mine.shape, bf16),
    )(place, scalars, own, other, mine, theirs)


def transpose_kernel(patches, normed_ref, out_ref):
    block = normed_ref[...]
    kept = lax.broadcasted_iota(jnp.int32, block.shape, 0) < patches
    out_ref[...] = jnp.where(kept, block, jnp.zeros_like(block)).T


def transposed(normed, rows):
    patches, width = normed.shape
    step = 3 * LANES
    return pl.pallas_call(
        functools.partial(transpose_kernel, patches),
        grid=(width // step,),
        in_specs=[pl.BlockSpec((rows, step), lambda i: (0, i))],
        out_specs=pl.BlockSpec((step, rows), lambda i: (i, 0)),
        out_shape=jax.ShapeDtypeStruct((width, rows), bf16),
        compiler_params=pltpu.CompilerParams(vmem_limit_bytes=8 * 2**20),
        cost_estimate=LIGHT,
    )(normed)


def copy_all(pairs, sems, first):
    copies = [pltpu.make_async_copy(src, dst, sems.at[first + i]) for i, (src, dst) in enumerate(pairs)]
    for copy in copies:
        copy.start()
    return copies


def base_kernel(place_ref, share_ref, weight_tail, hidden_tail, cotangent_hbm, weight_hbm, hidden_hbm, *refs):
    base_hbm, slope_hbm, cotangent, weight, hidden, base, slope, sems = refs
    patches, columns = base.shape
    start = columns - LANES
    step = start // 2
    begin = place_ref[0] * start
    halves = [pl.ds(pl.multiple_of(begin + i * step, step), step) for i in range(2)]
    wheres = [pl.ds(i * step, step) for i in range(2)]
    loads = copy_all(
        [
            (hidden_hbm.at[:, halves[0]], hidden.at[:, wheres[0]]),
            (cotangent_hbm, cotangent),
            (weight_hbm.at[halves[0], :], weight.at[wheres[0], :]),
            (hidden_hbm.at[:, halves[1]], hidden.at[:, wheres[1]]),
            (weight_hbm.at[halves[1], :], weight.at[wheres[1], :]),
        ],
        sems,
        0,
    )
    share = share_ref[...].T[:patches, :1]

    def block(weight_rows, hidden_block, where, ready):
        kept = gelu_slope(hidden_block.astype(f32))
        slope[:, where] = (share * kept).astype(bf16)
        for copy in ready:
            copy.wait()
        base[:, where] = (dot_nt(cotangent[...], weight_rows[...]) * kept).astype(bf16)

    def store(where, first):
        return copy_all(
            [(base.at[:, where], base_hbm.at[:, where]), (slope.at[:, where], slope_hbm.at[:, where])], sems, first
        )

    loads[0].wait()
    block(weight.at[wheres[0], :], hidden[:, wheres[0]], wheres[0], loads[1:3])
    stores = store(wheres[0], 5)
    loads[3].wait()
    block(weight.at[wheres[1], :], hidden[:, wheres[1]], wheres[1], loads[4:])
    stores += store(wheres[1], 7)
    where = pl.ds(start, LANES)
    block(weight_tail, hidden_tail[...], where, [])
    stores += store(where, 9)
    for copy in stores:
        copy.wait()


def hidden_base(place, columns, cotangent, share, weight, hidden):
    patches, width = cotangent.shape
    start = columns - LANES
    tiles = start // LANES
    hbm = pl.BlockSpec(memory_space=pl.ANY)
    out = jax.ShapeDtypeStruct((patches, columns), bf16)
    return pl.pallas_call(
        base_kernel,
        grid_spec=pltpu.PrefetchScalarGridSpec(
            num_scalar_prefetch=1,
            grid=(1,),
            in_specs=[
                pl.BlockSpec(share.shape, lambda i, place: (0, 0)),
                pl.BlockSpec((LANES, width), lambda i, place: (tiles * (1 + place[0]), 0)),
                pl.BlockSpec((patches, LANES), lambda i, place: (0, tiles * (1 + place[0]))),
                hbm,
                hbm,
                hbm,
            ],
            out_specs=[hbm, hbm],
            scratch_shapes=[
                pltpu.VMEM((patches, width), bf16),
                pltpu.VMEM((start, width), bf16),
                pltpu.VMEM((patches, start), bf16),
                pltpu.VMEM((patches, columns), bf16),
                pltpu.VMEM((patches, columns), bf16),
                pltpu.SemaphoreType.DMA((11,)),
            ],
        ),
        out_shape=[out, out],
        compiler_params=pltpu.CompilerParams(vmem_limit_bytes=60 * 2**20),
        cost_estimate=LIGHT,
    )(place, share, weight, hidden, cotangent, weight, hidden)


def block_rows(targets_ref, height, dy, dx):
    return pl.ds(pl.multiple_of(targets_ref[dy * N_X + dx] * height, 16), height)


def terms_kernel(
    place_ref,
    targets_ref,
    pooled0_ref,
    pooled1_ref,
    weight_tail,
    normed0_hbm,
    normed1_hbm,
    base0_hbm,
    base1_hbm,
    slope0_hbm,
    slope1_hbm,
    weight_hbm,
    a_keep,
    a_sent1,
    a_sent2,
    a_sent3,
    c_keep,
    c_sent,
    weight,
    normed,
    base,
    slope,
    sum_a,
    sum_c,
    stage_a,
    stage_c,
    sems,
):
    _, patches, columns = base.shape
    width = weight.shape[1]
    start = columns - LANES
    split = a_keep.shape[2]
    height = a_keep.shape[1]
    begin = pl.multiple_of(place_ref[0] * start, start)
    part_a, part_c = pl.ds(0, split), pl.ds(split, columns - split)
    images = ((slope0_hbm, base0_hbm, normed0_hbm), (slope1_hbm, base1_hbm, normed1_hbm))
    pairs = [(weight_hbm.at[pl.ds(begin, start), :], weight)]
    for i, (slope_hbm, base_hbm, normed_hbm) in enumerate(images):
        pairs += [
            (slope_hbm.at[:, part_c], slope.at[i, :, part_c]),
            (base_hbm.at[:, part_c], base.at[i, :, part_c]),
            (normed_hbm, normed.at[i]),
        ]
    for i, (slope_hbm, base_hbm, normed_hbm) in enumerate(images):
        pairs += [
            (slope_hbm.at[:, part_a], slope.at[i, :, part_a]),
            (base_hbm.at[:, part_a], base.at[i, :, part_a]),
        ]
    loads = copy_all(pairs, sems, 0)
    pooled = jnp.concatenate(
        [jnp.broadcast_to(ref[...].astype(f32), (8, width)) for ref in (pooled0_ref, pooled1_ref)], axis=0
    ).astype(bf16)
    loads[0].wait()
    lift = jnp.concatenate([dot_nt(pooled, weight[...]), dot_nt(pooled, weight_tail[...])], axis=1)

    def product(image, first, last):
        lifted = lift[8 * image : 8 * image + 1, first:last] * slope[image, :, first:last].astype(f32)
        grad = (base[image, :, first:last].astype(f32) + lifted).astype(bf16)
        return jnp.dot(normed[image, :, :patches], grad, preferred_element_type=f32)

    for copy in loads[1:4]:
        copy.wait()
    sum_c[...] = product(0, split, columns)
    for copy in loads[4:7]:
        copy.wait()
    sum_c[...] += product(1, split, columns)
    stores = copy_all(
        [(sum_c.at[block_rows(targets_ref, height, 0, dx), :], c_keep.at[dx]) for dx in range(N_X)], sems, 11
    )
    for dx in range(N_X):
        stage_c[dx] = sum_c[block_rows(targets_ref, height, 1, dx), :].astype(bf16)
    stores += copy_all([(stage_c, c_sent)], sems, 15)
    for copy in loads[7:]:
        copy.wait()
    sum_a[...] = product(0, 0, split) + product(1, 0, split)
    stores += copy_all(
        [(sum_a.at[block_rows(targets_ref, height, dy, 0), :], a_keep.at[dy]) for dy in range(N_YH)], sems, 16
    )
    for dx, out in ((1, a_sent1), (2, a_sent2), (3, a_sent3)):
        for dy in range(N_YH):
            stage_a[dx - 1, dy] = sum_a[block_rows(targets_ref, height, dy, dx), :].astype(bf16)
        stores += copy_all([(stage_a.at[dx - 1], out)], sems, 17 + dx)
    for copy in stores:
        copy.wait()


def up_terms(place, targets, split, normed_t, base, slope, weight, pooled):
    width, depth = normed_t[0].shape
    patches, columns = base[0].shape
    height = width // (N_YH * N_X)
    hbm = pl.BlockSpec(memory_space=pl.ANY)
    tiles = columns // LANES - 1
    row = pl.BlockSpec((1, width), lambda i, place, targets: (0, 0))
    part_a, part_c = (N_YH, height, split), (N_X, height, columns - split)
    return pl.pallas_call(
        terms_kernel,
        grid_spec=pltpu.PrefetchScalarGridSpec(
            num_scalar_prefetch=2,
            grid=(1,),
            in_specs=[
                row,
                row,
                pl.BlockSpec((LANES, width), lambda i, place, targets: (tiles * (1 + place[0]), 0)),
            ]
            + [hbm] * 7,
            out_specs=[hbm] * 6,
            scratch_shapes=[
                pltpu.VMEM((columns - LANES, width), bf16),
                pltpu.VMEM((2, width, depth), bf16),
                pltpu.VMEM((2, patches, columns), bf16),
                pltpu.VMEM((2, patches, columns), bf16),
                pltpu.VMEM((width, split), f32),
                pltpu.VMEM((width, columns - split), f32),
                pltpu.VMEM((N_X - 1,) + part_a, bf16),
                pltpu.VMEM(part_c, bf16),
                pltpu.SemaphoreType.DMA((21,)),
            ],
        ),
        out_shape=[
            jax.ShapeDtypeStruct(part_a, f32),
            jax.ShapeDtypeStruct(part_a, bf16),
            jax.ShapeDtypeStruct(part_a, bf16),
            jax.ShapeDtypeStruct(part_a, bf16),
            jax.ShapeDtypeStruct(part_c, f32),
            jax.ShapeDtypeStruct(part_c, bf16),
        ],
        compiler_params=pltpu.CompilerParams(vmem_limit_bytes=60 * 2**20),
        cost_estimate=LIGHT,
    )(place, targets, *pooled, weight, *normed_t, *base, *slope, weight)


def per_device(
    image_raw,
    text_raw,
    logit_scale,
    logit_bias,
    pair_offset,
    normed_patches,
    head_cotangent,
    hidden_pre,
    pool_share,
    down_weight,
):
    place = lax.axis_index("dp")
    tensor_index = lax.axis_index("tensor")
    yh = place // (N_CORE * N_Z * N_X)
    x = place // (N_CORE * N_Z) % N_X
    z = place // N_CORE % N_Z
    core = place % N_CORE
    image_rows, width = image_raw.shape
    text_rows = text_raw.shape[0]
    half = text_rows // N_TENSOR
    hidden_here = hidden_pre.shape[1]
    spot = jnp.stack([core, tensor_index]).astype(jnp.int32)
    scalars = jnp.stack([logit_scale, logit_bias])

    text_half = text_half_key(spot, text_raw, half)
    text_half, image_raw, pair_offset, normed_patches, head_cotangent, hidden_pre, pool_share = lax.optimization_barrier(
        (text_half, image_raw, pair_offset, normed_patches, head_cotangent, hidden_pre, pool_share)
    )
    text_far = ring_send(text_half, 7, only=1)
    text_near = jnp.concatenate([text_half, ring_send(text_half, 2)], axis=0)
    image_other = tensor_swap(image_raw)
    text_near, image_other, cotangent_own = lax.optimization_barrier((text_near, image_other, head_cotangent))
    text_next = ring_send(text_near, 4)
    rels = jnp.concatenate(
        [
            jnp.array([0, 2, 4, 6], jnp.int32),
            jnp.array([-1, 1, 3, 5], jnp.int32) + 2 * core,
            jnp.array([7], jnp.int32) + 2 * core,
        ]
    )
    text_row = jnp.arange(half, dtype=jnp.int32) + tensor_index * half
    text_value = (text_row[None, :] - text_rows * rels[:, None]).reshape(-1)
    text_valid = jnp.repeat((rels >= 0) & (rels < WINDOW), half)

    offset_other = tensor_swap(pair_offset)
    row = jnp.arange(image_rows, dtype=jnp.int32)
    own_row = row + tensor_index * image_rows
    other_row = row + (1 - tensor_index) * image_rows
    image_value = jnp.concatenate([own_row - pair_offset, other_row - offset_other])

    columns = 9 * LANES
    start = 8 * LANES
    cotangent_other = torus_send(head_cotangent, core=1)
    hidden_other = torus_send(hidden_pre, core=1)
    share_other = torus_send(pool_share, core=1)
    share_own, share_other = [
        jnp.broadcast_to(jnp.pad(part, (0, 6 * LANES - part.shape[0]))[None, :], (8, 6 * LANES))
        for part in (pool_share, share_other)
    ]
    base_own, slope_own = hidden_base(
        spot, columns, cotangent_own, share_own, down_weight, hidden_pre
    )
    text_next, text_far, base_own, slope_own = lax.optimization_barrier((text_next, text_far, base_own, slope_own))
    text_window = [text_near, text_next, torus_send(text_near, core=1), torus_send(text_next, core=1), text_far]
    normed_own = transposed(normed_patches, 6 * LANES)
    normed_other = torus_send(normed_own, core=1)

    text_last = text_window[3]
    text_last, share_other = lax.optimization_barrier((text_last, share_other))
    text_window[3] = text_last
    image_part, image_swapped, zero_row, text_own, text_sibling, far = pair_products(
        spot, scalars, image_value, text_value, text_valid, image_raw, image_other, text_window
    )
    zero_theirs = tensor_swap(zero_row)

    near = 2 * half
    returned = torus_send(text_sibling, core=1)
    far = ring_send(far, -7, only=0)
    image_swapped = tensor_swap(image_swapped)
    zero_row, returned, cotangent_other = lax.optimization_barrier((zero_row, returned, cotangent_other))
    text_next = ring_send((text_own[near:] + returned[near:].astype(f32)).astype(bf16), -4)

    base_other, slope_other = hidden_base(
        spot, columns, cotangent_other, share_other, down_weight, hidden_other
    )
    zero_theirs, base_other, slope_other = lax.optimization_barrier((zero_theirs, base_other, slope_other))
    pooled = pooled_row(spot, scalars, image_raw, image_other, zero_row, zero_theirs)
    pooled_other = torus_send(pooled, core=1)
    pooled_other, text_next, far, image_swapped = lax.optimization_barrier(
        (pooled_other, text_next, far, image_swapped)
    )

    split = 5 * LANES
    targets = jnp.stack(
        [(yh + dy) % N_YH * N_X + (x + dx) % N_X for dy in range(N_YH) for dx in range(N_X)]
    ).astype(jnp.int32)
    a_keep, a_sent1, a_sent2, a_sent3, c_keep, c_sent = up_terms(
        spot,
        targets,
        split,
        [normed_own, normed_other],
        [base_own, base_other],
        [slope_own, slope_other],
        down_weight,
        [pooled, pooled_other],
    )
    a_keep, image_part, late_text, late_image = lax.optimization_barrier((a_keep, image_part, text_raw, image_raw))
    c_come = torus_send(c_sent, yh=1)
    a_come = [torus_send(part, x=dx) for dx, part in ((2, a_sent2), (1, a_sent1), (3, a_sent3))]
    c_keep = c_keep + c_come.astype(f32)
    c_keep, a_keep, text_own, returned, text_next = lax.optimization_barrier(
        (c_keep, a_keep, text_own, returned, text_next)
    )
    a_keep = a_keep + (a_come[0].astype(f32) + a_come[1].astype(f32) + a_come[2].astype(f32))
    c_come = [torus_send(c_keep[dx].astype(bf16), x=dx) for dx in (2, 1, 3)]
    a_come = torus_send(a_keep[1].astype(bf16), yh=1)
    total = jnp.concatenate(
        [
            a_keep[0] + a_come.astype(f32),
            c_keep[0] + (c_come[0].astype(f32) + c_come[1].astype(f32) + c_come[2].astype(f32)),
        ],
        axis=1,
    )

    text_near = text_own[:near] + returned[:near].astype(f32) + text_next.astype(f32)
    text_back = ring_send(text_near[half:].astype(bf16), -2)
    total, text_back = lax.optimization_barrier((total, text_back))
    text_dir = logit_scale * (text_near[:half] + text_back.astype(f32) + far.astype(f32))
    text_unit, text_length = unit_rows(lax.dynamic_slice_in_dim(late_text, tensor_index * half, half, 0))
    text_mine = project_back(text_unit, text_length, text_dir).astype(bf16)

    image_unit, image_length = unit_rows(late_image)
    image_dir = logit_scale * (image_part + image_swapped.astype(f32))
    image_grad = project_back(image_unit, image_length, image_dir).astype(bf16)

    rows_chip = total.shape[0] // N_Z
    chunks = total.reshape(N_Z // 2, 2, rows_chip, columns)
    swap_pairs = [(j, j ^ N_CORE) for j in range(N_DP)]
    chunk = lax.dynamic_index_in_dim(chunks, 1 - z % 2, 1, keepdims=False).astype(bf16)
    chunks = lax.dynamic_index_in_dim(chunks, z % 2, 1, keepdims=False)
    chunks = chunks + lax.ppermute(chunk, "dp", swap_pairs).astype(f32)
    total = lax.dynamic_index_in_dim(chunks, z // 2, 0, keepdims=False)
    for hop in (2, 1, 3):
        chunk = lax.dynamic_index_in_dim(chunks, (z // 2 + hop) % (N_Z // 2), 0, keepdims=False).astype(bf16)
        total = total + torus_send(chunk, z=2 * hop).astype(f32)
    text_theirs = tensor_swap(text_mine)
    total, text_theirs, image_grad = lax.optimization_barrier((total, text_theirs, image_grad))
    rows_here = rows_chip // N_CORE
    mine = jnp.where(core == 0, total[:rows_here], total[rows_here:])
    theirs = torus_send(jnp.where(core == 0, total[rows_here:], total[:rows_here]), core=1)
    left = jnp.where(core == 0, mine, theirs)
    right = jnp.where(core == 0, theirs, mine)
    up_grad = jnp.concatenate([left, right[:, columns - start : hidden_here - start]], axis=1)

    text_grad = jnp.where(
        tensor_index == 0,
        jnp.concatenate([text_mine, text_theirs], axis=0),
        jnp.concatenate([text_theirs, text_mine], axis=0),
    )
    return (image_grad, text_grad, up_grad)


def solution(mesh):
    return jax.shard_map(
        per_device,
        mesh=mesh,
        in_specs=(
            P(("dp", "tensor"), None),
            P("dp", None),
            P(),
            P(),
            P(("dp", "tensor")),
            P("dp", None),
            P("dp", None),
            P("dp", "tensor"),
            P("dp"),
            P("tensor", None),
        ),
        out_specs=(P(("dp", "tensor"), None), P("dp", None), P("dp", "tensor")),
        check_vma=False,
    )
```

```python
import functools

import jax
import jax.numpy as jnp
from jax import lax
from jax.experimental import pallas as pl
from jax.experimental.pallas import tpu as pltpu
from jax.sharding import PartitionSpec as P

WINDOW = 8
N_YH, N_X, N_Z, N_CORE = 2, 4, 8, 2
N_DP = N_YH * N_X * N_Z * N_CORE
N_TENSOR = 2
LANES = 128
LIGHT = pl.CostEstimate(flops=1, bytes_accessed=1, transcendentals=0)
HEAVY = pl.CostEstimate(flops=10**10, bytes_accessed=1, transcendentals=0)

epsilon = 1e-06
gelu_root = 0.7978845608028654
gelu_cubic = 0.044715

f32 = jnp.float32
bf16 = jnp.bfloat16


def encode(yh, x, z, core):
    return (((yh % N_YH) * N_X + x % N_X) * N_Z + z % N_Z) * N_CORE + core % N_CORE


def torus_pairs(yh=0, x=0, z=0, core=0):
    pairs = []
    for j in range(N_DP):
        own = (j // (N_CORE * N_Z * N_X), j // (N_CORE * N_Z) % N_X, j // N_CORE % N_Z, j % N_CORE)
        pairs.append((j, encode(own[0] + yh, own[1] + x, own[2] + z, own[3] + core)))
    return pairs


def torus_send(array, **shift):
    return lax.ppermute(array, "dp", torus_pairs(**shift))


def ring_send(array, by, only=None):
    pairs = [(j, (j + by) % N_DP) for j in range(N_DP) if only is None or j % N_CORE == only]
    return lax.ppermute(array, "dp", pairs)


def tensor_swap(array):
    return lax.ppermute(array, "tensor", [(0, 1), (1, 0)])


def unit_rows(raw_rows):
    widened = raw_rows.astype(f32)
    lengths = jnp.sqrt(jnp.sum(widened * widened, axis=-1, keepdims=True) + epsilon)
    return (widened / lengths, lengths)


def project_back(unit_part, lengths, direction):
    radial = jnp.sum(unit_part * direction, axis=-1, keepdims=True)
    return (direction - unit_part * radial) / lengths


def gelu_slope(hidden_in):
    square = hidden_in * hidden_in
    tangent = jnp.tanh(hidden_in * (gelu_root + gelu_root * gelu_cubic * square))
    inner_slope = hidden_in * (0.5 * gelu_root + 1.5 * gelu_root * gelu_cubic * square)
    return 0.5 + 0.5 * tangent + (1.0 - tangent * tangent) * inner_slope


def dot_nt(a, b):
    return lax.dot_general(a, b, (((1,), (1,)), ((), ())), preferred_element_type=f32)


def dot_tn(a, b):
    return lax.dot_general(a, b, (((0,), (0,)), ((), ())), preferred_element_type=f32)


def key_rows(raw):
    return unit_rows(raw)[0].astype(bf16)


def text_key_kernel(half, place_ref, raw_ref, half_ref):
    begin = pl.multiple_of(place_ref[1] * half, half)
    half_ref[...] = key_rows(raw_ref[pl.ds(begin, half), :])


def text_half_key(place, text_raw, half):
    return pl.pallas_call(
        functools.partial(text_key_kernel, half),
        in_specs=[pl.BlockSpec(memory_space=pltpu.SMEM), pl.BlockSpec(memory_space=pltpu.VMEM)],
        out_specs=pl.BlockSpec(memory_space=pltpu.VMEM),
        out_shape=jax.ShapeDtypeStruct((half, text_raw.shape[1]), bf16),
    )(place, text_raw)


def pair_kernel(place_ref, scalar_ref, value_ref, window_value_ref, valid_ref, own_ref, other_ref, *refs):
    window_refs = refs[:-8]
    own_part, other_part, zero_ref, text_own, text_sibling, text_far, key_ref, window_key = refs[-8:]
    half = own_ref.shape[0]
    key_ref[:half, :] = key_rows(own_ref[...])
    key_ref[half:, :] = key_rows(other_ref[...])
    begin = 0
    for ref in window_refs:
        window_key[begin : begin + ref.shape[0], :] = ref[...]
        begin += ref.shape[0]
    logits = scalar_ref[0] * dot_nt(key_ref[...], window_key[...]) + scalar_ref[1]
    target = (value_ref[...] == window_value_ref[...]).astype(f32)
    weight = jnp.where(valid_ref[...] > 0, jax.nn.sigmoid(logits) - target, 0.0).astype(bf16)
    part = jnp.dot(weight, window_key[...], preferred_element_type=f32)
    own_part[...] = part[:half]
    other_part[...] = part[half:].astype(bf16)
    text_part = dot_tn(weight, key_ref[...])
    count = text_own.shape[0]
    text_own[...] = text_part[:count]
    text_sibling[...] = text_part[count : 2 * count].astype(bf16)
    text_far[...] = text_part[2 * count :].astype(bf16)
    zero_ref[...] = jnp.where(place_ref[1] == 0, part[:1], part[half : half + 1])


def pair_products(place, scalars, value, window_value, valid, own, other, window):
    width = own.shape[1]
    rows = value.shape[0]
    depth = window_value.shape[0]
    smem = pl.BlockSpec(memory_space=pltpu.SMEM)
    vmem = pl.BlockSpec(memory_space=pltpu.VMEM)
    return pl.pallas_call(
        pair_kernel,
        in_specs=[smem, smem] + [vmem] * (5 + len(window)),
        out_specs=[vmem] * 6,
        out_shape=[
            jax.ShapeDtypeStruct((rows // 2, width), f32),
            jax.ShapeDtypeStruct((rows // 2, width), bf16),
            jax.ShapeDtypeStruct((1, width), f32),
            jax.ShapeDtypeStruct((2 * rows, width), f32),
            jax.ShapeDtypeStruct((2 * rows, width), bf16),
            jax.ShapeDtypeStruct((depth - 4 * rows, width), bf16),
        ],
        scratch_shapes=[pltpu.VMEM((rows, width), bf16), pltpu.VMEM((depth, width), bf16)],
        compiler_params=pltpu.CompilerParams(vmem_limit_bytes=16 * 2**20),
        cost_estimate=LIGHT,
    )(
        place,
        scalars,
        value[:, None],
        window_value[None, :],
        valid.astype(jnp.int32)[None, :],
        own,
        other,
        *window,
    )


def pooled_kernel(place_ref, scalar_ref, own_ref, other_ref, mine_ref, theirs_ref, pooled_ref):
    raw = jnp.where(place_ref[1] == 0, own_ref[:1, :].astype(f32), other_ref[:1, :].astype(f32))
    unit, length = unit_rows(raw)
    direction = scalar_ref[0] * (mine_ref[...] + theirs_ref[...])
    pooled_ref[...] = project_back(unit, length, direction).astype(bf16)


def pooled_row(place, scalars, own, other, mine, theirs):
    smem = pl.BlockSpec(memory_space=pltpu.SMEM)
    vmem = pl.BlockSpec(memory_space=pltpu.VMEM)
    return pl.pallas_call(
        pooled_kernel,
        in_specs=[smem, smem] + [vmem] * 4,
        out_specs=vmem,
        out_shape=jax.ShapeDtypeStruct(mine.shape, bf16),
    )(place, scalars, own, other, mine, theirs)


def transpose_kernel(patches, normed_ref, out_ref):
    block = normed_ref[...]
    kept = lax.broadcasted_iota(jnp.int32, block.shape, 0) < patches
    out_ref[...] = jnp.where(kept, block, jnp.zeros_like(block)).T


def transposed(normed, rows):
    patches, width = normed.shape
    step = 3 * LANES
    return pl.pallas_call(
        functools.partial(transpose_kernel, patches),
        grid=(width // step,),
        in_specs=[pl.BlockSpec((rows, step), lambda i: (0, i))],
        out_specs=pl.BlockSpec((step, rows), lambda i: (i, 0)),
        out_shape=jax.ShapeDtypeStruct((width, rows), bf16),
        compiler_params=pltpu.CompilerParams(vmem_limit_bytes=8 * 2**20),
        cost_estimate=LIGHT,
    )(normed)


def copy_all(pairs, sems, first):
    copies = [pltpu.make_async_copy(src, dst, sems.at[first + i]) for i, (src, dst) in enumerate(pairs)]
    for copy in copies:
        copy.start()
    return copies


def base_kernel(place_ref, share_ref, weight_tail, hidden_tail, cotangent_hbm, weight_hbm, hidden_hbm, *refs):
    base_hbm, slope_hbm, cotangent, weight, hidden, base, slope, sems = refs
    patches, columns = base.shape
    start = columns - LANES
    step = start // 2
    begin = place_ref[0] * start
    halves = [pl.ds(pl.multiple_of(begin + i * step, step), step) for i in range(2)]
    wheres = [pl.ds(i * step, step) for i in range(2)]
    loads = copy_all(
        [
            (hidden_hbm.at[:, halves[0]], hidden.at[:, wheres[0]]),
            (cotangent_hbm, cotangent),
            (weight_hbm.at[halves[0], :], weight.at[wheres[0], :]),
            (hidden_hbm.at[:, halves[1]], hidden.at[:, wheres[1]]),
            (weight_hbm.at[halves[1], :], weight.at[wheres[1], :]),
        ],
        sems,
        0,
    )
    share = share_ref[...].T[:patches, :1]

    def block(weight_rows, hidden_block, where, ready):
        kept = gelu_slope(hidden_block.astype(f32))
        slope[:, where] = (share * kept).astype(bf16)
        for copy in ready:
            copy.wait()
        base[:, where] = (dot_nt(cotangent[...], weight_rows[...]) * kept).astype(bf16)

    def store(where, first):
        return copy_all(
            [(base.at[:, where], base_hbm.at[:, where]), (slope.at[:, where], slope_hbm.at[:, where])], sems, first
        )

    loads[0].wait()
    block(weight.at[wheres[0], :], hidden[:, wheres[0]], wheres[0], loads[1:3])
    stores = store(wheres[0], 5)
    loads[3].wait()
    block(weight.at[wheres[1], :], hidden[:, wheres[1]], wheres[1], loads[4:])
    stores += store(wheres[1], 7)
    where = pl.ds(start, LANES)
    block(weight_tail, hidden_tail[...], where, [])
    stores += store(where, 9)
    for copy in stores:
        copy.wait()


def hidden_base(place, columns, cotangent, share, weight, hidden, cost):
    patches, width = cotangent.shape
    start = columns - LANES
    tiles = start // LANES
    hbm = pl.BlockSpec(memory_space=pl.ANY)
    out = jax.ShapeDtypeStruct((patches, columns), bf16)
    return pl.pallas_call(
        base_kernel,
        grid_spec=pltpu.PrefetchScalarGridSpec(
            num_scalar_prefetch=1,
            grid=(1,),
            in_specs=[
                pl.BlockSpec(share.shape, lambda i, place: (0, 0)),
                pl.BlockSpec((LANES, width), lambda i, place: (tiles * (1 + place[0]), 0)),
                pl.BlockSpec((patches, LANES), lambda i, place: (0, tiles * (1 + place[0]))),
                hbm,
                hbm,
                hbm,
            ],
            out_specs=[hbm, hbm],
            scratch_shapes=[
                pltpu.VMEM((patches, width), bf16),
                pltpu.VMEM((start, width), bf16),
                pltpu.VMEM((patches, start), bf16),
                pltpu.VMEM((patches, columns), bf16),
                pltpu.VMEM((patches, columns), bf16),
                pltpu.SemaphoreType.DMA((11,)),
            ],
        ),
        out_shape=[out, out],
        compiler_params=pltpu.CompilerParams(vmem_limit_bytes=60 * 2**20),
        cost_estimate=cost,
    )(place, share, weight, hidden, cotangent, weight, hidden)


def block_rows(targets_ref, height, dy, dx):
    return pl.ds(pl.multiple_of(targets_ref[dy * N_X + dx] * height, 16), height)


def terms_kernel(
    place_ref,
    targets_ref,
    pooled0_ref,
    pooled1_ref,
    weight_tail,
    normed0_hbm,
    normed1_hbm,
    base0_hbm,
    base1_hbm,
    slope0_hbm,
    slope1_hbm,
    weight_hbm,
    a_keep,
    a_sent1,
    a_sent2,
    a_sent3,
    c_keep,
    c_sent,
    weight,
    normed,
    base,
    slope,
    sum_a,
    sum_c,
    stage_a,
    stage_c,
    sems,
):
    _, patches, columns = base.shape
    width = weight.shape[1]
    start = columns - LANES
    split = a_keep.shape[2]
    height = a_keep.shape[1]
    begin = pl.multiple_of(place_ref[0] * start, start)
    part_a, part_c = pl.ds(0, split), pl.ds(split, columns - split)
    images = ((slope0_hbm, base0_hbm, normed0_hbm), (slope1_hbm, base1_hbm, normed1_hbm))
    pairs = [(weight_hbm.at[pl.ds(begin, start), :], weight)]
    for i, (slope_hbm, base_hbm, normed_hbm) in enumerate(images):
        pairs += [
            (slope_hbm.at[:, part_c], slope.at[i, :, part_c]),
            (base_hbm.at[:, part_c], base.at[i, :, part_c]),
            (normed_hbm, normed.at[i]),
        ]
    for i, (slope_hbm, base_hbm, normed_hbm) in enumerate(images):
        pairs += [
            (slope_hbm.at[:, part_a], slope.at[i, :, part_a]),
            (base_hbm.at[:, part_a], base.at[i, :, part_a]),
        ]
    loads = copy_all(pairs, sems, 0)
    pooled = jnp.concatenate(
        [jnp.broadcast_to(ref[...].astype(f32), (8, width)) for ref in (pooled0_ref, pooled1_ref)], axis=0
    ).astype(bf16)
    loads[0].wait()
    lift = jnp.concatenate([dot_nt(pooled, weight[...]), dot_nt(pooled, weight_tail[...])], axis=1)

    def product(image, first, last):
        lifted = lift[8 * image : 8 * image + 1, first:last] * slope[image, :, first:last].astype(f32)
        grad = (base[image, :, first:last].astype(f32) + lifted).astype(bf16)
        return jnp.dot(normed[image, :, :patches], grad, preferred_element_type=f32)

    for copy in loads[1:4]:
        copy.wait()
    sum_c[...] = product(0, split, columns)
    for copy in loads[4:7]:
        copy.wait()
    sum_c[...] += product(1, split, columns)
    stores = copy_all(
        [(sum_c.at[block_rows(targets_ref, height, 0, dx), :], c_keep.at[dx]) for dx in range(N_X)], sems, 11
    )
    for dx in range(N_X):
        stage_c[dx] = sum_c[block_rows(targets_ref, height, 1, dx), :].astype(bf16)
    stores += copy_all([(stage_c, c_sent)], sems, 15)
    for copy in loads[7:]:
        copy.wait()
    sum_a[...] = product(0, 0, split) + product(1, 0, split)
    stores += copy_all(
        [(sum_a.at[block_rows(targets_ref, height, dy, 0), :], a_keep.at[dy]) for dy in range(N_YH)], sems, 16
    )
    for dx, out in ((1, a_sent1), (2, a_sent2), (3, a_sent3)):
        for dy in range(N_YH):
            stage_a[dx - 1, dy] = sum_a[block_rows(targets_ref, height, dy, dx), :].astype(bf16)
        stores += copy_all([(stage_a.at[dx - 1], out)], sems, 17 + dx)
    for copy in stores:
        copy.wait()


def up_terms(place, targets, split, normed_t, base, slope, weight, pooled):
    width, depth = normed_t[0].shape
    patches, columns = base[0].shape
    height = width // (N_YH * N_X)
    hbm = pl.BlockSpec(memory_space=pl.ANY)
    tiles = columns // LANES - 1
    row = pl.BlockSpec((1, width), lambda i, place, targets: (0, 0))
    part_a, part_c = (N_YH, height, split), (N_X, height, columns - split)
    return pl.pallas_call(
        terms_kernel,
        grid_spec=pltpu.PrefetchScalarGridSpec(
            num_scalar_prefetch=2,
            grid=(1,),
            in_specs=[
                row,
                row,
                pl.BlockSpec((LANES, width), lambda i, place, targets: (tiles * (1 + place[0]), 0)),
            ]
            + [hbm] * 7,
            out_specs=[hbm] * 6,
            scratch_shapes=[
                pltpu.VMEM((columns - LANES, width), bf16),
                pltpu.VMEM((2, width, depth), bf16),
                pltpu.VMEM((2, patches, columns), bf16),
                pltpu.VMEM((2, patches, columns), bf16),
                pltpu.VMEM((width, split), f32),
                pltpu.VMEM((width, columns - split), f32),
                pltpu.VMEM((N_X - 1,) + part_a, bf16),
                pltpu.VMEM(part_c, bf16),
                pltpu.SemaphoreType.DMA((21,)),
            ],
        ),
        out_shape=[
            jax.ShapeDtypeStruct(part_a, f32),
            jax.ShapeDtypeStruct(part_a, bf16),
            jax.ShapeDtypeStruct(part_a, bf16),
            jax.ShapeDtypeStruct(part_a, bf16),
            jax.ShapeDtypeStruct(part_c, f32),
            jax.ShapeDtypeStruct(part_c, bf16),
        ],
        compiler_params=pltpu.CompilerParams(vmem_limit_bytes=60 * 2**20),
        cost_estimate=LIGHT,
    )(place, targets, *pooled, weight, *normed_t, *base, *slope, weight)


def per_device(
    image_raw,
    text_raw,
    logit_scale,
    logit_bias,
    pair_offset,
    normed_patches,
    head_cotangent,
    hidden_pre,
    pool_share,
    down_weight,
):
    place = lax.axis_index("dp")
    tensor_index = lax.axis_index("tensor")
    yh = place // (N_CORE * N_Z * N_X)
    x = place // (N_CORE * N_Z) % N_X
    z = place // N_CORE % N_Z
    core = place % N_CORE
    image_rows, width = image_raw.shape
    text_rows = text_raw.shape[0]
    half = text_rows // N_TENSOR
    hidden_here = hidden_pre.shape[1]
    spot = jnp.stack([core, tensor_index]).astype(jnp.int32)
    scalars = jnp.stack([logit_scale, logit_bias])

    text_half = text_half_key(spot, text_raw, half)
    text_half, image_raw, pair_offset, normed_patches, head_cotangent, hidden_pre, pool_share = lax.optimization_barrier(
        (text_half, image_raw, pair_offset, normed_patches, head_cotangent, hidden_pre, pool_share)
    )
    text_far = ring_send(text_half, 7, only=1)
    text_near = jnp.concatenate([text_half, ring_send(text_half, 2)], axis=0)
    image_other = tensor_swap(image_raw)
    text_near, image_other, cotangent_own, offset_sent = lax.optimization_barrier(
        (text_near, image_other, head_cotangent, pair_offset)
    )
    offset_other = tensor_swap(offset_sent)
    text_next = ring_send(text_near, 4)
    rels = jnp.concatenate(
        [
            jnp.array([0, 2, 4, 6], jnp.int32),
            jnp.array([-1, 1, 3, 5], jnp.int32) + 2 * core,
            jnp.array([7], jnp.int32) + 2 * core,
        ]
    )
    text_row = jnp.arange(half, dtype=jnp.int32) + tensor_index * half
    text_value = (text_row[None, :] - text_rows * rels[:, None]).reshape(-1)
    text_valid = jnp.repeat((rels >= 0) & (rels < WINDOW), half)


    columns = 9 * LANES
    start = 8 * LANES
    cotangent_other = torus_send(head_cotangent, core=1)
    hidden_other = torus_send(hidden_pre, core=1)
    share_other = torus_send(pool_share, core=1)
    share_own, share_other = [
        jnp.broadcast_to(jnp.pad(part, (0, 6 * LANES - part.shape[0]))[None, :], (8, 6 * LANES))
        for part in (pool_share, share_other)
    ]
    base_own, slope_own = hidden_base(
        spot, columns, cotangent_own, share_own, down_weight, hidden_pre, HEAVY
    )
    text_next, text_far, base_own, slope_own, offset_other = lax.optimization_barrier(
        (text_next, text_far, base_own, slope_own, offset_other)
    )
    text_window = [text_near, text_next, torus_send(text_near, core=1), torus_send(text_next, core=1), text_far]
    normed_own = transposed(normed_patches, 6 * LANES)
    normed_other = torus_send(normed_own, core=1)

    text_last = text_window[3]
    row = jnp.arange(image_rows, dtype=jnp.int32)
    own_row = row + tensor_index * image_rows
    other_row = row + (1 - tensor_index) * image_rows
    image_value = jnp.concatenate([own_row - pair_offset, other_row - offset_other])
    targets = jnp.stack(
        [(yh + dy) % N_YH * N_X + (x + dx) % N_X for dy in range(N_YH) for dx in range(N_X)]
    ).astype(jnp.int32)
    text_last, share_other, targets = lax.optimization_barrier((text_last, share_other, targets))
    text_window[3] = text_last
    image_part, image_swapped, zero_row, text_own, text_sibling, far = pair_products(
        spot, scalars, image_value, text_value, text_valid, image_raw, image_other, text_window
    )
    zero_theirs = tensor_swap(zero_row)

    near = 2 * half
    returned = torus_send(text_sibling, core=1)
    image_swapped = tensor_swap(image_swapped)
    zero_row, returned, cotangent_other = lax.optimization_barrier((zero_row, returned, cotangent_other))
    text_next = ring_send((text_own[near:] + returned[near:].astype(f32)).astype(bf16), -4)

    base_other, slope_other = hidden_base(
        spot, columns, cotangent_other, share_other, down_weight, hidden_other, LIGHT
    )
    zero_theirs, base_other, slope_other = lax.optimization_barrier((zero_theirs, base_other, slope_other))
    pooled = pooled_row(spot, scalars, image_raw, image_other, zero_row, zero_theirs)
    pooled_other = torus_send(pooled, core=1)
    pooled_other, text_next, image_swapped = lax.optimization_barrier((pooled_other, text_next, image_swapped))

    split = 5 * LANES
    a_keep, a_sent1, a_sent2, a_sent3, c_keep, c_sent = up_terms(
        spot,
        targets,
        split,
        [normed_own, normed_other],
        [base_own, base_other],
        [slope_own, slope_other],
        down_weight,
        [pooled, pooled_other],
    )
    a_keep, image_part, late_text, late_image = lax.optimization_barrier((a_keep, image_part, text_raw, image_raw))
    c_come = torus_send(c_sent, yh=1)
    a_come = [torus_send(part, x=dx) for dx, part in ((2, a_sent2), (1, a_sent1), (3, a_sent3))]
    c_keep = c_keep + c_come.astype(f32)
    c_keep, a_keep, text_own, returned, text_next, far = lax.optimization_barrier(
        (c_keep, a_keep, text_own, returned, text_next, far)
    )
    far = ring_send(far, -7, only=0)
    a_keep = a_keep + (a_come[0].astype(f32) + a_come[1].astype(f32) + a_come[2].astype(f32))
    c_come = [torus_send(c_keep[dx].astype(bf16), x=dx) for dx in (2, 1, 3)]
    a_come = torus_send(a_keep[1].astype(bf16), yh=1)
    total = jnp.concatenate(
        [
            a_keep[0] + a_come.astype(f32),
            c_keep[0] + (c_come[0].astype(f32) + c_come[1].astype(f32) + c_come[2].astype(f32)),
        ],
        axis=1,
    )

    text_near = text_own[:near] + returned[:near].astype(f32) + text_next.astype(f32)
    text_back = ring_send(text_near[half:].astype(bf16), -2)
    total, text_back = lax.optimization_barrier((total, text_back))
    text_dir = logit_scale * (text_near[:half] + text_back.astype(f32) + far.astype(f32))
    text_unit, text_length = unit_rows(lax.dynamic_slice_in_dim(late_text, tensor_index * half, half, 0))
    text_mine = project_back(text_unit, text_length, text_dir).astype(bf16)

    image_unit, image_length = unit_rows(late_image)
    image_dir = logit_scale * (image_part + image_swapped.astype(f32))
    image_grad = project_back(image_unit, image_length, image_dir).astype(bf16)

    rows_chip = total.shape[0] // N_Z
    chunks = total.reshape(N_Z // 2, 2, rows_chip, columns)
    swap_pairs = [(j, j ^ N_CORE) for j in range(N_DP)]
    chunk = lax.dynamic_index_in_dim(chunks, 1 - z % 2, 1, keepdims=False).astype(bf16)
    chunks = lax.dynamic_index_in_dim(chunks, z % 2, 1, keepdims=False)
    chunks = chunks + lax.ppermute(chunk, "dp", swap_pairs).astype(f32)
    total = lax.dynamic_index_in_dim(chunks, z // 2, 0, keepdims=False)
    for hop in (2, 1, 3):
        chunk = lax.dynamic_index_in_dim(chunks, (z // 2 + hop) % (N_Z // 2), 0, keepdims=False).astype(bf16)
        total = total + torus_send(chunk, z=2 * hop).astype(f32)
    text_theirs = tensor_swap(text_mine)
    total, text_theirs, image_grad = lax.optimization_barrier((total, text_theirs, image_grad))
    rows_here = rows_chip // N_CORE
    mine = jnp.where(core == 0, total[:rows_here], total[rows_here:])
    theirs = torus_send(jnp.where(core == 0, total[rows_here:], total[:rows_here]), core=1)
    left = jnp.where(core == 0, mine, theirs)
    right = jnp.where(core == 0, theirs, mine)
    up_grad = jnp.concatenate([left, right[:, columns - start : hidden_here - start]], axis=1)

    text_grad = jnp.where(
        tensor_index == 0,
        jnp.concatenate([text_mine, text_theirs], axis=0),
        jnp.concatenate([text_theirs, text_mine], axis=0),
    )
    return (image_grad, text_grad, up_grad)


def solution(mesh):
    return jax.shard_map(
        per_device,
        mesh=mesh,
        in_specs=(
            P(("dp", "tensor"), None),
            P("dp", None),
            P(),
            P(),
            P(("dp", "tensor")),
            P("dp", None),
            P("dp", None),
            P("dp", "tensor"),
            P("dp"),
            P("tensor", None),
        ),
        out_specs=(P(("dp", "tensor"), None), P("dp", None), P("dp", "tensor")),
        check_vma=False,
    )
```

```python
import functools

import jax
import jax.numpy as jnp
from jax import lax
from jax.experimental import pallas as pl
from jax.experimental.pallas import tpu as pltpu
from jax.sharding import PartitionSpec as P

WINDOW = 8
N_YH, N_X, N_Z, N_CORE = 2, 4, 8, 2
N_DP = N_YH * N_X * N_Z * N_CORE
N_TENSOR = 2
LANES = 128
LIGHT = pl.CostEstimate(flops=1, bytes_accessed=1, transcendentals=0)
HEAVY = pl.CostEstimate(flops=10**10, bytes_accessed=1, transcendentals=0)

epsilon = 1e-06
gelu_root = 0.7978845608028654
gelu_cubic = 0.044715

f32 = jnp.float32
bf16 = jnp.bfloat16


def encode(yh, x, z, core):
    return (((yh % N_YH) * N_X + x % N_X) * N_Z + z % N_Z) * N_CORE + core % N_CORE


def torus_pairs(yh=0, x=0, z=0, core=0):
    pairs = []
    for j in range(N_DP):
        own = (j // (N_CORE * N_Z * N_X), j // (N_CORE * N_Z) % N_X, j // N_CORE % N_Z, j % N_CORE)
        pairs.append((j, encode(own[0] + yh, own[1] + x, own[2] + z, own[3] + core)))
    return pairs


def torus_send(array, **shift):
    return lax.ppermute(array, "dp", torus_pairs(**shift))


def ring_send(array, by, only=None):
    pairs = [(j, (j + by) % N_DP) for j in range(N_DP) if only is None or j % N_CORE == only]
    return lax.ppermute(array, "dp", pairs)


def tensor_swap(array):
    return lax.ppermute(array, "tensor", [(0, 1), (1, 0)])


def unit_rows(raw_rows):
    widened = raw_rows.astype(f32)
    lengths = jnp.sqrt(jnp.sum(widened * widened, axis=-1, keepdims=True) + epsilon)
    return (widened / lengths, lengths)


def project_back(unit_part, lengths, direction):
    radial = jnp.sum(unit_part * direction, axis=-1, keepdims=True)
    return (direction - unit_part * radial) / lengths


def gelu_slope(hidden_in):
    square = hidden_in * hidden_in
    tangent = jnp.tanh(hidden_in * (gelu_root + gelu_root * gelu_cubic * square))
    inner_slope = hidden_in * (0.5 * gelu_root + 1.5 * gelu_root * gelu_cubic * square)
    return 0.5 + 0.5 * tangent + (1.0 - tangent * tangent) * inner_slope


def dot_nt(a, b):
    return lax.dot_general(a, b, (((1,), (1,)), ((), ())), preferred_element_type=f32)


def dot_tn(a, b):
    return lax.dot_general(a, b, (((0,), (0,)), ((), ())), preferred_element_type=f32)


def key_rows(raw):
    return unit_rows(raw)[0].astype(bf16)


def text_key_kernel(half, place_ref, raw_ref, half_ref):
    begin = pl.multiple_of(place_ref[1] * half, half)
    half_ref[...] = key_rows(raw_ref[pl.ds(begin, half), :])


def text_half_key(place, text_raw, half):
    return pl.pallas_call(
        functools.partial(text_key_kernel, half),
        in_specs=[pl.BlockSpec(memory_space=pltpu.SMEM), pl.BlockSpec(memory_space=pltpu.VMEM)],
        out_specs=pl.BlockSpec(memory_space=pltpu.VMEM),
        out_shape=jax.ShapeDtypeStruct((half, text_raw.shape[1]), bf16),
    )(place, text_raw)


def pair_kernel(place_ref, scalar_ref, value_ref, window_value_ref, valid_ref, own_ref, other_ref, *refs):
    window_refs = refs[:-8]
    own_part, other_part, zero_ref, text_own, text_sibling, text_far, key_ref, window_key = refs[-8:]
    half = own_ref.shape[0]
    key_ref[:half, :] = key_rows(own_ref[...])
    key_ref[half:, :] = key_rows(other_ref[...])
    begin = 0
    for ref in window_refs:
        window_key[begin : begin + ref.shape[0], :] = ref[...]
        begin += ref.shape[0]
    logits = scalar_ref[0] * dot_nt(key_ref[...], window_key[...]) + scalar_ref[1]
    target = (value_ref[...] == window_value_ref[...]).astype(f32)
    weight = jnp.where(valid_ref[...] > 0, jax.nn.sigmoid(logits) - target, 0.0).astype(bf16)
    part = jnp.dot(weight, window_key[...], preferred_element_type=f32)
    own_part[...] = part[:half]
    other_part[...] = part[half:].astype(bf16)
    text_part = dot_tn(weight, key_ref[...])
    count = text_own.shape[0]
    text_own[...] = text_part[:count]
    text_sibling[...] = text_part[count : 2 * count].astype(bf16)
    text_far[...] = text_part[2 * count :].astype(bf16)
    zero_ref[...] = jnp.where(place_ref[1] == 0, part[:1], part[half : half + 1])


def pair_products(place, scalars, value, window_value, valid, own, other, window):
    width = own.shape[1]
    rows = value.shape[0]
    depth = window_value.shape[0]
    smem = pl.BlockSpec(memory_space=pltpu.SMEM)
    vmem = pl.BlockSpec(memory_space=pltpu.VMEM)
    return pl.pallas_call(
        pair_kernel,
        in_specs=[smem, smem] + [vmem] * (5 + len(window)),
        out_specs=[vmem] * 6,
        out_shape=[
            jax.ShapeDtypeStruct((rows // 2, width), f32),
            jax.ShapeDtypeStruct((rows // 2, width), bf16),
            jax.ShapeDtypeStruct((1, width), f32),
            jax.ShapeDtypeStruct((2 * rows, width), f32),
            jax.ShapeDtypeStruct((2 * rows, width), bf16),
            jax.ShapeDtypeStruct((depth - 4 * rows, width), bf16),
        ],
        scratch_shapes=[pltpu.VMEM((rows, width), bf16), pltpu.VMEM((depth, width), bf16)],
        compiler_params=pltpu.CompilerParams(vmem_limit_bytes=16 * 2**20),
        cost_estimate=LIGHT,
    )(
        place,
        scalars,
        value[:, None],
        window_value[None, :],
        valid.astype(jnp.int32)[None, :],
        own,
        other,
        *window,
    )


def pooled_kernel(place_ref, scalar_ref, own_ref, other_ref, mine_ref, theirs_ref, pooled_ref):
    raw = jnp.where(place_ref[1] == 0, own_ref[:1, :].astype(f32), other_ref[:1, :].astype(f32))
    unit, length = unit_rows(raw)
    direction = scalar_ref[0] * (mine_ref[...] + theirs_ref[...])
    pooled_ref[...] = project_back(unit, length, direction).astype(bf16)


def pooled_row(place, scalars, own, other, mine, theirs):
    smem = pl.BlockSpec(memory_space=pltpu.SMEM)
    vmem = pl.BlockSpec(memory_space=pltpu.VMEM)
    return pl.pallas_call(
        pooled_kernel,
        in_specs=[smem, smem] + [vmem] * 4,
        out_specs=vmem,
        out_shape=jax.ShapeDtypeStruct(mine.shape, bf16),
    )(place, scalars, own, other, mine, theirs)


def transpose_kernel(patches, normed_ref, out_ref):
    block = normed_ref[...]
    kept = lax.broadcasted_iota(jnp.int32, block.shape, 0) < patches
    out_ref[...] = jnp.where(kept, block, jnp.zeros_like(block)).T


def transposed(normed, rows):
    patches, width = normed.shape
    step = 3 * LANES
    return pl.pallas_call(
        functools.partial(transpose_kernel, patches),
        grid=(width // step,),
        in_specs=[pl.BlockSpec((rows, step), lambda i: (0, i))],
        out_specs=pl.BlockSpec((step, rows), lambda i: (i, 0)),
        out_shape=jax.ShapeDtypeStruct((width, rows), bf16),
        compiler_params=pltpu.CompilerParams(vmem_limit_bytes=8 * 2**20),
        cost_estimate=LIGHT,
    )(normed)


def copy_all(pairs, sems, first):
    copies = [pltpu.make_async_copy(src, dst, sems.at[first + i]) for i, (src, dst) in enumerate(pairs)]
    for copy in copies:
        copy.start()
    return copies


def base_kernel(place_ref, share_ref, weight_tail, hidden_tail, cotangent_hbm, weight_hbm, hidden_hbm, *refs):
    base_hbm, slope_hbm, cotangent, weight, hidden, base, slope, sems = refs
    patches, columns = base.shape
    start = columns - LANES
    step = start // 2
    begin = place_ref[0] * start
    halves = [pl.ds(pl.multiple_of(begin + i * step, step), step) for i in range(2)]
    wheres = [pl.ds(i * step, step) for i in range(2)]
    loads = copy_all(
        [
            (hidden_hbm.at[:, halves[0]], hidden.at[:, wheres[0]]),
            (cotangent_hbm, cotangent),
            (weight_hbm.at[halves[0], :], weight.at[wheres[0], :]),
            (hidden_hbm.at[:, halves[1]], hidden.at[:, wheres[1]]),
            (weight_hbm.at[halves[1], :], weight.at[wheres[1], :]),
        ],
        sems,
        0,
    )
    share = share_ref[...].T[:patches, :1]

    def block(weight_rows, hidden_block, where, ready):
        kept = gelu_slope(hidden_block.astype(f32))
        slope[:, where] = (share * kept).astype(bf16)
        for copy in ready:
            copy.wait()
        base[:, where] = (dot_nt(cotangent[...], weight_rows[...]) * kept).astype(bf16)

    def store(where, first):
        return copy_all(
            [(base.at[:, where], base_hbm.at[:, where]), (slope.at[:, where], slope_hbm.at[:, where])], sems, first
        )

    loads[0].wait()
    block(weight.at[wheres[0], :], hidden[:, wheres[0]], wheres[0], loads[1:3])
    stores = store(wheres[0], 5)
    loads[3].wait()
    block(weight.at[wheres[1], :], hidden[:, wheres[1]], wheres[1], loads[4:])
    stores += store(wheres[1], 7)
    where = pl.ds(start, LANES)
    block(weight_tail, hidden_tail[...], where, [])
    stores += store(where, 9)
    for copy in stores:
        copy.wait()


def hidden_base(place, columns, cotangent, share, weight, hidden, cost):
    patches, width = cotangent.shape
    start = columns - LANES
    tiles = start // LANES
    hbm = pl.BlockSpec(memory_space=pl.ANY)
    out = jax.ShapeDtypeStruct((patches, columns), bf16)
    return pl.pallas_call(
        base_kernel,
        grid_spec=pltpu.PrefetchScalarGridSpec(
            num_scalar_prefetch=1,
            grid=(1,),
            in_specs=[
                pl.BlockSpec(share.shape, lambda i, place: (0, 0)),
                pl.BlockSpec((LANES, width), lambda i, place: (tiles * (1 + place[0]), 0)),
                pl.BlockSpec((patches, LANES), lambda i, place: (0, tiles * (1 + place[0]))),
                hbm,
                hbm,
                hbm,
            ],
            out_specs=[hbm, hbm],
            scratch_shapes=[
                pltpu.VMEM((patches, width), bf16),
                pltpu.VMEM((start, width), bf16),
                pltpu.VMEM((patches, start), bf16),
                pltpu.VMEM((patches, columns), bf16),
                pltpu.VMEM((patches, columns), bf16),
                pltpu.SemaphoreType.DMA((11,)),
            ],
        ),
        out_shape=[out, out],
        compiler_params=pltpu.CompilerParams(vmem_limit_bytes=60 * 2**20),
        cost_estimate=cost,
    )(place, share, weight, hidden, cotangent, weight, hidden)


def block_rows(targets_ref, height, dy, dx):
    return pl.ds(pl.multiple_of(targets_ref[dy * N_X + dx] * height, 16), height)


def terms_kernel(
    place_ref,
    targets_ref,
    pooled0_ref,
    pooled1_ref,
    weight_tail,
    normed0_hbm,
    normed1_hbm,
    base0_hbm,
    base1_hbm,
    slope0_hbm,
    slope1_hbm,
    weight_hbm,
    a_keep,
    a_sent1,
    a_sent2,
    a_sent3,
    c_keep,
    c_sent,
    weight,
    normed,
    base,
    slope,
    sum_a,
    sum_c,
    stage_a,
    stage_c,
    sems,
):
    _, patches, columns = base.shape
    width = weight.shape[1]
    start = columns - LANES
    split = a_keep.shape[2]
    height = a_keep.shape[1]
    begin = pl.multiple_of(place_ref[0] * start, start)
    part_a, part_c = pl.ds(0, split), pl.ds(split, columns - split)
    images = ((slope0_hbm, base0_hbm, normed0_hbm), (slope1_hbm, base1_hbm, normed1_hbm))
    pairs = [(weight_hbm.at[pl.ds(begin, start), :], weight)]
    for i, (slope_hbm, base_hbm, normed_hbm) in enumerate(images):
        pairs += [
            (slope_hbm.at[:, part_c], slope.at[i, :, part_c]),
            (base_hbm.at[:, part_c], base.at[i, :, part_c]),
            (normed_hbm, normed.at[i]),
        ]
    for i, (slope_hbm, base_hbm, normed_hbm) in enumerate(images):
        pairs += [
            (slope_hbm.at[:, part_a], slope.at[i, :, part_a]),
            (base_hbm.at[:, part_a], base.at[i, :, part_a]),
        ]
    loads = copy_all(pairs, sems, 0)
    pooled = jnp.concatenate(
        [jnp.broadcast_to(ref[...].astype(f32), (8, width)) for ref in (pooled0_ref, pooled1_ref)], axis=0
    ).astype(bf16)
    loads[0].wait()
    lift = jnp.concatenate([dot_nt(pooled, weight[...]), dot_nt(pooled, weight_tail[...])], axis=1)

    def product(image, first, last):
        lifted = lift[8 * image : 8 * image + 1, first:last] * slope[image, :, first:last].astype(f32)
        grad = (base[image, :, first:last].astype(f32) + lifted).astype(bf16)
        return jnp.dot(normed[image, :, :patches], grad, preferred_element_type=f32)

    for copy in loads[1:4]:
        copy.wait()
    sum_c[...] = product(0, split, columns)
    for copy in loads[4:7]:
        copy.wait()
    sum_c[...] += product(1, split, columns)
    stores = copy_all(
        [(sum_c.at[block_rows(targets_ref, height, 0, dx), :], c_keep.at[dx]) for dx in range(N_X)], sems, 11
    )
    for dx in range(N_X):
        stage_c[dx] = sum_c[block_rows(targets_ref, height, 1, dx), :].astype(bf16)
    stores += copy_all([(stage_c, c_sent)], sems, 15)
    for copy in loads[7:]:
        copy.wait()
    sum_a[...] = product(0, 0, split) + product(1, 0, split)
    stores += copy_all(
        [(sum_a.at[block_rows(targets_ref, height, dy, 0), :], a_keep.at[dy]) for dy in range(N_YH)], sems, 16
    )
    for dx, out in ((1, a_sent1), (2, a_sent2), (3, a_sent3)):
        for dy in range(N_YH):
            stage_a[dx - 1, dy] = sum_a[block_rows(targets_ref, height, dy, dx), :].astype(bf16)
        stores += copy_all([(stage_a.at[dx - 1], out)], sems, 17 + dx)
    for copy in stores:
        copy.wait()


def up_terms(place, targets, split, normed_t, base, slope, weight, pooled):
    width, depth = normed_t[0].shape
    patches, columns = base[0].shape
    height = width // (N_YH * N_X)
    hbm = pl.BlockSpec(memory_space=pl.ANY)
    tiles = columns // LANES - 1
    row = pl.BlockSpec((1, width), lambda i, place, targets: (0, 0))
    part_a, part_c = (N_YH, height, split), (N_X, height, columns - split)
    return pl.pallas_call(
        terms_kernel,
        grid_spec=pltpu.PrefetchScalarGridSpec(
            num_scalar_prefetch=2,
            grid=(1,),
            in_specs=[
                row,
                row,
                pl.BlockSpec((LANES, width), lambda i, place, targets: (tiles * (1 + place[0]), 0)),
            ]
            + [hbm] * 7,
            out_specs=[hbm] * 6,
            scratch_shapes=[
                pltpu.VMEM((columns - LANES, width), bf16),
                pltpu.VMEM((2, width, depth), bf16),
                pltpu.VMEM((2, patches, columns), bf16),
                pltpu.VMEM((2, patches, columns), bf16),
                pltpu.VMEM((width, split), f32),
                pltpu.VMEM((width, columns - split), f32),
                pltpu.VMEM((N_X - 1,) + part_a, bf16),
                pltpu.VMEM(part_c, bf16),
                pltpu.SemaphoreType.DMA((21,)),
            ],
        ),
        out_shape=[
            jax.ShapeDtypeStruct(part_a, f32),
            jax.ShapeDtypeStruct(part_a, bf16),
            jax.ShapeDtypeStruct(part_a, bf16),
            jax.ShapeDtypeStruct(part_a, bf16),
            jax.ShapeDtypeStruct(part_c, f32),
            jax.ShapeDtypeStruct(part_c, bf16),
        ],
        compiler_params=pltpu.CompilerParams(vmem_limit_bytes=60 * 2**20),
        cost_estimate=LIGHT,
    )(place, targets, *pooled, weight, *normed_t, *base, *slope, weight)


def per_device(
    image_raw,
    text_raw,
    logit_scale,
    logit_bias,
    pair_offset,
    normed_patches,
    head_cotangent,
    hidden_pre,
    pool_share,
    down_weight,
):
    place = lax.axis_index("dp")
    tensor_index = lax.axis_index("tensor")
    yh = place // (N_CORE * N_Z * N_X)
    x = place // (N_CORE * N_Z) % N_X
    z = place // N_CORE % N_Z
    core = place % N_CORE
    image_rows, width = image_raw.shape
    text_rows = text_raw.shape[0]
    half = text_rows // N_TENSOR
    hidden_here = hidden_pre.shape[1]
    spot = jnp.stack([core, tensor_index]).astype(jnp.int32)
    scalars = jnp.stack([logit_scale, logit_bias])

    text_half = text_half_key(spot, text_raw, half)
    text_half, image_raw, pair_offset, normed_patches, head_cotangent, hidden_pre, pool_share = lax.optimization_barrier(
        (text_half, image_raw, pair_offset, normed_patches, head_cotangent, hidden_pre, pool_share)
    )
    text_far = ring_send(text_half, 7, only=1)
    text_near = jnp.concatenate([text_half, ring_send(text_half, 2)], axis=0)
    image_other = tensor_swap(image_raw)
    text_near, image_other, cotangent_own, offset_sent = lax.optimization_barrier(
        (text_near, image_other, head_cotangent, pair_offset)
    )
    offset_other = tensor_swap(offset_sent)
    text_next = ring_send(text_near, 4)
    rels = jnp.concatenate(
        [
            jnp.array([0, 2, 4, 6], jnp.int32),
            jnp.array([-1, 1, 3, 5], jnp.int32) + 2 * core,
            jnp.array([7], jnp.int32) + 2 * core,
        ]
    )
    text_row = jnp.arange(half, dtype=jnp.int32) + tensor_index * half
    text_value = (text_row[None, :] - text_rows * rels[:, None]).reshape(-1)
    text_valid = jnp.repeat((rels >= 0) & (rels < WINDOW), half)


    columns = 9 * LANES
    start = 8 * LANES
    cotangent_other = torus_send(head_cotangent, core=1)
    hidden_other = torus_send(hidden_pre, core=1)
    share_other = torus_send(pool_share, core=1)
    share_own, share_other = [
        jnp.broadcast_to(jnp.pad(part, (0, 6 * LANES - part.shape[0]))[None, :], (8, 6 * LANES))
        for part in (pool_share, share_other)
    ]
    base_own, slope_own = hidden_base(
        spot, columns, cotangent_own, share_own, down_weight, hidden_pre, HEAVY
    )
    text_next, text_far, base_own, slope_own, offset_other = lax.optimization_barrier(
        (text_next, text_far, base_own, slope_own, offset_other)
    )
    text_window = [text_near, text_next, torus_send(text_near, core=1), torus_send(text_next, core=1), text_far]
    normed_own = transposed(normed_patches, 6 * LANES)
    normed_other = torus_send(normed_own, core=1)

    text_last = text_window[3]
    row = jnp.arange(image_rows, dtype=jnp.int32)
    own_row = row + tensor_index * image_rows
    other_row = row + (1 - tensor_index) * image_rows
    image_value = jnp.concatenate([own_row - pair_offset, other_row - offset_other])
    targets = jnp.stack(
        [(yh + dy) % N_YH * N_X + (x + dx) % N_X for dy in range(N_YH) for dx in range(N_X)]
    ).astype(jnp.int32)
    text_last, share_other, targets = lax.optimization_barrier((text_last, share_other, targets))
    text_window[3] = text_last
    image_part, image_swapped, zero_row, text_own, text_sibling, far = pair_products(
        spot, scalars, image_value, text_value, text_valid, image_raw, image_other, text_window
    )
    zero_theirs = tensor_swap(zero_row)

    near = 2 * half
    image_swapped = tensor_swap(image_swapped)
    zero_row, cotangent_other = lax.optimization_barrier((zero_row, cotangent_other))

    base_other, slope_other = hidden_base(
        spot, columns, cotangent_other, share_other, down_weight, hidden_other, LIGHT
    )
    zero_theirs, base_other, slope_other = lax.optimization_barrier((zero_theirs, base_other, slope_other))
    pooled = pooled_row(spot, scalars, image_raw, image_other, zero_row, zero_theirs)
    pooled_other = torus_send(pooled, core=1)
    pooled_other, image_swapped = lax.optimization_barrier((pooled_other, image_swapped))

    split = 5 * LANES
    a_keep, a_sent1, a_sent2, a_sent3, c_keep, c_sent = up_terms(
        spot,
        targets,
        split,
        [normed_own, normed_other],
        [base_own, base_other],
        [slope_own, slope_other],
        down_weight,
        [pooled, pooled_other],
    )
    a_keep, image_part, late_text, late_image, text_own, text_sibling = lax.optimization_barrier(
        (a_keep, image_part, text_raw, image_raw, text_own, text_sibling)
    )
    returned = torus_send(text_sibling, core=1)
    text_next = ring_send((text_own[near:] + returned[near:].astype(f32)).astype(bf16), -4)
    c_come = torus_send(c_sent, yh=1)
    a_come = [torus_send(part, x=dx) for dx, part in ((2, a_sent2), (1, a_sent1), (3, a_sent3))]
    c_keep = c_keep + c_come.astype(f32)
    c_keep, a_keep, text_own, returned, text_next, far = lax.optimization_barrier(
        (c_keep, a_keep, text_own, returned, text_next, far)
    )
    far = ring_send(far, -7, only=0)
    a_keep = a_keep + (a_come[0].astype(f32) + a_come[1].astype(f32) + a_come[2].astype(f32))
    c_come = [torus_send(c_keep[dx].astype(bf16), x=dx) for dx in (2, 1, 3)]
    a_come = torus_send(a_keep[1].astype(bf16), yh=1)
    total = jnp.concatenate(
        [
            a_keep[0] + a_come.astype(f32),
            c_keep[0] + (c_come[0].astype(f32) + c_come[1].astype(f32) + c_come[2].astype(f32)),
        ],
        axis=1,
    )

    text_near = text_own[:near] + returned[:near].astype(f32) + text_next.astype(f32)
    text_back = ring_send(text_near[half:].astype(bf16), -2)
    total, text_back = lax.optimization_barrier((total, text_back))
    text_dir = logit_scale * (text_near[:half] + text_back.astype(f32) + far.astype(f32))
    text_unit, text_length = unit_rows(lax.dynamic_slice_in_dim(late_text, tensor_index * half, half, 0))
    text_mine = project_back(text_unit, text_length, text_dir).astype(bf16)

    image_unit, image_length = unit_rows(late_image)
    image_dir = logit_scale * (image_part + image_swapped.astype(f32))
    image_grad = project_back(image_unit, image_length, image_dir).astype(bf16)

    rows_chip = total.shape[0] // N_Z
    chunks = total.reshape(N_Z // 2, 2, rows_chip, columns)
    swap_pairs = [(j, j ^ N_CORE) for j in range(N_DP)]
    chunk = lax.dynamic_index_in_dim(chunks, 1 - z % 2, 1, keepdims=False).astype(bf16)
    chunks = lax.dynamic_index_in_dim(chunks, z % 2, 1, keepdims=False)
    chunks = chunks + lax.ppermute(chunk, "dp", swap_pairs).astype(f32)
    total = lax.dynamic_index_in_dim(chunks, z // 2, 0, keepdims=False)
    for hop in (2, 1, 3):
        chunk = lax.dynamic_index_in_dim(chunks, (z // 2 + hop) % (N_Z // 2), 0, keepdims=False).astype(bf16)
        total = total + torus_send(chunk, z=2 * hop).astype(f32)
    text_theirs = tensor_swap(text_mine)
    total, text_theirs, image_grad = lax.optimization_barrier((total, text_theirs, image_grad))
    rows_here = rows_chip // N_CORE
    mine = jnp.where(core == 0, total[:rows_here], total[rows_here:])
    theirs = torus_send(jnp.where(core == 0, total[rows_here:], total[:rows_here]), core=1)
    left = jnp.where(core == 0, mine, theirs)
    right = jnp.where(core == 0, theirs, mine)
    up_grad = jnp.concatenate([left, right[:, columns - start : hidden_here - start]], axis=1)

    text_grad = jnp.where(
        tensor_index == 0,
        jnp.concatenate([text_mine, text_theirs], axis=0),
        jnp.concatenate([text_theirs, text_mine], axis=0),
    )
    return (image_grad, text_grad, up_grad)


def solution(mesh):
    return jax.shard_map(
        per_device,
        mesh=mesh,
        in_specs=(
            P(("dp", "tensor"), None),
            P("dp", None),
            P(),
            P(),
            P(("dp", "tensor")),
            P("dp", None),
            P("dp", None),
            P("dp", "tensor"),
            P("dp"),
            P("tensor", None),
        ),
        out_specs=(P(("dp", "tensor"), None), P("dp", None), P("dp", "tensor")),
        check_vma=False,
    )
```

```python
import functools

import jax
import jax.numpy as jnp
from jax import lax
from jax.experimental import pallas as pl
from jax.experimental.pallas import tpu as pltpu
from jax.sharding import PartitionSpec as P

WINDOW = 8
N_YH, N_X, N_Z, N_CORE = 2, 4, 8, 2
N_DP = N_YH * N_X * N_Z * N_CORE
N_TENSOR = 2
LANES = 128
LIGHT = pl.CostEstimate(flops=1, bytes_accessed=1, transcendentals=0)
HEAVY = pl.CostEstimate(flops=10**10, bytes_accessed=1, transcendentals=0)

epsilon = 1e-06
gelu_root = 0.7978845608028654
gelu_cubic = 0.044715

f32 = jnp.float32
bf16 = jnp.bfloat16


def encode(yh, x, z, core):
    return (((yh % N_YH) * N_X + x % N_X) * N_Z + z % N_Z) * N_CORE + core % N_CORE


def torus_pairs(yh=0, x=0, z=0, core=0):
    pairs = []
    for j in range(N_DP):
        own = (j // (N_CORE * N_Z * N_X), j // (N_CORE * N_Z) % N_X, j // N_CORE % N_Z, j % N_CORE)
        pairs.append((j, encode(own[0] + yh, own[1] + x, own[2] + z, own[3] + core)))
    return pairs


def torus_send(array, **shift):
    return lax.ppermute(array, "dp", torus_pairs(**shift))


def ring_send(array, by, only=None):
    pairs = [(j, (j + by) % N_DP) for j in range(N_DP) if only is None or j % N_CORE == only]
    return lax.ppermute(array, "dp", pairs)


def tensor_swap(array):
    return lax.ppermute(array, "tensor", [(0, 1), (1, 0)])


def unit_rows(raw_rows):
    widened = raw_rows.astype(f32)
    lengths = jnp.sqrt(jnp.sum(widened * widened, axis=-1, keepdims=True) + epsilon)
    return (widened / lengths, lengths)


def project_back(unit_part, lengths, direction):
    radial = jnp.sum(unit_part * direction, axis=-1, keepdims=True)
    return (direction - unit_part * radial) / lengths


def gelu_slope(hidden_in):
    square = hidden_in * hidden_in
    tangent = jnp.tanh(hidden_in * (gelu_root + gelu_root * gelu_cubic * square))
    inner_slope = hidden_in * (0.5 * gelu_root + 1.5 * gelu_root * gelu_cubic * square)
    return 0.5 + 0.5 * tangent + (1.0 - tangent * tangent) * inner_slope


def dot_nt(a, b):
    return lax.dot_general(a, b, (((1,), (1,)), ((), ())), preferred_element_type=f32)


def dot_tn(a, b):
    return lax.dot_general(a, b, (((0,), (0,)), ((), ())), preferred_element_type=f32)


def key_rows(raw):
    return unit_rows(raw)[0].astype(bf16)


def text_key_kernel(half, place_ref, raw_ref, half_ref):
    begin = pl.multiple_of(place_ref[1] * half, half)
    half_ref[...] = key_rows(raw_ref[pl.ds(begin, half), :])


def text_half_key(place, text_raw, half):
    return pl.pallas_call(
        functools.partial(text_key_kernel, half),
        in_specs=[pl.BlockSpec(memory_space=pltpu.SMEM), pl.BlockSpec(memory_space=pltpu.VMEM)],
        out_specs=pl.BlockSpec(memory_space=pltpu.VMEM),
        out_shape=jax.ShapeDtypeStruct((half, text_raw.shape[1]), bf16),
    )(place, text_raw)


def pair_kernel(place_ref, scalar_ref, value_ref, window_value_ref, valid_ref, own_ref, other_ref, *refs):
    window_refs = refs[:-8]
    own_part, other_part, zero_ref, text_own, text_sibling, text_far, key_ref, window_key = refs[-8:]
    half = own_ref.shape[0]
    key_ref[:half, :] = key_rows(own_ref[...])
    key_ref[half:, :] = key_rows(other_ref[...])
    begin = 0
    for ref in window_refs:
        window_key[begin : begin + ref.shape[0], :] = ref[...]
        begin += ref.shape[0]
    logits = scalar_ref[0] * dot_nt(key_ref[...], window_key[...]) + scalar_ref[1]
    target = (value_ref[...] == window_value_ref[...]).astype(f32)
    weight = jnp.where(valid_ref[...] > 0, jax.nn.sigmoid(logits) - target, 0.0).astype(bf16)
    part = jnp.dot(weight, window_key[...], preferred_element_type=f32)
    own_part[...] = part[:half]
    other_part[...] = part[half:].astype(bf16)
    text_part = dot_tn(weight, key_ref[...])
    count = text_own.shape[0]
    text_own[...] = text_part[:count]
    text_sibling[...] = text_part[count : 2 * count].astype(bf16)
    text_far[...] = text_part[2 * count :].astype(bf16)
    zero_ref[...] = jnp.where(place_ref[1] == 0, part[:1], part[half : half + 1])


def pair_products(place, scalars, value, window_value, valid, own, other, window):
    width = own.shape[1]
    rows = value.shape[0]
    depth = window_value.shape[0]
    smem = pl.BlockSpec(memory_space=pltpu.SMEM)
    vmem = pl.BlockSpec(memory_space=pltpu.VMEM)
    return pl.pallas_call(
        pair_kernel,
        in_specs=[smem, smem] + [vmem] * (5 + len(window)),
        out_specs=[vmem] * 6,
        out_shape=[
            jax.ShapeDtypeStruct((rows // 2, width), f32),
            jax.ShapeDtypeStruct((rows // 2, width), bf16),
            jax.ShapeDtypeStruct((1, width), f32),
            jax.ShapeDtypeStruct((2 * rows, width), f32),
            jax.ShapeDtypeStruct((2 * rows, width), bf16),
            jax.ShapeDtypeStruct((depth - 4 * rows, width), bf16),
        ],
        scratch_shapes=[pltpu.VMEM((rows, width), bf16), pltpu.VMEM((depth, width), bf16)],
        compiler_params=pltpu.CompilerParams(vmem_limit_bytes=16 * 2**20),
        cost_estimate=LIGHT,
    )(
        place,
        scalars,
        value[:, None],
        window_value[None, :],
        valid.astype(jnp.int32)[None, :],
        own,
        other,
        *window,
    )


def transpose_kernel(patches, normed_ref, out_ref):
    block = normed_ref[...]
    kept = lax.broadcasted_iota(jnp.int32, block.shape, 0) < patches
    out_ref[...] = jnp.where(kept, block, jnp.zeros_like(block)).T


def transposed(normed, rows):
    patches, width = normed.shape
    step = 3 * LANES
    return pl.pallas_call(
        functools.partial(transpose_kernel, patches),
        grid=(width // step,),
        in_specs=[pl.BlockSpec((rows, step), lambda i: (0, i))],
        out_specs=pl.BlockSpec((step, rows), lambda i: (i, 0)),
        out_shape=jax.ShapeDtypeStruct((width, rows), bf16),
        compiler_params=pltpu.CompilerParams(vmem_limit_bytes=8 * 2**20),
        cost_estimate=LIGHT,
    )(normed)


def copy_all(pairs, sems, first):
    copies = [pltpu.make_async_copy(src, dst, sems.at[first + i]) for i, (src, dst) in enumerate(pairs)]
    for copy in copies:
        copy.start()
    return copies


def base_kernel(place_ref, share_ref, weight_tail, hidden_tail, cotangent_hbm, weight_hbm, hidden_hbm, *refs):
    base_hbm, slope_hbm, cotangent, weight, hidden, base, slope, sems = refs
    patches, columns = base.shape
    start = columns - LANES
    step = start // 2
    begin = place_ref[0] * start
    halves = [pl.ds(pl.multiple_of(begin + i * step, step), step) for i in range(2)]
    wheres = [pl.ds(i * step, step) for i in range(2)]
    loads = copy_all(
        [
            (hidden_hbm.at[:, halves[0]], hidden.at[:, wheres[0]]),
            (cotangent_hbm, cotangent),
            (weight_hbm.at[halves[0], :], weight.at[wheres[0], :]),
            (hidden_hbm.at[:, halves[1]], hidden.at[:, wheres[1]]),
            (weight_hbm.at[halves[1], :], weight.at[wheres[1], :]),
        ],
        sems,
        0,
    )
    share = share_ref[...].T[:patches, :1]

    def block(weight_rows, hidden_block, where, ready):
        kept = gelu_slope(hidden_block.astype(f32))
        slope[:, where] = (share * kept).astype(bf16)
        for copy in ready:
            copy.wait()
        base[:, where] = (dot_nt(cotangent[...], weight_rows[...]) * kept).astype(bf16)

    def store(where, first):
        return copy_all(
            [(base.at[:, where], base_hbm.at[:, where]), (slope.at[:, where], slope_hbm.at[:, where])], sems, first
        )

    loads[0].wait()
    block(weight.at[wheres[0], :], hidden[:, wheres[0]], wheres[0], loads[1:3])
    stores = store(wheres[0], 5)
    loads[3].wait()
    block(weight.at[wheres[1], :], hidden[:, wheres[1]], wheres[1], loads[4:])
    stores += store(wheres[1], 7)
    where = pl.ds(start, LANES)
    block(weight_tail, hidden_tail[...], where, [])
    stores += store(where, 9)
    for copy in stores:
        copy.wait()


def hidden_base(place, columns, cotangent, share, weight, hidden, cost):
    patches, width = cotangent.shape
    start = columns - LANES
    tiles = start // LANES
    hbm = pl.BlockSpec(memory_space=pl.ANY)
    out = jax.ShapeDtypeStruct((patches, columns), bf16)
    return pl.pallas_call(
        base_kernel,
        grid_spec=pltpu.PrefetchScalarGridSpec(
            num_scalar_prefetch=1,
            grid=(1,),
            in_specs=[
                pl.BlockSpec(share.shape, lambda i, place: (0, 0)),
                pl.BlockSpec((LANES, width), lambda i, place: (tiles * (1 + place[0]), 0)),
                pl.BlockSpec((patches, LANES), lambda i, place: (0, tiles * (1 + place[0]))),
                hbm,
                hbm,
                hbm,
            ],
            out_specs=[hbm, hbm],
            scratch_shapes=[
                pltpu.VMEM((patches, width), bf16),
                pltpu.VMEM((start, width), bf16),
                pltpu.VMEM((patches, start), bf16),
                pltpu.VMEM((patches, columns), bf16),
                pltpu.VMEM((patches, columns), bf16),
                pltpu.SemaphoreType.DMA((11,)),
            ],
        ),
        out_shape=[out, out],
        compiler_params=pltpu.CompilerParams(vmem_limit_bytes=60 * 2**20),
        cost_estimate=cost,
    )(place, share, weight, hidden, cotangent, weight, hidden)


def block_rows(targets_ref, height, dy, dx):
    return pl.ds(pl.multiple_of(targets_ref[dy * N_X + dx] * height, 16), height)


def terms_kernel(
    place_ref,
    targets_ref,
    row0_ref,
    row1_ref,
    weight_tail,
    normed0_hbm,
    normed1_hbm,
    base0_hbm,
    base1_hbm,
    slope0_hbm,
    slope1_hbm,
    weight_hbm,
    a_keep,
    a_sent1,
    a_sent2,
    a_sent3,
    c_keep,
    c_sent,
    weight,
    normed,
    base,
    slope,
    sum_a,
    sum_c,
    stage_a,
    stage_c,
    sems,
):
    _, patches, columns = base.shape
    width = weight.shape[1]
    start = columns - LANES
    split = a_keep.shape[2]
    height = a_keep.shape[1]
    begin = pl.multiple_of(place_ref[0] * start, start)
    part_a, part_c = pl.ds(0, split), pl.ds(split, columns - split)
    images = ((slope0_hbm, base0_hbm, normed0_hbm), (slope1_hbm, base1_hbm, normed1_hbm))
    pairs = [(weight_hbm.at[pl.ds(begin, start), :], weight)]
    for i, (slope_hbm, base_hbm, normed_hbm) in enumerate(images):
        pairs += [
            (slope_hbm.at[:, part_c], slope.at[i, :, part_c]),
            (base_hbm.at[:, part_c], base.at[i, :, part_c]),
            (normed_hbm, normed.at[i]),
        ]
    for i, (slope_hbm, base_hbm, normed_hbm) in enumerate(images):
        pairs += [
            (slope_hbm.at[:, part_a], slope.at[i, :, part_a]),
            (base_hbm.at[:, part_a], base.at[i, :, part_a]),
        ]
    loads = copy_all(pairs, sems, 0)
    pooled = []
    for ref in (row0_ref, row1_ref):
        unit, length = unit_rows(ref[1:2, :])
        pooled.append(jnp.broadcast_to(project_back(unit, length, ref[0:1, :]), (8, width)))
    pooled = jnp.concatenate(pooled, axis=0).astype(bf16)
    loads[0].wait()
    lift = jnp.concatenate([dot_nt(pooled, weight[...]), dot_nt(pooled, weight_tail[...])], axis=1)

    def product(image, first, last):
        lifted = lift[8 * image : 8 * image + 1, first:last] * slope[image, :, first:last].astype(f32)
        grad = (base[image, :, first:last].astype(f32) + lifted).astype(bf16)
        return jnp.dot(normed[image, :, :patches], grad, preferred_element_type=f32)

    for copy in loads[1:4]:
        copy.wait()
    sum_c[...] = product(0, split, columns)
    for copy in loads[4:7]:
        copy.wait()
    sum_c[...] += product(1, split, columns)
    stores = copy_all(
        [(sum_c.at[block_rows(targets_ref, height, 0, dx), :], c_keep.at[dx]) for dx in range(N_X)], sems, 11
    )
    for dx in range(N_X):
        stage_c[dx] = sum_c[block_rows(targets_ref, height, 1, dx), :].astype(bf16)
    stores += copy_all([(stage_c, c_sent)], sems, 15)
    for copy in loads[7:]:
        copy.wait()
    sum_a[...] = product(0, 0, split) + product(1, 0, split)
    stores += copy_all(
        [(sum_a.at[block_rows(targets_ref, height, dy, 0), :], a_keep.at[dy]) for dy in range(N_YH)], sems, 16
    )
    for dx, out in ((1, a_sent1), (2, a_sent2), (3, a_sent3)):
        for dy in range(N_YH):
            stage_a[dx - 1, dy] = sum_a[block_rows(targets_ref, height, dy, dx), :].astype(bf16)
        stores += copy_all([(stage_a.at[dx - 1], out)], sems, 17 + dx)
    for copy in stores:
        copy.wait()


def up_terms(place, targets, split, normed_t, base, slope, weight, rows):
    width, depth = normed_t[0].shape
    patches, columns = base[0].shape
    height = width // (N_YH * N_X)
    hbm = pl.BlockSpec(memory_space=pl.ANY)
    tiles = columns // LANES - 1
    row = pl.BlockSpec((2, width), lambda i, place, targets: (0, 0))
    part_a, part_c = (N_YH, height, split), (N_X, height, columns - split)
    return pl.pallas_call(
        terms_kernel,
        grid_spec=pltpu.PrefetchScalarGridSpec(
            num_scalar_prefetch=2,
            grid=(1,),
            in_specs=[
                row,
                row,
                pl.BlockSpec((LANES, width), lambda i, place, targets: (tiles * (1 + place[0]), 0)),
            ]
            + [hbm] * 7,
            out_specs=[hbm] * 6,
            scratch_shapes=[
                pltpu.VMEM((columns - LANES, width), bf16),
                pltpu.VMEM((2, width, depth), bf16),
                pltpu.VMEM((2, patches, columns), bf16),
                pltpu.VMEM((2, patches, columns), bf16),
                pltpu.VMEM((width, split), f32),
                pltpu.VMEM((width, columns - split), f32),
                pltpu.VMEM((N_X - 1,) + part_a, bf16),
                pltpu.VMEM(part_c, bf16),
                pltpu.SemaphoreType.DMA((21,)),
            ],
        ),
        out_shape=[
            jax.ShapeDtypeStruct(part_a, f32),
            jax.ShapeDtypeStruct(part_a, bf16),
            jax.ShapeDtypeStruct(part_a, bf16),
            jax.ShapeDtypeStruct(part_a, bf16),
            jax.ShapeDtypeStruct(part_c, f32),
            jax.ShapeDtypeStruct(part_c, bf16),
        ],
        compiler_params=pltpu.CompilerParams(vmem_limit_bytes=60 * 2**20),
        cost_estimate=LIGHT,
    )(place, targets, *rows, weight, *normed_t, *base, *slope, weight)


def per_device(
    image_raw,
    text_raw,
    logit_scale,
    logit_bias,
    pair_offset,
    normed_patches,
    head_cotangent,
    hidden_pre,
    pool_share,
    down_weight,
):
    place = lax.axis_index("dp")
    tensor_index = lax.axis_index("tensor")
    yh = place // (N_CORE * N_Z * N_X)
    x = place // (N_CORE * N_Z) % N_X
    z = place // N_CORE % N_Z
    core = place % N_CORE
    image_rows, width = image_raw.shape
    text_rows = text_raw.shape[0]
    half = text_rows // N_TENSOR
    hidden_here = hidden_pre.shape[1]
    spot = jnp.stack([core, tensor_index]).astype(jnp.int32)
    scalars = jnp.stack([logit_scale, logit_bias])

    text_half = text_half_key(spot, text_raw, half)
    text_half, image_raw, pair_offset, normed_patches, head_cotangent, hidden_pre, pool_share = lax.optimization_barrier(
        (text_half, image_raw, pair_offset, normed_patches, head_cotangent, hidden_pre, pool_share)
    )
    text_far = ring_send(text_half, 7, only=1)
    text_near = jnp.concatenate([text_half, ring_send(text_half, 2)], axis=0)
    image_other = tensor_swap(image_raw)
    text_near, image_other, cotangent_own, offset_sent = lax.optimization_barrier(
        (text_near, image_other, head_cotangent, pair_offset)
    )
    offset_other = tensor_swap(offset_sent)
    text_next = ring_send(text_near, 4)
    rels = jnp.concatenate(
        [
            jnp.array([0, 2, 4, 6], jnp.int32),
            jnp.array([-1, 1, 3, 5], jnp.int32) + 2 * core,
            jnp.array([7], jnp.int32) + 2 * core,
        ]
    )
    text_row = jnp.arange(half, dtype=jnp.int32) + tensor_index * half
    text_value = (text_row[None, :] - text_rows * rels[:, None]).reshape(-1)
    text_valid = jnp.repeat((rels >= 0) & (rels < WINDOW), half)


    columns = 9 * LANES
    start = 8 * LANES
    cotangent_other = torus_send(head_cotangent, core=1)
    hidden_other = torus_send(hidden_pre, core=1)
    share_other = torus_send(pool_share, core=1)
    share_own, share_other = [
        jnp.broadcast_to(jnp.pad(part, (0, 6 * LANES - part.shape[0]))[None, :], (8, 6 * LANES))
        for part in (pool_share, share_other)
    ]
    base_own, slope_own = hidden_base(
        spot, columns, cotangent_own, share_own, down_weight, hidden_pre, HEAVY
    )
    text_next, text_far, base_own, slope_own, offset_other = lax.optimization_barrier(
        (text_next, text_far, base_own, slope_own, offset_other)
    )
    text_window = [text_near, text_next, torus_send(text_near, core=1), torus_send(text_next, core=1), text_far]
    normed_own = transposed(normed_patches, 6 * LANES)
    normed_other = torus_send(normed_own, core=1)

    text_last = text_window[3]
    row = jnp.arange(image_rows, dtype=jnp.int32)
    own_row = row + tensor_index * image_rows
    other_row = row + (1 - tensor_index) * image_rows
    image_value = jnp.concatenate([own_row - pair_offset, other_row - offset_other])
    targets = jnp.stack(
        [(yh + dy) % N_YH * N_X + (x + dx) % N_X for dy in range(N_YH) for dx in range(N_X)]
    ).astype(jnp.int32)
    text_last, share_other, targets = lax.optimization_barrier((text_last, share_other, targets))
    text_window[3] = text_last
    image_part, image_swapped, zero_row, text_own, text_sibling, far = pair_products(
        spot, scalars, image_value, text_value, text_valid, image_raw, image_other, text_window
    )
    zero_theirs = tensor_swap(zero_row)

    near = 2 * half
    returned = torus_send(text_sibling, core=1)
    image_swapped = tensor_swap(image_swapped)
    zero_row, returned, cotangent_other = lax.optimization_barrier((zero_row, returned, cotangent_other))
    text_next = ring_send((text_own[near:] + returned[near:].astype(f32)).astype(bf16), -4)

    base_other, slope_other = hidden_base(
        spot, columns, cotangent_other, share_other, down_weight, hidden_other, LIGHT
    )
    zero_theirs, base_other, slope_other = lax.optimization_barrier((zero_theirs, base_other, slope_other))
    zero_raw = jnp.where(tensor_index == 0, image_raw[:1], image_other[:1]).astype(f32)
    zero_both = jnp.concatenate([logit_scale * (zero_row + zero_theirs), zero_raw], axis=0)
    zero_sibling = torus_send(zero_both, core=1)
    zero_sibling, text_next, image_swapped = lax.optimization_barrier((zero_sibling, text_next, image_swapped))

    split = 5 * LANES
    a_keep, a_sent1, a_sent2, a_sent3, c_keep, c_sent = up_terms(
        spot,
        targets,
        split,
        [normed_own, normed_other],
        [base_own, base_other],
        [slope_own, slope_other],
        down_weight,
        [zero_both, zero_sibling],
    )
    a_keep, image_part, late_text, late_image = lax.optimization_barrier((a_keep, image_part, text_raw, image_raw))
    c_come = torus_send(c_sent, yh=1)
    a_come = [torus_send(part, x=dx) for dx, part in ((2, a_sent2), (1, a_sent1), (3, a_sent3))]
    c_keep = c_keep + c_come.astype(f32)
    c_keep, a_keep, text_own, returned, text_next, far = lax.optimization_barrier(
        (c_keep, a_keep, text_own, returned, text_next, far)
    )
    far = ring_send(far, -7, only=0)
    a_keep = a_keep + (a_come[0].astype(f32) + a_come[1].astype(f32) + a_come[2].astype(f32))
    c_come = [torus_send(c_keep[dx].astype(bf16), x=dx) for dx in (2, 1, 3)]
    a_come = torus_send(a_keep[1].astype(bf16), yh=1)
    total = jnp.concatenate(
        [
            a_keep[0] + a_come.astype(f32),
            c_keep[0] + (c_come[0].astype(f32) + c_come[1].astype(f32) + c_come[2].astype(f32)),
        ],
        axis=1,
    )

    text_near = text_own[:near] + returned[:near].astype(f32) + text_next.astype(f32)
    text_back = ring_send(text_near[half:].astype(bf16), -2)
    total, text_back = lax.optimization_barrier((total, text_back))
    text_dir = logit_scale * (text_near[:half] + text_back.astype(f32) + far.astype(f32))
    text_unit, text_length = unit_rows(lax.dynamic_slice_in_dim(late_text, tensor_index * half, half, 0))
    text_mine = project_back(text_unit, text_length, text_dir).astype(bf16)

    image_unit, image_length = unit_rows(late_image)
    image_dir = logit_scale * (image_part + image_swapped.astype(f32))
    image_grad = project_back(image_unit, image_length, image_dir).astype(bf16)

    rows_chip = total.shape[0] // N_Z
    chunks = total.reshape(N_Z // 2, 2, rows_chip, columns)
    swap_pairs = [(j, j ^ N_CORE) for j in range(N_DP)]
    chunk = lax.dynamic_index_in_dim(chunks, 1 - z % 2, 1, keepdims=False).astype(bf16)
    chunks = lax.dynamic_index_in_dim(chunks, z % 2, 1, keepdims=False)
    chunks = chunks + lax.ppermute(chunk, "dp", swap_pairs).astype(f32)
    total = lax.dynamic_index_in_dim(chunks, z // 2, 0, keepdims=False)
    for hop in (2, 1, 3):
        chunk = lax.dynamic_index_in_dim(chunks, (z // 2 + hop) % (N_Z // 2), 0, keepdims=False).astype(bf16)
        total = total + torus_send(chunk, z=2 * hop).astype(f32)
    text_theirs = tensor_swap(text_mine)
    total, text_theirs, image_grad = lax.optimization_barrier((total, text_theirs, image_grad))
    rows_here = rows_chip // N_CORE
    mine = jnp.where(core == 0, total[:rows_here], total[rows_here:])
    theirs = torus_send(jnp.where(core == 0, total[rows_here:], total[:rows_here]), core=1)
    left = jnp.where(core == 0, mine, theirs)
    right = jnp.where(core == 0, theirs, mine)
    up_grad = jnp.concatenate([left, right[:, columns - start : hidden_here - start]], axis=1)

    text_grad = jnp.where(
        tensor_index == 0,
        jnp.concatenate([text_mine, text_theirs], axis=0),
        jnp.concatenate([text_theirs, text_mine], axis=0),
    )
    return (image_grad, text_grad, up_grad)


def solution(mesh):
    return jax.shard_map(
        per_device,
        mesh=mesh,
        in_specs=(
            P(("dp", "tensor"), None),
            P("dp", None),
            P(),
            P(),
            P(("dp", "tensor")),
            P("dp", None),
            P("dp", None),
            P("dp", "tensor"),
            P("dp"),
            P("tensor", None),
        ),
        out_specs=(P(("dp", "tensor"), None), P("dp", None), P("dp", "tensor")),
        check_vma=False,
    )
```

```python
import functools

import jax
import jax.numpy as jnp
from jax import lax
from jax.experimental import pallas as pl
from jax.experimental.pallas import tpu as pltpu
from jax.sharding import PartitionSpec as P

WINDOW = 8
N_YH, N_X, N_Z, N_CORE = 2, 4, 8, 2
N_DP = N_YH * N_X * N_Z * N_CORE
N_TENSOR = 2
LANES = 128
LIGHT = pl.CostEstimate(flops=1, bytes_accessed=1, transcendentals=0)
HEAVY = pl.CostEstimate(flops=10**10, bytes_accessed=1, transcendentals=0)

epsilon = 1e-06
gelu_root = 0.7978845608028654
gelu_cubic = 0.044715

f32 = jnp.float32
bf16 = jnp.bfloat16


def encode(yh, x, z, core):
    return (((yh % N_YH) * N_X + x % N_X) * N_Z + z % N_Z) * N_CORE + core % N_CORE


def torus_pairs(yh=0, x=0, z=0, core=0):
    pairs = []
    for j in range(N_DP):
        own = (j // (N_CORE * N_Z * N_X), j // (N_CORE * N_Z) % N_X, j // N_CORE % N_Z, j % N_CORE)
        pairs.append((j, encode(own[0] + yh, own[1] + x, own[2] + z, own[3] + core)))
    return pairs


def torus_send(array, **shift):
    return lax.ppermute(array, "dp", torus_pairs(**shift))


def ring_send(array, by, only=None):
    pairs = [(j, (j + by) % N_DP) for j in range(N_DP) if only is None or j % N_CORE == only]
    return lax.ppermute(array, "dp", pairs)


def tensor_swap(array):
    return lax.ppermute(array, "tensor", [(0, 1), (1, 0)])


def unit_rows(raw_rows):
    widened = raw_rows.astype(f32)
    lengths = jnp.sqrt(jnp.sum(widened * widened, axis=-1, keepdims=True) + epsilon)
    return (widened / lengths, lengths)


def project_back(unit_part, lengths, direction):
    radial = jnp.sum(unit_part * direction, axis=-1, keepdims=True)
    return (direction - unit_part * radial) / lengths


def gelu_slope(hidden_in):
    square = hidden_in * hidden_in
    tangent = jnp.tanh(hidden_in * (gelu_root + gelu_root * gelu_cubic * square))
    inner_slope = hidden_in * (0.5 * gelu_root + 1.5 * gelu_root * gelu_cubic * square)
    return 0.5 + 0.5 * tangent + (1.0 - tangent * tangent) * inner_slope


def dot_nt(a, b):
    return lax.dot_general(a, b, (((1,), (1,)), ((), ())), preferred_element_type=f32)


def dot_tn(a, b):
    return lax.dot_general(a, b, (((0,), (0,)), ((), ())), preferred_element_type=f32)


def key_rows(raw):
    return unit_rows(raw)[0].astype(bf16)


def text_key_kernel(half, place_ref, raw_ref, half_ref):
    begin = pl.multiple_of(place_ref[1] * half, half)
    half_ref[...] = key_rows(raw_ref[pl.ds(begin, half), :])


def text_half_key(place, text_raw, half):
    return pl.pallas_call(
        functools.partial(text_key_kernel, half),
        in_specs=[pl.BlockSpec(memory_space=pltpu.SMEM), pl.BlockSpec(memory_space=pltpu.VMEM)],
        out_specs=pl.BlockSpec(memory_space=pltpu.VMEM),
        out_shape=jax.ShapeDtypeStruct((half, text_raw.shape[1]), bf16),
    )(place, text_raw)


def pair_kernel(place_ref, scalar_ref, value_ref, window_value_ref, valid_ref, own_ref, other_ref, *refs):
    window_refs = refs[:-8]
    own_part, other_part, zero_ref, text_own, text_sibling, text_far, key_ref, window_key = refs[-8:]
    half = own_ref.shape[0]
    key_ref[:half, :] = key_rows(own_ref[...])
    key_ref[half:, :] = key_rows(other_ref[...])
    begin = 0
    for ref in window_refs:
        window_key[begin : begin + ref.shape[0], :] = ref[...]
        begin += ref.shape[0]
    logits = scalar_ref[0] * dot_nt(key_ref[...], window_key[...]) + scalar_ref[1]
    target = (value_ref[...] == window_value_ref[...]).astype(f32)
    weight = jnp.where(valid_ref[...] > 0, jax.nn.sigmoid(logits) - target, 0.0).astype(bf16)
    part = jnp.dot(weight, window_key[...], preferred_element_type=f32)
    own_part[...] = part[:half]
    other_part[...] = part[half:].astype(bf16)
    text_part = dot_tn(weight, key_ref[...])
    count = text_own.shape[0]
    text_own[...] = text_part[:count]
    text_sibling[...] = text_part[count : 2 * count].astype(bf16)
    text_far[...] = text_part[2 * count :].astype(bf16)
    zero_ref[...] = jnp.where(place_ref[1] == 0, part[:1], part[half : half + 1])


def pair_products(place, scalars, value, window_value, valid, own, other, window):
    width = own.shape[1]
    rows = value.shape[0]
    depth = window_value.shape[0]
    smem = pl.BlockSpec(memory_space=pltpu.SMEM)
    vmem = pl.BlockSpec(memory_space=pltpu.VMEM)
    return pl.pallas_call(
        pair_kernel,
        in_specs=[smem, smem] + [vmem] * (5 + len(window)),
        out_specs=[vmem] * 6,
        out_shape=[
            jax.ShapeDtypeStruct((rows // 2, width), f32),
            jax.ShapeDtypeStruct((rows // 2, width), bf16),
            jax.ShapeDtypeStruct((1, width), f32),
            jax.ShapeDtypeStruct((2 * rows, width), f32),
            jax.ShapeDtypeStruct((2 * rows, width), bf16),
            jax.ShapeDtypeStruct((depth - 4 * rows, width), bf16),
        ],
        scratch_shapes=[pltpu.VMEM((rows, width), bf16), pltpu.VMEM((depth, width), bf16)],
        compiler_params=pltpu.CompilerParams(vmem_limit_bytes=16 * 2**20),
        cost_estimate=LIGHT,
    )(
        place,
        scalars,
        value[:, None],
        window_value[None, :],
        valid.astype(jnp.int32)[None, :],
        own,
        other,
        *window,
    )


def transpose_kernel(patches, normed_ref, out_ref):
    block = normed_ref[...]
    kept = lax.broadcasted_iota(jnp.int32, block.shape, 0) < patches
    out_ref[...] = jnp.where(kept, block, jnp.zeros_like(block)).T


def transposed(normed, rows):
    patches, width = normed.shape
    step = 3 * LANES
    return pl.pallas_call(
        functools.partial(transpose_kernel, patches),
        grid=(width // step,),
        in_specs=[pl.BlockSpec((rows, step), lambda i: (0, i))],
        out_specs=pl.BlockSpec((step, rows), lambda i: (i, 0)),
        out_shape=jax.ShapeDtypeStruct((width, rows), bf16),
        compiler_params=pltpu.CompilerParams(vmem_limit_bytes=8 * 2**20),
        cost_estimate=LIGHT,
    )(normed)


def copy_all(pairs, sems, first):
    copies = [pltpu.make_async_copy(src, dst, sems.at[first + i]) for i, (src, dst) in enumerate(pairs)]
    for copy in copies:
        copy.start()
    return copies


def base_kernel(place_ref, share_ref, weight_tail, hidden_tail, cotangent_hbm, weight_hbm, hidden_hbm, *refs):
    base_hbm, slope_hbm, cotangent, weight, hidden, base, slope, sems = refs
    patches, columns = base.shape
    start = columns - LANES
    step = start // 2
    begin = place_ref[0] * start
    halves = [pl.ds(pl.multiple_of(begin + i * step, step), step) for i in range(2)]
    wheres = [pl.ds(i * step, step) for i in range(2)]
    loads = copy_all(
        [
            (hidden_hbm.at[:, halves[0]], hidden.at[:, wheres[0]]),
            (cotangent_hbm, cotangent),
            (weight_hbm.at[halves[0], :], weight.at[wheres[0], :]),
            (hidden_hbm.at[:, halves[1]], hidden.at[:, wheres[1]]),
            (weight_hbm.at[halves[1], :], weight.at[wheres[1], :]),
        ],
        sems,
        0,
    )
    share = jnp.broadcast_to(share_ref[...], (8, share_ref.shape[1])).T[:patches, :1]

    def block(weight_rows, hidden_block, where, ready):
        kept = gelu_slope(hidden_block.astype(f32))
        slope[:, where] = (share * kept).astype(bf16)
        for copy in ready:
            copy.wait()
        base[:, where] = (dot_nt(cotangent[...], weight_rows[...]) * kept).astype(bf16)

    def store(where, first):
        return copy_all(
            [(base.at[:, where], base_hbm.at[:, where]), (slope.at[:, where], slope_hbm.at[:, where])], sems, first
        )

    loads[0].wait()
    block(weight.at[wheres[0], :], hidden[:, wheres[0]], wheres[0], loads[1:3])
    stores = store(wheres[0], 5)
    loads[3].wait()
    block(weight.at[wheres[1], :], hidden[:, wheres[1]], wheres[1], loads[4:])
    stores += store(wheres[1], 7)
    where = pl.ds(start, LANES)
    block(weight_tail, hidden_tail[...], where, [])
    stores += store(where, 9)
    for copy in stores:
        copy.wait()


def hidden_base(place, columns, cotangent, share, weight, hidden, cost):
    patches, width = cotangent.shape
    start = columns - LANES
    tiles = start // LANES
    hbm = pl.BlockSpec(memory_space=pl.ANY)
    out = jax.ShapeDtypeStruct((patches, columns), bf16)
    return pl.pallas_call(
        base_kernel,
        grid_spec=pltpu.PrefetchScalarGridSpec(
            num_scalar_prefetch=1,
            grid=(1,),
            in_specs=[
                pl.BlockSpec(share.shape, lambda i, place: (0, 0)),
                pl.BlockSpec((LANES, width), lambda i, place: (tiles * (1 + place[0]), 0)),
                pl.BlockSpec((patches, LANES), lambda i, place: (0, tiles * (1 + place[0]))),
                hbm,
                hbm,
                hbm,
            ],
            out_specs=[hbm, hbm],
            scratch_shapes=[
                pltpu.VMEM((patches, width), bf16),
                pltpu.VMEM((start, width), bf16),
                pltpu.VMEM((patches, start), bf16),
                pltpu.VMEM((patches, columns), bf16),
                pltpu.VMEM((patches, columns), bf16),
                pltpu.SemaphoreType.DMA((11,)),
            ],
        ),
        out_shape=[out, out],
        compiler_params=pltpu.CompilerParams(vmem_limit_bytes=60 * 2**20),
        cost_estimate=cost,
    )(place, share, weight, hidden, cotangent, weight, hidden)


def block_rows(targets_ref, height, dy, dx):
    return pl.ds(pl.multiple_of(targets_ref[dy * N_X + dx] * height, 16), height)


def terms_kernel(
    place_ref,
    targets_ref,
    row0_ref,
    row1_ref,
    weight_tail,
    normed0_hbm,
    normed1_hbm,
    base0_hbm,
    base1_hbm,
    slope0_hbm,
    slope1_hbm,
    weight_hbm,
    a_keep,
    a_sent1,
    a_sent2,
    a_sent3,
    c_keep,
    c_sent,
    weight,
    normed,
    base,
    slope,
    sum_a,
    sum_c,
    stage_a,
    stage_c,
    sems,
):
    _, patches, columns = base.shape
    width = weight.shape[1]
    start = columns - LANES
    split = a_keep.shape[2]
    height = a_keep.shape[1]
    begin = pl.multiple_of(place_ref[0] * start, start)
    part_a, part_c = pl.ds(0, split), pl.ds(split, columns - split)
    images = ((slope0_hbm, base0_hbm, normed0_hbm), (slope1_hbm, base1_hbm, normed1_hbm))
    pairs = [(weight_hbm.at[pl.ds(begin, start), :], weight)]
    for i, (slope_hbm, base_hbm, normed_hbm) in enumerate(images):
        pairs += [
            (slope_hbm.at[:, part_c], slope.at[i, :, part_c]),
            (base_hbm.at[:, part_c], base.at[i, :, part_c]),
            (normed_hbm, normed.at[i]),
        ]
    for i, (slope_hbm, base_hbm, normed_hbm) in enumerate(images):
        pairs += [
            (slope_hbm.at[:, part_a], slope.at[i, :, part_a]),
            (base_hbm.at[:, part_a], base.at[i, :, part_a]),
        ]
    loads = copy_all(pairs, sems, 0)
    pooled = []
    for ref in (row0_ref, row1_ref):
        unit, length = unit_rows(ref[1:2, :])
        pooled.append(jnp.broadcast_to(project_back(unit, length, ref[0:1, :]), (8, width)))
    pooled = jnp.concatenate(pooled, axis=0).astype(bf16)
    loads[0].wait()
    lift = jnp.concatenate([dot_nt(pooled, weight[...]), dot_nt(pooled, weight_tail[...])], axis=1)

    def product(image, first, last):
        lifted = lift[8 * image : 8 * image + 1, first:last] * slope[image, :, first:last].astype(f32)
        grad = (base[image, :, first:last].astype(f32) + lifted).astype(bf16)
        return jnp.dot(normed[image, :, :patches], grad, preferred_element_type=f32)

    for copy in loads[1:4]:
        copy.wait()
    sum_c[...] = product(0, split, columns)
    for copy in loads[4:7]:
        copy.wait()
    sum_c[...] += product(1, split, columns)
    stores = copy_all(
        [(sum_c.at[block_rows(targets_ref, height, 0, dx), :], c_keep.at[dx]) for dx in range(N_X)], sems, 11
    )
    for dx in range(N_X):
        stage_c[dx] = sum_c[block_rows(targets_ref, height, 1, dx), :].astype(bf16)
    stores += copy_all([(stage_c, c_sent)], sems, 15)
    for copy in loads[7:]:
        copy.wait()
    sum_a[...] = product(0, 0, split) + product(1, 0, split)
    stores += copy_all(
        [(sum_a.at[block_rows(targets_ref, height, dy, 0), :], a_keep.at[dy]) for dy in range(N_YH)], sems, 16
    )
    for dx, out in ((1, a_sent1), (2, a_sent2), (3, a_sent3)):
        for dy in range(N_YH):
            stage_a[dx - 1, dy] = sum_a[block_rows(targets_ref, height, dy, dx), :].astype(bf16)
        stores += copy_all([(stage_a.at[dx - 1], out)], sems, 17 + dx)
    for copy in stores:
        copy.wait()


def up_terms(place, targets, split, normed_t, base, slope, weight, rows):
    width, depth = normed_t[0].shape
    patches, columns = base[0].shape
    height = width // (N_YH * N_X)
    hbm = pl.BlockSpec(memory_space=pl.ANY)
    tiles = columns // LANES - 1
    row = pl.BlockSpec((2, width), lambda i, place, targets: (0, 0))
    part_a, part_c = (N_YH, height, split), (N_X, height, columns - split)
    return pl.pallas_call(
        terms_kernel,
        grid_spec=pltpu.PrefetchScalarGridSpec(
            num_scalar_prefetch=2,
            grid=(1,),
            in_specs=[
                row,
                row,
                pl.BlockSpec((LANES, width), lambda i, place, targets: (tiles * (1 + place[0]), 0)),
            ]
            + [hbm] * 7,
            out_specs=[hbm] * 6,
            scratch_shapes=[
                pltpu.VMEM((columns - LANES, width), bf16),
                pltpu.VMEM((2, width, depth), bf16),
                pltpu.VMEM((2, patches, columns), bf16),
                pltpu.VMEM((2, patches, columns), bf16),
                pltpu.VMEM((width, split), f32),
                pltpu.VMEM((width, columns - split), f32),
                pltpu.VMEM((N_X - 1,) + part_a, bf16),
                pltpu.VMEM(part_c, bf16),
                pltpu.SemaphoreType.DMA((21,)),
            ],
        ),
        out_shape=[
            jax.ShapeDtypeStruct(part_a, f32),
            jax.ShapeDtypeStruct(part_a, bf16),
            jax.ShapeDtypeStruct(part_a, bf16),
            jax.ShapeDtypeStruct(part_a, bf16),
            jax.ShapeDtypeStruct(part_c, f32),
            jax.ShapeDtypeStruct(part_c, bf16),
        ],
        compiler_params=pltpu.CompilerParams(vmem_limit_bytes=60 * 2**20),
        cost_estimate=LIGHT,
    )(place, targets, *rows, weight, *normed_t, *base, *slope, weight)


def per_device(
    image_raw,
    text_raw,
    logit_scale,
    logit_bias,
    pair_offset,
    normed_patches,
    head_cotangent,
    hidden_pre,
    pool_share,
    down_weight,
):
    place = lax.axis_index("dp")
    tensor_index = lax.axis_index("tensor")
    yh = place // (N_CORE * N_Z * N_X)
    x = place // (N_CORE * N_Z) % N_X
    z = place // N_CORE % N_Z
    core = place % N_CORE
    image_rows, width = image_raw.shape
    text_rows = text_raw.shape[0]
    half = text_rows // N_TENSOR
    hidden_here = hidden_pre.shape[1]
    spot = jnp.stack([core, tensor_index]).astype(jnp.int32)
    scalars = jnp.stack([logit_scale, logit_bias])

    text_half = text_half_key(spot, text_raw, half)
    text_half, image_raw, pair_offset, normed_patches, head_cotangent, hidden_pre, pool_share = lax.optimization_barrier(
        (text_half, image_raw, pair_offset, normed_patches, head_cotangent, hidden_pre, pool_share)
    )
    text_far = ring_send(text_half, 7, only=1)
    text_near = jnp.concatenate([text_half, ring_send(text_half, 2)], axis=0)
    image_other = tensor_swap(image_raw)
    text_near, image_other, cotangent_own, offset_sent = lax.optimization_barrier(
        (text_near, image_other, head_cotangent, pair_offset)
    )
    offset_other = tensor_swap(offset_sent)
    text_next = ring_send(text_near, 4)
    rels = jnp.concatenate(
        [
            jnp.array([0, 2, 4, 6], jnp.int32),
            jnp.array([-1, 1, 3, 5], jnp.int32) + 2 * core,
            jnp.array([7], jnp.int32) + 2 * core,
        ]
    )
    text_row = jnp.arange(half, dtype=jnp.int32) + tensor_index * half
    text_value = (text_row[None, :] - text_rows * rels[:, None]).reshape(-1)
    text_valid = jnp.repeat((rels >= 0) & (rels < WINDOW), half)


    columns = 9 * LANES
    start = 8 * LANES
    cotangent_other = torus_send(head_cotangent, core=1)
    hidden_other = torus_send(hidden_pre, core=1)
    share_other = torus_send(pool_share, core=1)
    share_own, share_other = [
        jnp.pad(part, (0, 6 * LANES - part.shape[0]))[None, :]
        for part in (pool_share, share_other)
    ]
    base_own, slope_own = hidden_base(
        spot, columns, cotangent_own, share_own, down_weight, hidden_pre, HEAVY
    )
    text_next, text_far, base_own, slope_own, offset_other = lax.optimization_barrier(
        (text_next, text_far, base_own, slope_own, offset_other)
    )
    text_window = [text_near, text_next, torus_send(text_near, core=1), torus_send(text_next, core=1), text_far]
    normed_own = transposed(normed_patches, 6 * LANES)
    normed_other = torus_send(normed_own, core=1)

    text_last = text_window[3]
    row = jnp.arange(image_rows, dtype=jnp.int32)
    own_row = row + tensor_index * image_rows
    other_row = row + (1 - tensor_index) * image_rows
    image_value = jnp.concatenate([own_row - pair_offset, other_row - offset_other])
    targets = jnp.stack(
        [(yh + dy) % N_YH * N_X + (x + dx) % N_X for dy in range(N_YH) for dx in range(N_X)]
    ).astype(jnp.int32)
    text_last, share_other, targets = lax.optimization_barrier((text_last, share_other, targets))
    text_window[3] = text_last
    image_part, image_swapped, zero_row, text_own, text_sibling, far = pair_products(
        spot, scalars, image_value, text_value, text_valid, image_raw, image_other, text_window
    )
    zero_theirs = tensor_swap(zero_row)

    near = 2 * half
    returned = torus_send(text_sibling, core=1)
    image_swapped = tensor_swap(image_swapped)
    zero_row, returned, cotangent_other = lax.optimization_barrier((zero_row, returned, cotangent_other))
    text_next = ring_send((text_own[near:] + returned[near:].astype(f32)).astype(bf16), -4)

    base_other, slope_other = hidden_base(
        spot, columns, cotangent_other, share_other, down_weight, hidden_other, LIGHT
    )
    zero_theirs, base_other, slope_other = lax.optimization_barrier((zero_theirs, base_other, slope_other))
    zero_raw = jnp.where(tensor_index == 0, image_raw[:1], image_other[:1]).astype(f32)
    zero_both = jnp.concatenate([logit_scale * (zero_row + zero_theirs), zero_raw], axis=0)
    zero_sibling = torus_send(zero_both, core=1)
    zero_sibling, text_next, image_swapped = lax.optimization_barrier((zero_sibling, text_next, image_swapped))

    split = 5 * LANES
    a_keep, a_sent1, a_sent2, a_sent3, c_keep, c_sent = up_terms(
        spot,
        targets,
        split,
        [normed_own, normed_other],
        [base_own, base_other],
        [slope_own, slope_other],
        down_weight,
        [zero_both, zero_sibling],
    )
    a_keep, image_part, late_text, late_image = lax.optimization_barrier((a_keep, image_part, text_raw, image_raw))
    c_come = torus_send(c_sent, yh=1)
    a_come = [torus_send(part, x=dx) for dx, part in ((2, a_sent2), (1, a_sent1), (3, a_sent3))]
    c_keep = c_keep + c_come.astype(f32)
    c_keep, a_keep, text_own, returned, text_next, far = lax.optimization_barrier(
        (c_keep, a_keep, text_own, returned, text_next, far)
    )
    far = ring_send(far, -7, only=0)
    a_keep = a_keep + (a_come[0].astype(f32) + a_come[1].astype(f32) + a_come[2].astype(f32))
    c_come = [torus_send(c_keep[dx].astype(bf16), x=dx) for dx in (2, 1, 3)]
    a_come = torus_send(a_keep[1].astype(bf16), yh=1)
    total = jnp.concatenate(
        [
            a_keep[0] + a_come.astype(f32),
            c_keep[0] + (c_come[0].astype(f32) + c_come[1].astype(f32) + c_come[2].astype(f32)),
        ],
        axis=1,
    )

    text_near = text_own[:near] + returned[:near].astype(f32) + text_next.astype(f32)
    text_back = ring_send(text_near[half:].astype(bf16), -2)
    total, text_back = lax.optimization_barrier((total, text_back))
    text_dir = logit_scale * (text_near[:half] + text_back.astype(f32) + far.astype(f32))
    text_unit, text_length = unit_rows(lax.dynamic_slice_in_dim(late_text, tensor_index * half, half, 0))
    text_mine = project_back(text_unit, text_length, text_dir).astype(bf16)

    image_unit, image_length = unit_rows(late_image)
    image_dir = logit_scale * (image_part + image_swapped.astype(f32))
    image_grad = project_back(image_unit, image_length, image_dir).astype(bf16)

    rows_chip = total.shape[0] // N_Z
    chunks = total.reshape(N_Z // 2, 2, rows_chip, columns)
    swap_pairs = [(j, j ^ N_CORE) for j in range(N_DP)]
    chunk = lax.dynamic_index_in_dim(chunks, 1 - z % 2, 1, keepdims=False).astype(bf16)
    chunks = lax.dynamic_index_in_dim(chunks, z % 2, 1, keepdims=False)
    chunks = chunks + lax.ppermute(chunk, "dp", swap_pairs).astype(f32)
    total = lax.dynamic_index_in_dim(chunks, z // 2, 0, keepdims=False)
    for hop in (2, 1, 3):
        chunk = lax.dynamic_index_in_dim(chunks, (z // 2 + hop) % (N_Z // 2), 0, keepdims=False).astype(bf16)
        total = total + torus_send(chunk, z=2 * hop).astype(f32)
    text_theirs = tensor_swap(text_mine)
    total, text_theirs, image_grad = lax.optimization_barrier((total, text_theirs, image_grad))
    rows_here = rows_chip // N_CORE
    mine = jnp.where(core == 0, total[:rows_here], total[rows_here:])
    theirs = torus_send(jnp.where(core == 0, total[rows_here:], total[:rows_here]), core=1)
    left = jnp.where(core == 0, mine, theirs)
    right = jnp.where(core == 0, theirs, mine)
    up_grad = jnp.concatenate([left, right[:, columns - start : hidden_here - start]], axis=1)

    text_grad = jnp.where(
        tensor_index == 0,
        jnp.concatenate([text_mine, text_theirs], axis=0),
        jnp.concatenate([text_theirs, text_mine], axis=0),
    )
    return (image_grad, text_grad, up_grad)


def solution(mesh):
    return jax.shard_map(
        per_device,
        mesh=mesh,
        in_specs=(
            P(("dp", "tensor"), None),
            P("dp", None),
            P(),
            P(),
            P(("dp", "tensor")),
            P("dp", None),
            P("dp", None),
            P("dp", "tensor"),
            P("dp"),
            P("tensor", None),
        ),
        out_specs=(P(("dp", "tensor"), None), P("dp", None), P("dp", "tensor")),
        check_vma=False,
    )
```
